32 devices in a mesh: dp: 8 (over z, y), tensor: 4 (over x, core).
Axes of the slice: x: 2, y: 2, z: 4, core: 2. Of those that a mesh axis runs over, the one named last changes fastest.
Arguments:
- block_input: bfloat16 [8192, 2048], P(('dp', 'tensor')), may hold values from -6 to 6
- cotangent: bfloat16 [8192, 2048], P(('dp', 'tensor')), may hold values from -6 to 6
- ln1_gain: float32 [2048], replicated, may hold values from 0.5 to 1.5
- ln1_bias: float32 [2048], replicated, may hold values from -1.5 to 1.5
- w_query: bfloat16 [2048, 2048], P('dp', 'tensor'), may hold values from -0.125 to 0.125
- q_bias: float32 [2048], replicated, may hold values from -1.5 to 1.5
- w_key: bfloat16 [2048, 2048], P('dp', 'tensor'), may hold values from -0.125 to 0.125
- k_bias: float32 [512], replicated, may hold values from -1.5 to 1.5
- w_value: bfloat16 [2048, 2048], P('dp', 'tensor'), may hold values from -0.125 to 0.125
- v_bias: float32 [2048], replicated, may hold values from -1.5 to 1.5
- w_out: bfloat16 [2048, 2048], P('dp', 'tensor'), may hold values from -0.375 to 0.375
- ln2_gain: float32 [2048], replicated, may hold values from 0.5 to 1.5
- ln2_bias: float32 [2048], replicated, may hold values from -1.5 to 1.5
- w_gate: bfloat16 [2048, 5632], P('dp', 'tensor'), may hold values from -0.125 to 0.125
- w_up: bfloat16 [2048, 5632], P('dp', 'tensor'), may hold values from -0.125 to 0.125
- w_down: bfloat16 [2048, 5632], P('dp', 'tensor'), may hold values from -0.15625 to 0.15625
Outputs:
- block_output: bfloat16 [8192, 2048], P(('dp', 'tensor'))
- input_grad: float32 [8192, 2048], P(('dp', 'tensor'))
- ln1_gain_grad: float32 [2048], replicated
- ln1_bias_grad: float32 [2048], replicated
- w_query_grad: float32 [2048, 2048], P('dp', 'tensor')
- q_bias_grad: float32 [2048], replicated
- w_key_grad: float32 [2048, 2048], P('dp', 'tensor')
- k_bias_grad: float32 [512], replicated
- w_value_grad: float32 [2048, 2048], P('dp', 'tensor')
- v_bias_grad: float32 [2048], replicated
- w_out_grad: float32 [2048, 2048], P('dp', 'tensor')
- ln2_gain_grad: float32 [2048], replicated
- ln2_bias_grad: float32 [2048], replicated
- w_gate_grad: float32 [2048, 5632], P('dp', 'tensor')
- w_up_grad: float32 [2048, 5632], P('dp', 'tensor')
- w_down_grad: float32 [2048, 5632], P('dp', 'tensor')
The draws below stay inside these ranges and needn't reach their ends.
All inputs are finite; a program needn't handle non-finite values.
Results may differ from the reference program's by a relative error of at most 0.019.
Values may be sent and summed in bfloat16 or wider, within the bound.
No kernel may reach another device: no remote copies, remote signals or barrier semaphores. Data moves between devices by JAX's collectives and lax.ppermute only.
A program may use at most 192 MiB of HBM per device.

```python
import jax
import jax.numpy as jnp
from jax import lax

D = 2048
HEADS = 32
HEAD = 64
ROT = 16
FF = 5632
LENGTH = 1024
TOKENS = 8192
N_DP = 8


def strengthened(values, key, source, target, shards_of, factor):
    owner, partner = [(jnp.arange(values.shape[axis_at]) // (values.shape[axis_at] // shards_of)).reshape([-1 if axis == axis_at else 1 for axis in range(values.ndim)]) for axis_at in (source, target)]
    chosen = jax.random.permutation(key, shards_of)[partner]
    strong = (owner == chosen) | (owner == (partner + shards_of // 2) % shards_of)
    return jnp.where(strong, factor * values, values)


def shard_levels(key, extent, pieces, least, top_value):
    level = 1.0
    for position, shards_of in pieces:
        heights = jax.random.uniform(jax.random.fold_in(jax.random.fold_in(key, 6), position), (shards_of,), jnp.float32, least / len(pieces), top_value / len(pieces))
        level = level * jnp.repeat(jnp.exp(heights), extent[position] // shards_of).reshape((-1,) + (1,) * (len(extent) - 1 - position))
    return level


def bell_draw(own_key, dims, deviation, bound, shards=(), kind=jnp.bfloat16):
    values = deviation * jax.random.normal(own_key, dims, jnp.float32)
    if shards:
        values = values * shard_levels(own_key, dims, shards, -0.22, 0.18)
    return jnp.clip(values, -bound, bound).astype(kind)


def gaussian_with(rng, extent, width, most, shards, heavy, kind=jnp.bfloat16):
    result = width * jax.random.normal(rng, extent, jnp.float32)
    if shards:
        result = result * shard_levels(rng, extent, shards, -0.22, 0.18)
    return jnp.clip(strengthened(result, jax.random.fold_in(rng, 3), *heavy), -most, most).astype(kind)


def setup_inputs(seed: int = 0) -> dict:
    seeds = jax.random.split(jax.random.key(seed), 17)
    block_input = gaussian_with(seeds[0], (TOKENS, D), 1.0, 6.0, ((0, 32),), (0, 1, 32, 2.75))
    cotangent = gaussian_with(seeds[1], (TOKENS, D), 1.0, 6.0, ((0, 32),), (0, 1, 32, 2.75))
    ln1_gain = jnp.clip(1.0 + 0.1 * jax.random.normal(seeds[2], (D,), jnp.float32), 0.5, 1.5)
    ln1_bias = bell_draw(seeds[3], (D,), 0.3, 1.5, (), jnp.float32)
    w_query = bell_draw(seeds[4], (D, D), D ** -0.5, 0.125, ((0, 8), (1, 4)))
    q_bias = bell_draw(seeds[5], (D,), 0.3, 1.5, (), jnp.float32)
    w_key = bell_draw(seeds[6], (D, D), D ** -0.5, 0.125, ((0, 8), (1, 4)))
    k_bias = bell_draw(seeds[7], (HEADS * ROT,), 0.3, 1.5, (), jnp.float32)
    w_value = bell_draw(seeds[8], (D, D), D ** -0.5, 0.125, ((0, 8), (1, 4)))
    v_bias = bell_draw(seeds[9], (D,), 0.3, 1.5, (), jnp.float32)
    w_out = bell_draw(seeds[10], (D, D), (D // 8) ** -0.5, 0.375, ((0, 8), (1, 4)))
    ln2_gain = jnp.clip(1.0 + 0.1 * jax.random.normal(seeds[11], (D,), jnp.float32), 0.5, 1.5)
    ln2_bias = bell_draw(seeds[12], (D,), 0.3, 1.5, (), jnp.float32)
    w_gate = bell_draw(seeds[13], (D, FF), D ** -0.5, 0.125, ((0, 8), (1, 4)))
    w_up = bell_draw(seeds[14], (D, FF), D ** -0.5, 0.125, ((0, 8), (1, 4)))
    w_down = bell_draw(seeds[15], (D, FF), (FF // 4) ** -0.5, 0.15625, ((0, 8), (1, 4)))
    return {"block_input": block_input, "cotangent": cotangent, "ln1_gain": ln1_gain, "ln1_bias": ln1_bias, "w_query": w_query, "q_bias": q_bias, "w_key": w_key, "k_bias": k_bias, "w_value": w_value, "v_bias": v_bias, "w_out": w_out, "ln2_gain": ln2_gain, "ln2_bias": ln2_bias, "w_gate": w_gate, "w_up": w_up, "w_down": w_down}


@jax.custom_vjp
def low(v):
    return lax.optimization_barrier(v.astype(jnp.bfloat16)).astype(jnp.float32)

@jax.custom_vjp
def low_back(v):
    return v

def low_keep(v):
    return (low(v), None)

def low_pass(kept, grad):
    return (grad,)

def back_keep(v):
    return (v, None)

def back_low(kept, grad):
    return (low(grad),)
low.defvjp(low_keep, low_pass)
low_back.defvjp(back_keep, back_low)
eps_norm = 1e-05
highest = lax.Precision.HIGHEST

def layer_norm(values, gain_vec, shift_vec):
    row_mean = lax.optimization_barrier(jnp.mean(values, axis=-1, keepdims=True))
    centered = values - row_mean
    variance = lax.optimization_barrier(jnp.mean(centered * centered, axis=-1, keepdims=True))
    return centered * lax.rsqrt(variance + eps_norm) * gain_vec + shift_vec

def rotary_tables(length):
    half_rot = ROT // 2
    frequency = 10000.0 ** (-2.0 * jnp.arange(half_rot, dtype=jnp.float32) / ROT)
    angles = jnp.arange(length, dtype=jnp.float32)[:, None] * frequency[None, :]
    return (jnp.cos(angles)[:, None, :], jnp.sin(angles)[:, None, :])

def rotate(values, cosine, sine):
    half_rot = ROT // 2
    leading = values[..., :half_rot]
    trailing = values[..., half_rot:ROT]
    return jnp.concatenate([leading * cosine - trailing * sine, trailing * cosine + leading * sine, values[..., ROT:]], axis=-1)

def block(rows, gain_one, shift_one, w_query, q_bias, w_key, k_bias, w_value, v_bias, w_out, gain_two, shift_two, w_gate, w_up, w_down):
    length = rows.shape[0]
    act_one = low(layer_norm(rows, gain_one, shift_one))
    key_shift = jnp.pad(k_bias.reshape(HEADS, ROT), ((0, 0), (0, HEAD - ROT))).reshape(D)
    query_pre = low_back(jnp.dot(act_one, w_query, precision=highest) + q_bias)
    key_pre = low_back(jnp.dot(act_one, w_key, precision=highest) + key_shift)
    value_all = low(low_back(jnp.dot(act_one, w_value, precision=highest) + v_bias)).reshape(length, HEADS, HEAD)
    cosine, sine = rotary_tables(length)
    query_all = low(rotate(query_pre.reshape(length, HEADS, HEAD), cosine, sine))
    key_all = low(rotate(key_pre.reshape(length, HEADS, HEAD), cosine, sine))
    scores = low_back(jnp.einsum('qhd,khd->hqk', query_all, key_all, precision=highest)) * 0.125
    places = jnp.arange(length)
    scores = jnp.where((places[None, :] <= places[:, None])[None], scores, -1e+30)
    probs = low(jax.nn.softmax(scores, axis=-1))
    context = low(low_back(jnp.einsum('hqk,khd->qhd', probs, value_all, precision=highest).reshape(length, D)))
    hidden = rows + low_back(jnp.dot(context, w_out.T, precision=highest))
    act_two = low(layer_norm(hidden, gain_two, shift_two))
    gate = low_back(jnp.dot(act_two, w_gate, precision=highest))
    upward = low_back(jnp.dot(act_two, w_up, precision=highest))
    inner_act = low(jax.nn.silu(gate) * upward)
    return hidden + jnp.dot(inner_act, w_down.T, precision=highest)

def reference(block_input, cotangent, ln1_gain, ln1_bias, w_query, q_bias, w_key, k_bias, w_value, v_bias, w_out, ln2_gain, ln2_bias, w_gate, w_up, w_down):
    params = tuple((item.astype(jnp.float32) for item in (ln1_gain, ln1_bias, w_query, q_bias, w_key, k_bias, w_value, v_bias, w_out, ln2_gain, ln2_bias, w_gate, w_up, w_down)))
    inputs = block_input.astype(jnp.float32).reshape(N_DP, LENGTH, D)
    stepped = jax.checkpoint(block)

    def whole(rows_all, *weights):
        return lax.map(lambda sequence: stepped(sequence, *weights), rows_all)
    outputs, pullback = jax.vjp(whole, inputs, *params)
    grads = pullback(cotangent.astype(jnp.float32).reshape(N_DP, LENGTH, D))
    return (outputs.reshape(TOKENS, D).astype(jnp.bfloat16), grads[0].reshape(TOKENS, D), grads[1], grads[2], grads[3], grads[4], grads[5], grads[6], grads[7], grads[8], grads[9], grads[10], grads[11], grads[12], grads[13], grads[14])
```

```python
import functools

import jax
import jax.numpy as jnp
from jax import lax
from jax.sharding import PartitionSpec as P

HEAD = 64
ROT = 16
EPS = 1e-05
BF = jnp.bfloat16
F32 = jnp.float32


def norm_forward(values, gain_vec, shift_vec):
    row_mean = jnp.mean(values, axis=-1, keepdims=True)
    centered = values - row_mean
    variance = jnp.mean(centered * centered, axis=-1, keepdims=True)
    inverse = lax.rsqrt(variance + EPS)
    normed = centered * inverse
    return (normed * gain_vec + shift_vec, normed, inverse)


def norm_backward(upstream, normed, inverse, gain_vec):
    scaled = upstream * gain_vec
    adjusted = (
        scaled
        - jnp.mean(scaled, axis=-1, keepdims=True)
        - normed * jnp.mean(scaled * normed, axis=-1, keepdims=True)
    )
    return (inverse * adjusted, jnp.sum(upstream * normed, axis=0), jnp.sum(upstream, axis=0))


def dot(left, right):
    return jnp.dot(left, right, preferred_element_type=F32)


def times_transposed(left, right):
    return lax.dot_general(left, right, (((1,), (1,)), ((), ())), preferred_element_type=F32)


def over_rows(left, right):
    return lax.dot_general(left, right, (((0,), (0,)), ((), ())), preferred_element_type=F32)


def rotate(values, cosine, sine):
    half = ROT // 2
    leading = values[..., :half]
    trailing = values[..., half:ROT]
    return jnp.concatenate(
        [leading * cosine - trailing * sine, trailing * cosine + leading * sine, values[..., ROT:]],
        axis=-1,
    )


class Place:
    def __init__(self, n_dp, n_tensor):
        self.n_dp, self.n_tensor = n_dp, n_tensor
        self.n_line = n_dp // 2
        dp, tensor = lax.axis_index("dp"), lax.axis_index("tensor")
        self.dp, self.tensor = dp, tensor
        self.line, self.pair = dp // 2, dp % 2

    def to_pair(self, v):
        return lax.ppermute(v, "dp", [(i, i ^ 1) for i in range(self.n_dp)])

    def to_side(self, v):
        return lax.ppermute(v, "tensor", [(i, i ^ 2) for i in range(self.n_tensor)])

    def to_core(self, v):
        return lax.ppermute(v, "tensor", [(i, i ^ 1) for i in range(self.n_tensor)])

    def up(self, v, first, last):
        return lax.ppermute(
            v, "dp", [(2 * i + p, 2 * i + 2 + p) for i in range(first, last) for p in (0, 1)]
        )

    def down(self, v, first, last):
        return lax.ppermute(
            v, "dp", [(2 * i + p, 2 * i - 2 + p) for i in range(first, last) for p in (0, 1)]
        )

    def by_pair(self, first, second, axis):
        return jnp.where(
            self.pair == 0,
            jnp.concatenate([first, second], axis),
            jnp.concatenate([second, first], axis),
        )

    def halves(self, v, axis):
        half = v.shape[axis] // 2
        low = lax.slice_in_dim(v, 0, half, axis=axis)
        high = lax.slice_in_dim(v, half, 2 * half, axis=axis)
        return jnp.where(self.pair == 0, low, high), jnp.where(self.pair == 0, high, low)

    def gather_weight(self, w):
        n = self.n_line
        mine, theirs = self.halves(w, 1)
        piece = self.by_pair(mine, self.to_pair(theirs), 0)
        ups, downs = [], []
        going_up = going_down = piece
        for k in range(1, n):
            going_up = self.up(going_up, k - 1, n - 1)
            going_down = self.down(going_down, 1, n - k + 1)
            ups.append(going_up)
            downs.append(going_down)
        slots = [piece]
        for j in range(1, n):
            slots.append(jnp.where(self.line + j < n, downs[j - 1], ups[n - j - 1]))
        return jnp.concatenate(slots, 0)

    def scatter_grad(self, g):
        n = self.n_line
        size = g.shape[0] // n
        block = [lax.slice_in_dim(g, j * size, (j + 1) * size, axis=0) for j in range(n)]
        up_sum = down_sum = None
        for s in range(1, n):
            up_load, down_load = block[n - s], block[s]
            if s > 1:
                up_load = (up_load.astype(F32) + up_sum.astype(F32)).astype(BF)
                down_load = (down_load.astype(F32) + down_sum.astype(F32)).astype(BF)
            up_sum = self.up(up_load, 0, s)
            down_sum = self.down(down_load, n - s, n)
        total = block[0].astype(F32) + up_sum.astype(F32) + down_sum.astype(F32)
        mine, theirs = self.halves(total, 0)
        other = self.to_pair(theirs.astype(BF)).astype(F32)
        return self.by_pair(mine, other, 1)

    def gather_rows(self, a):
        half = a.shape[0] // 2
        h1, h2 = a[:half], a[half:]
        x1, y2 = self.to_side(h1), self.to_pair(h2)
        own_core = self.to_core(a)
        first_core = self.to_core(jnp.stack([x1, y2]))
        y1 = self.to_pair(jnp.stack([h1, x1]))
        x2 = self.to_side(jnp.stack([h2, y2]))
        second = jnp.stack([y1, x2])
        second_core = self.to_core(second)

        def table(own, first, last):
            y1, x2 = last[0], last[1]
            r00 = own
            r01 = jnp.concatenate([first[0], x2[0]], 0)
            r10 = jnp.concatenate([y1[0], first[1]], 0)
            r11 = jnp.concatenate([y1[1], x2[1]], 0)
            return r00, r01, r10, r11

        m = table(a, jnp.stack([x1, y2]), second)
        o = table(own_core, first_core, second_core)
        return jnp.concatenate([m[0], o[0], m[1], o[1], m[2], o[2], m[3], o[3]], 0)

    def scatter_rows(self, p):
        rows = p.shape[0] // 8
        p = p.reshape(2, 2, 2, rows, p.shape[1])
        keep, send = p[:, :, 0], p[:, :, 1]
        acc = (keep.astype(F32) + self.to_core(send).astype(F32)).astype(BF)
        half = rows // 2
        h1, h2 = acc[:, :, :half], acc[:, :, half:]
        r1 = self.to_side(h1[:, 1])
        r2 = self.to_pair(h2[1])
        b1 = (h1[:, 0].astype(F32) + r1.astype(F32)).astype(BF)
        b2 = (h2[0].astype(F32) + r2.astype(F32)).astype(BF)
        s1 = self.to_pair(b1[1])
        s2 = self.to_side(b2[1])
        return jnp.concatenate(
            [b1[0].astype(F32) + s1.astype(F32), b2[0].astype(F32) + s2.astype(F32)], 0
        )

    def sum_all(self, v):
        step = 1
        while step < self.n_tensor:
            v = v + lax.ppermute(v, "tensor", [(i, i ^ step) for i in range(self.n_tensor)])
            step *= 2
        step = 1
        while step < self.n_dp:
            v = v + lax.ppermute(v, "dp", [(i, i ^ step) for i in range(self.n_dp)])
            step *= 2
        return v


def local(
    n_dp,
    n_tensor,
    block_input,
    cotangent,
    ln1_gain,
    ln1_bias,
    w_query,
    q_bias,
    w_key,
    k_bias,
    w_value,
    v_bias,
    w_out,
    ln2_gain,
    ln2_bias,
    w_gate,
    w_up,
    w_down,
):
    at = Place(n_dp, n_tensor)
    width = block_input.shape[1]
    rows = block_input.shape[0]
    length = rows * n_tensor
    shift = at.line * (width // at.n_line)

    def rolled(v, back=False):
        start = (width - shift) if back else shift
        return lax.dynamic_slice_in_dim(jnp.concatenate([v, v], -1), start, width, axis=v.ndim - 1)

    gain_one, bias_one = rolled(ln1_gain), rolled(ln1_bias)
    gain_two, bias_two = rolled(ln2_gain), rolled(ln2_bias)
    input_single = rolled(block_input).astype(F32)
    cot_own = rolled(cotangent)

    cols = w_query.shape[1] // 2
    heads = cols // HEAD
    full_query, full_key, full_value = (
        at.gather_weight(w_query),
        at.gather_weight(w_key),
        at.gather_weight(w_value),
    )
    full_out = at.gather_weight(w_out)
    full_gate = at.gather_weight(w_gate)
    full_up = at.gather_weight(w_up)
    full_down = at.gather_weight(w_down)

    column = at.tensor * 2 * cols + at.pair * cols
    query_shift = lax.dynamic_slice_in_dim(q_bias, column, cols)
    value_shift = lax.dynamic_slice_in_dim(v_bias, column, cols)
    key_column = at.tensor * 2 * heads * ROT + at.pair * heads * ROT
    key_rows = lax.dynamic_slice_in_dim(k_bias, key_column, heads * ROT)
    key_shift = jnp.pad(key_rows.reshape(heads, ROT), ((0, 0), (0, HEAD - ROT))).reshape(cols)

    normed_one, unit_one, inverse_one = norm_forward(input_single, gain_one, bias_one)
    act_one = at.gather_rows(normed_one.astype(BF))
    tokens = act_one.shape[0]

    slots = jnp.arange(n_tensor)
    place = ((at.tensor ^ slots)[:, None] * rows + jnp.arange(rows)[None, :]).reshape(length)
    half_rot = ROT // 2
    frequency = 10000.0 ** (-2.0 * jnp.arange(half_rot, dtype=F32) / ROT)
    angles = place.astype(F32)[:, None] * frequency[None, :]
    cosine, sine = jnp.cos(angles)[:, None, :], jnp.sin(angles)[:, None, :]

    def split(v):
        return v.reshape(2, length, heads, HEAD)

    query_all = rotate(split(dot(act_one, full_query) + query_shift), cosine, sine).astype(BF)
    key_all = rotate(split(dot(act_one, full_key) + key_shift), cosine, sine).astype(BF)
    value_all = split((dot(act_one, full_value) + value_shift).astype(BF))

    allowed = (place[None, :] <= place[:, None])[None]

    def masked_scores(query, key):
        scores = jnp.einsum("qhd,khd->hqk", query, key, preferred_element_type=F32) * 0.125
        return jnp.where(allowed, scores, -1e30)

    def attend(qkv):
        query, key, value = qkv
        scores = masked_scores(query, key)
        top = jnp.max(scores, axis=-1, keepdims=True)
        weights = jnp.exp(scores - top)
        totals = jnp.sum(weights, axis=-1, keepdims=True)
        probs = (weights / totals).astype(BF)
        context = jnp.einsum("hqk,khd->qhd", probs, value, preferred_element_type=F32)
        return context.astype(BF), top + jnp.log(totals)

    contexts, log_totals = lax.map(attend, (query_all, key_all, value_all))
    context_all = contexts.reshape(tokens, cols)

    cot_all = at.gather_rows(cot_own)

    hidden = input_single + at.scatter_rows(times_transposed(context_all, full_out).astype(BF))
    normed_two, unit_two, inverse_two = norm_forward(hidden, gain_two, bias_two)
    act_two = at.gather_rows(normed_two.astype(BF))
    gate = dot(act_two, full_gate)
    upward = dot(act_two, full_up)
    sigmoid_gate = jax.nn.sigmoid(gate)
    swish = gate * sigmoid_gate
    inner = (swish * upward).astype(BF)
    down_share = at.scatter_grad(over_rows(cot_all, inner).astype(BF))
    d_inner = dot(cot_all, full_down)
    d_gate = (d_inner * upward * sigmoid_gate * (1.0 + gate * (1.0 - sigmoid_gate))).astype(BF)
    d_upward = (d_inner * swish).astype(BF)
    d_act_two = at.scatter_rows(
        (times_transposed(d_gate, full_gate) + times_transposed(d_upward, full_up)).astype(BF)
    )
    gate_share = at.scatter_grad(over_rows(act_two, d_gate).astype(BF))
    up_share = at.scatter_grad(over_rows(act_two, d_upward).astype(BF))
    block_output = (
        hidden + at.scatter_rows(times_transposed(inner, full_down).astype(BF))
    ).astype(BF)

    d_norm_two, gain_two_part, bias_two_part = norm_backward(
        d_act_two, unit_two, inverse_two, gain_two
    )
    d_hidden = cot_own.astype(F32) + d_norm_two
    d_hidden_all = at.gather_rows(d_hidden.astype(BF))
    d_context = split(dot(d_hidden_all, full_out).astype(BF))
    out_share = at.scatter_grad(over_rows(d_hidden_all, context_all).astype(BF))

    def attend_back(args):
        query, key, value, d_ctx, log_total = args
        probs = jnp.exp(masked_scores(query, key) - log_total)
        d_probs = jnp.einsum("qhd,khd->hqk", d_ctx, value, preferred_element_type=F32)
        row_dot = jnp.sum(probs * d_probs, axis=-1, keepdims=True)
        d_scores = (0.125 * probs * (d_probs - row_dot)).astype(BF)
        d_query = jnp.einsum("hqk,khd->qhd", d_scores, key, preferred_element_type=F32)
        d_key = jnp.einsum("hqk,qhd->khd", d_scores, query, preferred_element_type=F32)
        d_value = jnp.einsum("hqk,qhd->khd", probs.astype(BF), d_ctx, preferred_element_type=F32)
        return d_query, d_key, d_value

    d_query_rot, d_key_rot, d_value_all = lax.map(
        attend_back, (query_all, key_all, value_all, d_context, log_totals)
    )
    d_query_pre = rotate(d_query_rot, cosine, -sine).reshape(tokens, cols).astype(BF)
    d_key_pre = rotate(d_key_rot, cosine, -sine).reshape(tokens, cols).astype(BF)
    d_value_pre = d_value_all.reshape(tokens, cols).astype(BF)
    d_act_one = at.scatter_rows(
        (
            times_transposed(d_query_pre, full_query)
            + times_transposed(d_key_pre, full_key)
            + times_transposed(d_value_pre, full_value)
        ).astype(BF)
    )
    query_share = at.scatter_grad(over_rows(act_one, d_query_pre).astype(BF))
    key_share = at.scatter_grad(over_rows(act_one, d_key_pre).astype(BF))
    value_share = at.scatter_grad(over_rows(act_one, d_value_pre).astype(BF))
    d_norm_one, gain_one_part, bias_one_part = norm_backward(
        d_act_one, unit_one, inverse_one, gain_one
    )
    input_grad = d_hidden + d_norm_one

    query_part = jnp.sum(d_query_pre.astype(F32), axis=0)
    value_part = jnp.sum(d_value_pre.astype(F32), axis=0)
    key_part = (
        jnp.sum(d_key_pre.astype(F32), axis=0).reshape(heads, HEAD)[:, :ROT].reshape(heads * ROT)
    )
    query_full = lax.dynamic_update_slice(jnp.zeros(q_bias.shape, F32), query_part, (column,))
    value_full = lax.dynamic_update_slice(jnp.zeros(v_bias.shape, F32), value_part, (column,))
    key_full = lax.dynamic_update_slice(jnp.zeros(k_bias.shape, F32), key_part, (key_column,))
    early = at.sum_all(
        jnp.concatenate(
            [
                rolled(gain_two_part, True),
                rolled(bias_two_part, True),
                query_full,
                value_full,
                key_full,
            ]
        )
    )
    late = at.sum_all(
        jnp.concatenate([rolled(gain_one_part, True), rolled(bias_one_part, True)])
    )
    n = width
    return (
        rolled(block_output, True),
        rolled(input_grad, True),
        late[:n],
        late[n:],
        query_share,
        early[2 * n : 3 * n],
        key_share,
        early[4 * n :],
        value_share,
        early[3 * n : 4 * n],
        out_share,
        early[:n],
        early[n : 2 * n],
        gate_share,
        up_share,
        down_share,
    )


def solution(mesh):
    rows = P(("dp", "tensor"), None)
    matrix = P("dp", "tensor")
    return jax.shard_map(
        functools.partial(local, mesh.shape["dp"], mesh.shape["tensor"]),
        mesh=mesh,
        in_specs=(
            rows, rows, P(), P(), matrix, P(), matrix, P(), matrix, P(), matrix, P(), P(),
            matrix, matrix, matrix,
        ),
        out_specs=(
            rows, rows, P(), P(), matrix, P(), matrix, P(), matrix, P(), matrix, P(), P(),
            matrix, matrix, matrix,
        ),
        check_vma=False,
    )
```

```python
import functools

import jax
import jax.numpy as jnp
from jax import lax
from jax.experimental import pallas as pl
from jax.experimental.pallas import tpu as pltpu
from jax.sharding import PartitionSpec as P

HEAD = 64
ROT = 16
EPS = 1e-05
BF = jnp.bfloat16
F32 = jnp.float32


def norm_forward(values, gain_vec, shift_vec):
    row_mean = jnp.mean(values, axis=-1, keepdims=True)
    centered = values - row_mean
    variance = jnp.mean(centered * centered, axis=-1, keepdims=True)
    inverse = lax.rsqrt(variance + EPS)
    normed = centered * inverse
    return (normed * gain_vec + shift_vec, normed, inverse)


def norm_backward(upstream, normed, inverse, gain_vec):
    scaled = upstream * gain_vec
    adjusted = (
        scaled
        - jnp.mean(scaled, axis=-1, keepdims=True)
        - normed * jnp.mean(scaled * normed, axis=-1, keepdims=True)
    )
    return (inverse * adjusted, jnp.sum(upstream * normed, axis=0), jnp.sum(upstream, axis=0))


def dot(left, right):
    return jnp.dot(left, right, preferred_element_type=F32)


def times_transposed(left, right):
    return lax.dot_general(left, right, (((1,), (1,)), ((), ())), preferred_element_type=F32)


def over_rows(left, right):
    return lax.dot_general(left, right, (((0,), (0,)), ((), ())), preferred_element_type=F32)


def dot_nt(left, right):
    return times_transposed(left, right)


def head_mask(shape, head):
    lane = lax.broadcasted_iota(jnp.int32, shape, len(shape) - 1)
    return (lane >= head * HEAD) & (lane < (head + 1) * HEAD)


def turn(values, cosine, sine):
    half = ROT // 2
    parts = []
    for start in range(0, values.shape[1], 128):
        v = values[:, start : start + 128]
        lane = lax.broadcasted_iota(jnp.int32, v.shape, 1) % HEAD
        other = jnp.where(lane < half, pltpu.roll(v, 128 - half, 1), pltpu.roll(v, half, 1))
        parts.append(v * cosine + other * sine)
    return jnp.concatenate(parts, 1)


def turn_tables(place):
    half = ROT // 2
    frequency = 10000.0 ** (-2.0 * jnp.arange(half, dtype=F32) / ROT)
    angles = place.astype(F32)[:, None] * frequency[None, :]
    cosine, sine = jnp.cos(angles), jnp.sin(angles)
    rest = jnp.ones((place.shape[0], HEAD - ROT), F32)
    one = jnp.concatenate([cosine, cosine, rest], 1)
    two = jnp.concatenate([-sine, sine, 0.0 * rest], 1)
    return jnp.concatenate([one, one], 1), jnp.concatenate([two, two], 1)


def attend_kernel(me, pre, shift, cosine, sine, qkv, context, log_total):
    slots, rows, wide = pre.shape[1:]
    cols = wide // 3
    heads = cols // HEAD
    for s in range(slots):
        for part in range(3):
            at = slice(part * cols, (part + 1) * cols)
            v = pre[0, s, :, at] + shift[:, at]
            if part < 2:
                v = turn(v, cosine[s], sine[s])
            qkv[0, s, :, at] = v.astype(BF)
    where = [jnp.bitwise_xor(me[0], b) for b in range(slots)]
    key_row = lax.broadcasted_iota(jnp.int32, (rows, rows), 1)
    query_row = lax.broadcasted_iota(jnp.int32, (rows, rows), 0)
    lane = lax.broadcasted_iota(jnp.int32, (rows, 128), 1)
    for i in range(slots):
        query = qkv[0, where[i], :, :cols] * jnp.asarray(0.125, BF)
        total_context = jnp.zeros((rows, cols), F32)
        logs = jnp.zeros((rows, 128), F32)
        for h in range(heads):
            mask = head_mask((rows, cols), h)
            one = jnp.where(mask, query, jnp.zeros_like(query))
            scores = [dot_nt(one, qkv[0, where[j], :, cols : 2 * cols]) for j in range(i + 1)]
            scores[i] = jnp.where(key_row <= query_row, scores[i], -1e30)
            top = jnp.max(functools.reduce(jnp.maximum, scores), 1, keepdims=True)
            weights = [jnp.exp(v - top) for v in scores]
            total = jnp.sum(functools.reduce(jnp.add, weights), 1, keepdims=True)
            mixed = functools.reduce(
                jnp.add,
                [dot(w.astype(BF), qkv[0, where[j], :, 2 * cols :]) for j, w in enumerate(weights)],
            )
            total_context = jnp.where(mask, mixed * (1.0 / total), total_context)
            logs = jnp.where(lane == h, top + jnp.log(total), logs)
        context[0, where[i]] = total_context.astype(BF)
        log_total[0, i] = logs.T[:8]


def attend(me, pre, shift, cosine, sine):
    two, slots, rows, wide = pre.shape
    cols = wide // 3

    def seq(*dims):
        return pl.BlockSpec((1, *dims), lambda i, me: (i,) + (0,) * len(dims))

    def whole(*dims):
        return pl.BlockSpec(dims, lambda i, me: (0,) * len(dims))

    pairs = two * slots * (slots + 1) // 2 * (cols // HEAD)
    return pl.pallas_call(
        attend_kernel,
        grid_spec=pltpu.PrefetchScalarGridSpec(
            num_scalar_prefetch=1,
            grid=(two,),
            in_specs=[seq(slots, rows, wide), whole(1, wide), whole(slots, rows, 128), whole(slots, rows, 128)],
            out_specs=[seq(slots, rows, wide), seq(slots, rows, cols), seq(slots, 8, rows)],
        ),
        out_shape=[
            jax.ShapeDtypeStruct((two, slots, rows, wide), BF),
            jax.ShapeDtypeStruct((two, slots, rows, cols), BF),
            jax.ShapeDtypeStruct((two, slots, 8, rows), F32),
        ],
        compiler_params=pltpu.CompilerParams(vmem_limit_bytes=40 * 2**20),
        cost_estimate=pl.CostEstimate(
            flops=4 * pairs * rows * rows * cols,
            bytes_accessed=two * slots * rows * wide * 8,
            transcendentals=pairs * rows * rows,
        ),
        name="attend",
    )(me, pre, shift, cosine, sine)


def attend_back_kernel(
    me, qkv, context, d_context, log_total, cosine, sine, d_qkv, sums, query, upstream, d_query, delta
):
    slots, rows, wide = qkv.shape[1:]
    cols = wide // 3
    heads = cols // HEAD
    where = [jnp.bitwise_xor(me[0], b) for b in range(slots)]
    row = lax.broadcasted_iota(jnp.int32, (8, cols), 0)
    picks = jnp.zeros((8, cols), F32)
    for h in range(heads):
        picks = jnp.where((row == h) & head_mask((8, cols), h), 1.0, picks)
    picks = picks.astype(BF)
    for i in range(slots):
        at = slice(i * rows, (i + 1) * rows)
        query[at] = qkv[0, where[i], :, :cols] * jnp.asarray(0.125, BF)
        up = d_context[0, where[i]]
        upstream[at] = up
        product = up.astype(F32) * context[0, where[i]].astype(F32)
        high = product.astype(BF)
        low = (product - high.astype(F32)).astype(BF)
        delta[:, at] = dot_nt(picks, high) + dot_nt(picks, low)
    key_row = lax.broadcasted_iota(jnp.int32, (rows, rows), 0)
    query_row = lax.broadcasted_iota(jnp.int32, (rows, rows), 1)
    total_sums = [jnp.zeros((1, cols), F32) for _ in range(3)]
    for j in range(slots):
        key = qkv[0, where[j], :, cols : 2 * cols]
        value = qkv[0, where[j], :, 2 * cols :]
        d_key = jnp.zeros((rows, cols), F32)
        d_value = jnp.zeros((rows, cols), F32)
        for h in range(heads):
            mask = head_mask((rows, cols), h)
            key_one = jnp.where(mask, key, jnp.zeros_like(key))
            value_one = jnp.where(mask, value, jnp.zeros_like(value))
            for i in range(j, slots):
                at = slice(i * rows, (i + 1) * rows)
                query_here, up_here = query[at], upstream[at]
                scores = dot_nt(key_one, query_here)
                if i == j:
                    scores = jnp.where(key_row <= query_row, scores, -1e30)
                probs = jnp.exp(scores - log_total[0, i, h : h + 1, :])
                d_probs = dot_nt(value_one, up_here)
                d_scores = (probs * (d_probs - delta[h : h + 1, at])).astype(BF)
                d_value = jnp.where(mask, d_value + dot(probs.astype(BF), up_here), d_value)
                d_key = jnp.where(mask, d_key + dot(d_scores, query_here), d_key)
                d_query_part = over_rows(d_scores, key_one)
                if j == 0 and h == 0:
                    d_query[at] = d_query_part
                else:
                    d_query[at] += d_query_part
        s = where[j]
        d_key_low = turn(d_key, cosine[s], -sine[s]).astype(BF)
        d_value_low = d_value.astype(BF)
        d_qkv[0, s, :, cols : 2 * cols] = d_key_low
        d_qkv[0, s, :, 2 * cols :] = d_value_low
        d_query_low = turn(d_query[j * rows : (j + 1) * rows] * 0.125, cosine[s], -sine[s]).astype(BF)
        d_qkv[0, s, :, :cols] = d_query_low
        for part, v in enumerate((d_query_low, d_key_low, d_value_low)):
            total_sums[part] += jnp.sum(v.astype(F32), 0, keepdims=True)
    sums[0] = jnp.concatenate(total_sums, 1)


def attend_back(me, qkv, context, d_context, log_total, cosine, sine):
    two, slots, rows, wide = qkv.shape
    cols = wide // 3

    def seq(*dims):
        return pl.BlockSpec((1, *dims), lambda i, me: (i,) + (0,) * len(dims))

    def whole(*dims):
        return pl.BlockSpec(dims, lambda i, me: (0,) * len(dims))

    pairs = two * slots * (slots + 1) // 2 * (cols // HEAD)
    return pl.pallas_call(
        attend_back_kernel,
        grid_spec=pltpu.PrefetchScalarGridSpec(
            num_scalar_prefetch=1,
            grid=(two,),
            in_specs=[
                seq(slots, rows, wide),
                seq(slots, rows, cols),
                seq(slots, rows, cols),
                seq(slots, 8, rows),
                whole(slots, rows, 128),
                whole(slots, rows, 128),
            ],
            out_specs=[seq(slots, rows, wide), seq(1, wide)],
            scratch_shapes=[
                pltpu.VMEM((slots * rows, cols), BF),
                pltpu.VMEM((slots * rows, cols), BF),
                pltpu.VMEM((slots * rows, cols), F32),
                pltpu.VMEM((8, slots * rows), F32),
            ],
        ),
        out_shape=[
            jax.ShapeDtypeStruct((two, slots, rows, wide), BF),
            jax.ShapeDtypeStruct((two, 1, wide), F32),
        ],
        compiler_params=pltpu.CompilerParams(vmem_limit_bytes=40 * 2**20),
        cost_estimate=pl.CostEstimate(
            flops=10 * pairs * rows * rows * cols,
            bytes_accessed=two * slots * rows * wide * 8,
            transcendentals=pairs * rows * rows,
        ),
        name="attend_back",
    )(me, qkv, context, d_context, log_total, cosine, sine)


class Place:
    def __init__(self, n_dp, n_tensor):
        self.n_dp, self.n_tensor = n_dp, n_tensor
        self.n_line = n_dp // 2
        dp, tensor = lax.axis_index("dp"), lax.axis_index("tensor")
        self.dp, self.tensor = dp, tensor
        self.line, self.pair = dp // 2, dp % 2

    def to_pair(self, v):
        return lax.ppermute(v, "dp", [(i, i ^ 1) for i in range(self.n_dp)])

    def to_side(self, v):
        return lax.ppermute(v, "tensor", [(i, i ^ 2) for i in range(self.n_tensor)])

    def to_core(self, v):
        return lax.ppermute(v, "tensor", [(i, i ^ 1) for i in range(self.n_tensor)])

    def by_pair(self, first, second, axis):
        return jnp.where(
            self.pair == 0,
            jnp.concatenate([first, second], axis),
            jnp.concatenate([second, first], axis),
        )

    def halves(self, v, axis):
        half = v.shape[axis] // 2
        low = lax.slice_in_dim(v, 0, half, axis=axis)
        high = lax.slice_in_dim(v, half, 2 * half, axis=axis)
        return jnp.where(self.pair == 0, low, high), jnp.where(self.pair == 0, high, low)

    def line_groups(self):
        return [[2 * i + p for i in range(self.n_line)] for p in (0, 1)]

    def widen(self, *weights):
        mine, theirs = zip(*[self.halves(w, 1) for w in weights])
        mine, theirs = jnp.concatenate(mine, 1), jnp.concatenate(theirs, 1)
        return self.by_pair(mine, self.to_pair(theirs), 0)

    def gather_weight(self, piece):
        return lax.all_gather(piece, "dp", axis=0, tiled=True, axis_index_groups=self.line_groups())

    def scatter_grad(self, *grads):
        total = lax.psum_scatter(
            jnp.concatenate(grads, 1),
            "dp",
            scatter_dimension=0,
            tiled=True,
            axis_index_groups=self.line_groups(),
        )
        mine, theirs = self.halves(total, 0)
        other = self.to_pair(theirs)
        shares, start = [], 0
        for g in grads:
            stop = start + g.shape[1]
            shares.append(self.by_pair(mine[:, start:stop], other[:, start:stop], 1).astype(F32))
            start = stop
        return shares

    def gather_rows(self, a):
        half = a.shape[0] // 2
        h1, h2 = a[:half], a[half:]
        x1, y2 = self.to_side(h1), self.to_pair(h2)
        own_core = self.to_core(a)
        first_core = self.to_core(jnp.stack([x1, y2]))
        y1 = self.to_pair(jnp.stack([h1, x1]))
        x2 = self.to_side(jnp.stack([h2, y2]))
        second = jnp.stack([y1, x2])
        second_core = self.to_core(second)

        def table(own, first, last):
            y1, x2 = last[0], last[1]
            r00 = own
            r01 = jnp.concatenate([first[0], x2[0]], 0)
            r10 = jnp.concatenate([y1[0], first[1]], 0)
            r11 = jnp.concatenate([y1[1], x2[1]], 0)
            return r00, r01, r10, r11

        m = table(a, jnp.stack([x1, y2]), second)
        o = table(own_core, first_core, second_core)
        return jnp.concatenate([m[0], o[0], m[1], o[1], m[2], o[2], m[3], o[3]], 0)

    def scatter_rows(self, p):
        rows = p.shape[0] // 8
        p = p.reshape(2, 2, 2, rows, p.shape[1])
        keep, send = p[:, :, 0], p[:, :, 1]
        acc = (keep.astype(F32) + self.to_core(send).astype(F32)).astype(BF)
        half = rows // 2
        h1, h2 = acc[:, :, :half], acc[:, :, half:]
        r1 = self.to_side(h1[:, 1])
        r2 = self.to_pair(h2[1])
        b1 = (h1[:, 0].astype(F32) + r1.astype(F32)).astype(BF)
        b2 = (h2[0].astype(F32) + r2.astype(F32)).astype(BF)
        s1 = self.to_pair(b1[1])
        s2 = self.to_side(b2[1])
        return jnp.concatenate(
            [b1[0].astype(F32) + s1.astype(F32), b2[0].astype(F32) + s2.astype(F32)], 0
        )

    def sum_all(self, v):
        step = 1
        while step < self.n_tensor:
            v = v + lax.ppermute(v, "tensor", [(i, i ^ step) for i in range(self.n_tensor)])
            step *= 2
        step = 1
        while step < self.n_dp:
            v = v + lax.ppermute(v, "dp", [(i, i ^ step) for i in range(self.n_dp)])
            step *= 2
        return v


def local(
    n_dp,
    n_tensor,
    block_input,
    cotangent,
    ln1_gain,
    ln1_bias,
    w_query,
    q_bias,
    w_key,
    k_bias,
    w_value,
    v_bias,
    w_out,
    ln2_gain,
    ln2_bias,
    w_gate,
    w_up,
    w_down,
):
    at = Place(n_dp, n_tensor)
    width = block_input.shape[1]
    rows = block_input.shape[0]
    length = rows * n_tensor
    gain_one, bias_one, gain_two, bias_two = ln1_gain, ln1_bias, ln2_gain, ln2_bias
    input_single = block_input.astype(F32)

    cols = w_query.shape[1] // 2
    heads = cols // HEAD
    ff = w_gate.shape[1] // 2
    full_attn = at.gather_weight(at.widen(w_query, w_key, w_value, w_out))
    full_qkv, full_out = full_attn[:, : 3 * cols], full_attn[:, 3 * cols :]
    full_wide = at.gather_weight(at.widen(w_gate, w_up))
    full_down = at.gather_weight(at.widen(w_down))

    column = at.tensor * 2 * cols + at.pair * cols
    query_shift = lax.dynamic_slice_in_dim(q_bias, column, cols)
    value_shift = lax.dynamic_slice_in_dim(v_bias, column, cols)
    key_column = at.tensor * 2 * heads * ROT + at.pair * heads * ROT
    key_rows = lax.dynamic_slice_in_dim(k_bias, key_column, heads * ROT)
    key_shift = jnp.pad(key_rows.reshape(heads, ROT), ((0, 0), (0, HEAD - ROT))).reshape(cols)

    normed_one, unit_one, inverse_one = norm_forward(input_single, gain_one, bias_one)
    act_one = at.gather_rows(normed_one.astype(BF))
    tokens = act_one.shape[0]

    slots = jnp.arange(n_tensor)
    place = ((at.tensor ^ slots)[:, None] * rows + jnp.arange(rows)[None, :]).reshape(length)
    cosine, sine = (v.reshape(n_tensor, rows, 128) for v in turn_tables(place))
    me = at.tensor.astype(jnp.int32).reshape(1)
    shift = jnp.concatenate([query_shift, key_shift, value_shift])[None]

    pre = dot(act_one, full_qkv).reshape(2, n_tensor, rows, 3 * cols)
    qkv, context, log_total = attend(me, pre, shift, cosine, sine)
    context_all = context.reshape(tokens, cols)

    cot_all = at.gather_rows(cotangent)

    hidden = input_single + at.scatter_rows(times_transposed(context_all, full_out).astype(BF))
    normed_two, unit_two, inverse_two = norm_forward(hidden, gain_two, bias_two)
    act_two = at.gather_rows(normed_two.astype(BF))
    wide = dot(act_two, full_wide)
    gate, upward = wide[:, :ff], wide[:, ff:]
    sigmoid_gate = jax.nn.sigmoid(gate)
    swish = gate * sigmoid_gate
    inner = (swish * upward).astype(BF)
    (down_share,) = at.scatter_grad(over_rows(cot_all, inner).astype(BF))
    d_inner = dot(cot_all, full_down)
    d_gate = (d_inner * upward * sigmoid_gate * (1.0 + gate * (1.0 - sigmoid_gate))).astype(BF)
    d_upward = (d_inner * swish).astype(BF)
    d_wide = jnp.concatenate([d_gate, d_upward], 1)
    d_act_two = at.scatter_rows(times_transposed(d_wide, full_wide).astype(BF))
    wide_grad = over_rows(act_two, d_wide).astype(BF)
    gate_share, up_share = at.scatter_grad(wide_grad[:, :ff], wide_grad[:, ff:])
    block_output = (
        hidden + at.scatter_rows(times_transposed(inner, full_down).astype(BF))
    ).astype(BF)

    d_norm_two, gain_two_part, bias_two_part = norm_backward(
        d_act_two, unit_two, inverse_two, gain_two
    )
    d_hidden = cotangent.astype(F32) + d_norm_two
    d_hidden_all = at.gather_rows(d_hidden.astype(BF))
    d_context = dot(d_hidden_all, full_out).astype(BF).reshape(context.shape)
    out_grad = over_rows(d_hidden_all, context_all).astype(BF)

    d_qkv, sums = attend_back(me, qkv, context, d_context, log_total, cosine, sine)
    d_qkv = d_qkv.reshape(tokens, 3 * cols)
    sums = jnp.sum(sums[:, 0], axis=0)
    d_act_one = at.scatter_rows(times_transposed(d_qkv, full_qkv).astype(BF))
    qkv_grad = over_rows(act_one, d_qkv).astype(BF)
    query_share, key_share, value_share, out_share = at.scatter_grad(
        qkv_grad[:, :cols], qkv_grad[:, cols : 2 * cols], qkv_grad[:, 2 * cols :], out_grad
    )
    d_norm_one, gain_one_part, bias_one_part = norm_backward(
        d_act_one, unit_one, inverse_one, gain_one
    )
    input_grad = d_hidden + d_norm_one

    query_part, value_part = sums[:cols], sums[2 * cols :]
    key_part = sums[cols : 2 * cols].reshape(heads, HEAD)[:, :ROT].reshape(heads * ROT)
    query_full = lax.dynamic_update_slice(jnp.zeros(q_bias.shape, F32), query_part, (column,))
    value_full = lax.dynamic_update_slice(jnp.zeros(v_bias.shape, F32), value_part, (column,))
    key_full = lax.dynamic_update_slice(jnp.zeros(k_bias.shape, F32), key_part, (key_column,))
    early = at.sum_all(
        jnp.concatenate(
            [
                gain_two_part,
                bias_two_part,
                query_full,
                value_full,
                key_full,
            ]
        )
    )
    late = at.sum_all(
        jnp.concatenate([gain_one_part, bias_one_part])
    )
    n = width
    return (
        block_output,
        input_grad,
        late[:n],
        late[n:],
        query_share,
        early[2 * n : 3 * n],
        key_share,
        early[4 * n :],
        value_share,
        early[3 * n : 4 * n],
        out_share,
        early[:n],
        early[n : 2 * n],
        gate_share,
        up_share,
        down_share,
    )


def solution(mesh):
    rows = P(("dp", "tensor"), None)
    matrix = P("dp", "tensor")
    return jax.shard_map(
        functools.partial(local, mesh.shape["dp"], mesh.shape["tensor"]),
        mesh=mesh,
        in_specs=(
            rows, rows, P(), P(), matrix, P(), matrix, P(), matrix, P(), matrix, P(), P(),
            matrix, matrix, matrix,
        ),
        out_specs=(
            rows, rows, P(), P(), matrix, P(), matrix, P(), matrix, P(), matrix, P(), P(),
            matrix, matrix, matrix,
        ),
        check_vma=False,
    )
```

```python
import functools

import jax
import jax.numpy as jnp
from jax import lax
from jax.experimental import pallas as pl
from jax.experimental.pallas import tpu as pltpu
from jax.sharding import PartitionSpec as P

HEAD = 64
ROT = 16
EPS = 1e-05
LITTLE = pl.CostEstimate(flops=0, bytes_accessed=0, transcendentals=0)
BF = jnp.bfloat16
F32 = jnp.float32


def dot(left, right):
    return jnp.dot(left, right, preferred_element_type=F32)


def times_transposed(left, right):
    return lax.dot_general(left, right, (((1,), (1,)), ((), ())), preferred_element_type=F32)


def over_rows(left, right):
    return lax.dot_general(left, right, (((0,), (0,)), ((), ())), preferred_element_type=F32)


def dot_nt(left, right):
    return times_transposed(left, right)


def after(value, *others):
    return lax.optimization_barrier((value, *others))[0]


def all_after(values, *others):
    return lax.optimization_barrier((*values, *others))[: len(values)]


def head_mask(shape, head):
    lane = lax.broadcasted_iota(jnp.int32, shape, len(shape) - 1)
    return (lane >= head * HEAD) & (lane < (head + 1) * HEAD)


def turn(values, cosine, sine):
    half = ROT // 2
    parts = []
    for start in range(0, values.shape[1], 128):
        v = values[:, start : start + 128]
        lane = lax.broadcasted_iota(jnp.int32, v.shape, 1) % HEAD
        other = jnp.where(lane < half, pltpu.roll(v, 128 - half, 1), pltpu.roll(v, half, 1))
        parts.append(v * cosine + other * sine)
    return jnp.concatenate(parts, 1)


def turn_tables(place):
    half = ROT // 2
    frequency = 10000.0 ** (-2.0 * jnp.arange(half, dtype=F32) / ROT)
    angles = place.astype(F32)[:, None] * frequency[None, :]
    cosine, sine = jnp.cos(angles), jnp.sin(angles)
    rest = jnp.ones((place.shape[0], HEAD - ROT), F32)
    one = jnp.concatenate([cosine, cosine, rest], 1)
    two = jnp.concatenate([-sine, sine, 0.0 * rest], 1)
    return jnp.concatenate([one, one], 1), jnp.concatenate([two, two], 1)


def attend_kernel(me, pre, shift, cosine, sine, qkv, context, log_total):
    slots, rows, wide = pre.shape[1:]
    cols = wide // 3
    heads = cols // HEAD
    for s in range(slots):
        for part in range(3):
            at = slice(part * cols, (part + 1) * cols)
            v = pre[0, s, :, at] + shift[:, at]
            if part < 2:
                v = turn(v, cosine[s], sine[s])
            qkv[0, s, :, at] = v.astype(BF)
    where = [jnp.bitwise_xor(me[0], b) for b in range(slots)]
    key_row = lax.broadcasted_iota(jnp.int32, (rows, rows), 1)
    query_row = lax.broadcasted_iota(jnp.int32, (rows, rows), 0)
    lane = lax.broadcasted_iota(jnp.int32, (rows, 128), 1)
    for i in range(slots):
        query = qkv[0, where[i], :, :cols] * jnp.asarray(0.125, BF)
        total_context = jnp.zeros((rows, cols), F32)
        logs = jnp.zeros((rows, 128), F32)
        for h in range(heads):
            mask = head_mask((rows, cols), h)
            one = jnp.where(mask, query, jnp.zeros_like(query))
            scores = [dot_nt(one, qkv[0, where[j], :, cols : 2 * cols]) for j in range(i + 1)]
            scores[i] = jnp.where(key_row <= query_row, scores[i], -1e30)
            top = jnp.max(functools.reduce(jnp.maximum, scores), 1, keepdims=True)
            weights = [jnp.exp(v - top) for v in scores]
            total = jnp.sum(functools.reduce(jnp.add, weights), 1, keepdims=True)
            mixed = functools.reduce(
                jnp.add,
                [dot(w.astype(BF), qkv[0, where[j], :, 2 * cols :]) for j, w in enumerate(weights)],
            )
            total_context = jnp.where(mask, mixed * (1.0 / total), total_context)
            logs = jnp.where(lane == h, top + jnp.log(total), logs)
        context[0, where[i]] = total_context.astype(BF)
        log_total[0, i] = logs.T[:8]


def attend(me, pre, shift, cosine, sine):
    two, slots, rows, wide = pre.shape
    cols = wide // 3

    def seq(*dims):
        return pl.BlockSpec((1, *dims), lambda i, me: (i,) + (0,) * len(dims))

    def whole(*dims):
        return pl.BlockSpec(dims, lambda i, me: (0,) * len(dims))

    pairs = two * slots * (slots + 1) // 2 * (cols // HEAD)
    return pl.pallas_call(
        attend_kernel,
        grid_spec=pltpu.PrefetchScalarGridSpec(
            num_scalar_prefetch=1,
            grid=(two,),
            in_specs=[seq(slots, rows, wide), whole(1, wide), whole(slots, rows, 128), whole(slots, rows, 128)],
            out_specs=[seq(slots, rows, wide), seq(slots, rows, cols), seq(slots, 8, rows)],
        ),
        out_shape=[
            jax.ShapeDtypeStruct((two, slots, rows, wide), BF),
            jax.ShapeDtypeStruct((two, slots, rows, cols), BF),
            jax.ShapeDtypeStruct((two, slots, 8, rows), F32),
        ],
        compiler_params=pltpu.CompilerParams(vmem_limit_bytes=40 * 2**20),
        cost_estimate=LITTLE,
        name="attend",
    )(me, pre, shift, cosine, sine)


def attend_back_kernel(
    me, qkv, context, d_context, log_total, cosine, sine, d_qkv, sums, query, upstream, d_query, delta
):
    slots, rows, wide = qkv.shape[1:]
    cols = wide // 3
    heads = cols // HEAD
    where = [jnp.bitwise_xor(me[0], b) for b in range(slots)]
    row = lax.broadcasted_iota(jnp.int32, (8, cols), 0)
    picks = jnp.zeros((8, cols), F32)
    for h in range(heads):
        picks = jnp.where((row == h) & head_mask((8, cols), h), 1.0, picks)
    picks = picks.astype(BF)
    for i in range(slots):
        at = slice(i * rows, (i + 1) * rows)
        query[at] = qkv[0, where[i], :, :cols] * jnp.asarray(0.125, BF)
        up = d_context[0, where[i]]
        upstream[at] = up
        product = up.astype(F32) * context[0, where[i]].astype(F32)
        high = product.astype(BF)
        low = (product - high.astype(F32)).astype(BF)
        delta[:, at] = dot_nt(picks, high) + dot_nt(picks, low)
    key_row = lax.broadcasted_iota(jnp.int32, (rows, rows), 0)
    query_row = lax.broadcasted_iota(jnp.int32, (rows, rows), 1)
    total_sums = [jnp.zeros((1, cols), F32) for _ in range(3)]
    for j in range(slots):
        key = qkv[0, where[j], :, cols : 2 * cols]
        value = qkv[0, where[j], :, 2 * cols :]
        d_key = jnp.zeros((rows, cols), F32)
        d_value = jnp.zeros((rows, cols), F32)
        for h in range(heads):
            mask = head_mask((rows, cols), h)
            key_one = jnp.where(mask, key, jnp.zeros_like(key))
            value_one = jnp.where(mask, value, jnp.zeros_like(value))
            for i in range(j, slots):
                at = slice(i * rows, (i + 1) * rows)
                query_here, up_here = query[at], upstream[at]
                scores = dot_nt(key_one, query_here)
                if i == j:
                    scores = jnp.where(key_row <= query_row, scores, -1e30)
                probs = jnp.exp(scores - log_total[0, i, h : h + 1, :])
                d_probs = dot_nt(value_one, up_here)
                d_scores = (probs * (d_probs - delta[h : h + 1, at])).astype(BF)
                d_value = jnp.where(mask, d_value + dot(probs.astype(BF), up_here), d_value)
                d_key = jnp.where(mask, d_key + dot(d_scores, query_here), d_key)
                d_query_part = over_rows(d_scores, key_one)
                if j == 0 and h == 0:
                    d_query[at] = d_query_part
                else:
                    d_query[at] += d_query_part
        s = where[j]
        d_key_low = turn(d_key, cosine[s], -sine[s]).astype(BF)
        d_value_low = d_value.astype(BF)
        d_qkv[0, s, :, cols : 2 * cols] = d_key_low
        d_qkv[0, s, :, 2 * cols :] = d_value_low
        d_query_low = turn(d_query[j * rows : (j + 1) * rows] * 0.125, cosine[s], -sine[s]).astype(BF)
        d_qkv[0, s, :, :cols] = d_query_low
        for part, v in enumerate((d_query_low, d_key_low, d_value_low)):
            total_sums[part] += jnp.sum(v.astype(F32), 0, keepdims=True)
    sums[0] = jnp.concatenate(total_sums, 1)


def attend_back(me, qkv, context, d_context, log_total, cosine, sine):
    two, slots, rows, wide = qkv.shape
    cols = wide // 3

    def seq(*dims):
        return pl.BlockSpec((1, *dims), lambda i, me: (i,) + (0,) * len(dims))

    def whole(*dims):
        return pl.BlockSpec(dims, lambda i, me: (0,) * len(dims))

    return pl.pallas_call(
        attend_back_kernel,
        grid_spec=pltpu.PrefetchScalarGridSpec(
            num_scalar_prefetch=1,
            grid=(two,),
            in_specs=[
                seq(slots, rows, wide),
                seq(slots, rows, cols),
                seq(slots, rows, cols),
                seq(slots, 8, rows),
                whole(slots, rows, 128),
                whole(slots, rows, 128),
            ],
            out_specs=[seq(slots, rows, wide), seq(1, wide)],
            scratch_shapes=[
                pltpu.VMEM((slots * rows, cols), BF),
                pltpu.VMEM((slots * rows, cols), BF),
                pltpu.VMEM((slots * rows, cols), F32),
                pltpu.VMEM((8, slots * rows), F32),
            ],
        ),
        out_shape=[
            jax.ShapeDtypeStruct((two, slots, rows, wide), BF),
            jax.ShapeDtypeStruct((two, 1, wide), F32),
        ],
        compiler_params=pltpu.CompilerParams(vmem_limit_bytes=56 * 2**20),
        cost_estimate=LITTLE,
        name="attend_back",
    )(me, qkv, context, d_context, log_total, cosine, sine)


def feed_kernel(count, first, *refs):
    pieces, w = refs[:count], refs[count]
    act, inner, slope, swish, held, in_sem, out_sem = refs[-7:]
    step = pl.program_id(0)
    height = pieces[0].shape[0]
    rows, ff = inner.shape
    each = rows // height

    def bring(i):
        return pltpu.make_async_copy(pieces[i], held.at[pl.ds(i * height, height)], in_sem.at[i])

    def put(i):
        return pltpu.make_async_copy(
            held.at[pl.ds(i * height, height)], act.at[pl.ds(first + i * height, height)], out_sem.at[i]
        )

    @pl.when(step == 0)
    def _():
        for i in range(count):
            bring(i).start()

    for k in range(count // each):

        @pl.when(step == k)
        def _(k=k):
            for i in range(k * each, (k + 1) * each):
                bring(i).wait()
                put(i).start()

    here = held[pl.ds(pl.multiple_of(step * rows, rows), rows), :]
    wide = dot(here, w[...])
    gate, upward = wide[:, :ff], wide[:, ff:]
    sigmoid = 1.0 / (1.0 + jnp.exp(-gate))
    product = gate * sigmoid
    inner[...] = (product * upward).astype(BF)
    swish[...] = product.astype(BF)
    slope[...] = (upward * sigmoid * (1.0 + gate * (1.0 - sigmoid))).astype(BF)

    @pl.when(step == count // each - 1)
    def _():
        for i in range(count):
            put(i).wait()


def feed(pieces, rows, w, earlier=None, total=None):
    count = len(pieces)
    height, width = pieces[0].shape
    ff = w.shape[1] // 2
    all_rows = count * height
    first = 0 if earlier is None else total - all_rows
    kept = () if earlier is None else earlier
    block = pl.BlockSpec((rows, ff), lambda i: (i + first // rows, 0))
    return pl.pallas_call(
        functools.partial(feed_kernel, count, first),
        grid=(all_rows // rows,),
        in_specs=[pl.BlockSpec(memory_space=pltpu.HBM)] * count
        + [pl.BlockSpec(w.shape, lambda i: (0, 0))]
        + [pl.BlockSpec(memory_space=pltpu.HBM)] * len(kept),
        out_specs=[pl.BlockSpec(memory_space=pltpu.HBM), block, block, block],
        out_shape=[jax.ShapeDtypeStruct((total, width), BF)] + [jax.ShapeDtypeStruct((total, ff), BF)] * 3,
        scratch_shapes=[
            pltpu.VMEM((all_rows, width), BF),
            pltpu.SemaphoreType.DMA((count,)),
            pltpu.SemaphoreType.DMA((count,)),
        ],
        input_output_aliases={count + 1 + i: i for i in range(len(kept))},
        compiler_params=pltpu.CompilerParams(vmem_limit_bytes=56 * 2**20),
        cost_estimate=pl.CostEstimate(
            flops=2 * all_rows * width * 2 * ff, bytes_accessed=2 * w.size, transcendentals=0
        ),
        name="feed",
    )(*pieces, w, *kept)


def feed_back_kernel(sends, *refs):
    cot, down, w, slope, swish = refs[:5]
    d_wide, sent, kept = refs[-3:]
    step = pl.program_id(0)
    d_inner = dot(cot[...], down[...])
    d_gate = (d_inner * slope[...].astype(F32)).astype(BF)
    d_upward = (d_inner * swish[...].astype(F32)).astype(BF)
    both = jnp.concatenate([d_gate, d_upward], 1)
    d_wide[...] = both
    result = dot_nt(both, w[...]).astype(BF)

    @pl.when(step < sends)
    def _():
        sent[0] = result

    @pl.when(step >= sends)
    def _():
        kept[0] = result


def feed_back(cot, down, w, slope, swish, slots, rows, earlier=None):
    total, width = cot.shape
    ff = down.shape[1]
    sends = len(slots) // 2
    first, stride = slots[0], 2

    def slot(i):
        return jnp.where(i < sends, first + stride * i, first - 1 + stride * (i - sends))

    def whole_of(v):
        return pl.BlockSpec(v.shape, lambda i: (0, 0))

    narrow = pl.BlockSpec((rows, ff), lambda i: (slot(i), 0))
    part = jax.ShapeDtypeStruct((sends, rows, width), BF)
    extra = () if earlier is None else (earlier,)
    return pl.pallas_call(
        functools.partial(feed_back_kernel, sends),
        grid=(2 * sends,),
        in_specs=[
            pl.BlockSpec((rows, width), lambda i: (slot(i), 0)),
            whole_of(down),
            whole_of(w),
            narrow,
            narrow,
        ]
        + [pl.BlockSpec(memory_space=pl.ANY)] * len(extra),
        out_specs=[
            pl.BlockSpec((rows, 2 * ff), lambda i: (slot(i), 0)),
            pl.BlockSpec((1, rows, width), lambda i: (jnp.minimum(i, sends - 1), 0, 0)),
            pl.BlockSpec((1, rows, width), lambda i: (jnp.maximum(i - sends, 0), 0, 0)),
        ],
        out_shape=[jax.ShapeDtypeStruct((total, 2 * ff), BF), part, part],
        input_output_aliases={5: 0} if extra else {},
        compiler_params=pltpu.CompilerParams(vmem_limit_bytes=56 * 2**20),
        cost_estimate=pl.CostEstimate(
            flops=2 * 2 * sends * rows * width * 3 * ff,
            bytes_accessed=2 * (w.size + down.size + 2 * sends * rows * (2 * width + 4 * ff)),
            transcendentals=0,
        ),
        name="feed_back",
    )(cot, down, w, slope, swish, *extra)


def over_rows_kernel(*refs):
    out, start = refs[-1], 0
    for left, right in zip(refs[:-1:2], refs[1:-1:2]):
        stop = start + right.shape[1]
        out[:, start:stop] = over_rows(left[...], right[...]).astype(BF)
        start = stop


def weight_grad(*pairs, tile=512):
    rows, width = pairs[0][0].shape
    cols = sum(right.shape[1] for _, right in pairs)
    specs = []
    for _, right in pairs:
        specs += [pl.BlockSpec((rows, tile), lambda i: (0, i)), pl.BlockSpec(right.shape, lambda i: (0, 0))]
    return pl.pallas_call(
        over_rows_kernel,
        grid=(width // tile,),
        in_specs=specs,
        out_specs=pl.BlockSpec((tile, cols), lambda i: (i, 0)),
        out_shape=jax.ShapeDtypeStruct((width, cols), BF),
        compiler_params=pltpu.CompilerParams(vmem_limit_bytes=56 * 2**20),
        cost_estimate=LITTLE,
        name="weight_grad",
    )(*(v for pair in pairs for v in pair))


def project_kernel(count, *refs):
    pieces, w = refs[:count], refs[count]
    all_rows, out, held, in_sem, out_sem = refs[-5:]
    step = pl.program_id(0)
    starts = [sum(p.shape[0] for p in pieces[:i]) for i in range(count)]
    rows = out.shape[0]

    def bring(i):
        return pltpu.make_async_copy(pieces[i], held.at[pl.ds(starts[i], pieces[i].shape[0])], in_sem.at[i])

    def put(i):
        at = pl.ds(starts[i], pieces[i].shape[0])
        return pltpu.make_async_copy(held.at[at], all_rows.at[at], out_sem.at[i])

    @pl.when(step == 0)
    def _():
        for i in range(count):
            bring(i).start()

    for k in range(held.shape[0] // rows):

        @pl.when(step == k)
        def _(k=k):
            for i in range(count):
                if k * rows <= starts[i] < (k + 1) * rows:
                    bring(i).wait()
                    put(i).start()

    here = held[pl.ds(pl.multiple_of(step * rows, rows), rows), :]
    out[...] = dot(here, w[...]).astype(out.dtype)

    @pl.when(step == held.shape[0] // rows - 1)
    def _():
        for i in range(count):
            put(i).wait()


def project(pieces, rows, w, kind):
    total, width = sum(p.shape[0] for p in pieces), pieces[0].shape[1]
    cols = w.shape[1]
    return pl.pallas_call(
        functools.partial(project_kernel, len(pieces)),
        grid=(total // rows,),
        in_specs=[pl.BlockSpec(memory_space=pltpu.HBM)] * len(pieces) + [pl.BlockSpec(w.shape, lambda i: (0, 0))],
        out_specs=[pl.BlockSpec(memory_space=pltpu.HBM), pl.BlockSpec((rows, cols), lambda i: (i, 0))],
        out_shape=[jax.ShapeDtypeStruct((total, width), BF), jax.ShapeDtypeStruct((total, cols), kind)],
        scratch_shapes=[
            pltpu.VMEM((total, width), BF),
            pltpu.SemaphoreType.DMA((len(pieces),)),
            pltpu.SemaphoreType.DMA((len(pieces),)),
        ],
        compiler_params=pltpu.CompilerParams(vmem_limit_bytes=56 * 2**20),
        cost_estimate=LITTLE,
        name="project",
    )(*pieces, w)


FAR, NEAR = (7, 6), (1, 3, 5, 0, 2, 4)


def assemble_kernel(count, *refs):
    pieces, out, held, in_sem, out_sem = refs[:count], refs[count], *refs[count + 1 :]
    ins, outs, start = [], [], 0
    for i, piece in enumerate(pieces):
        at = pl.ds(start, piece.shape[0])
        ins.append(pltpu.make_async_copy(piece, held.at[at], in_sem.at[i]))
        outs.append(pltpu.make_async_copy(held.at[at], out.at[at], out_sem.at[i]))
        start += piece.shape[0]
    for copy in ins:
        copy.start()
    for one, two in zip(ins, outs):
        one.wait()
        two.start()
    for copy in outs:
        copy.wait()


def assemble(*pieces):
    rows, width = sum(p.shape[0] for p in pieces), pieces[0].shape[1]
    return pl.pallas_call(
        functools.partial(assemble_kernel, len(pieces)),
        in_specs=[pl.BlockSpec(memory_space=pl.ANY)] * len(pieces),
        out_specs=pl.BlockSpec(memory_space=pltpu.HBM),
        out_shape=jax.ShapeDtypeStruct((rows, width), pieces[0].dtype),
        scratch_shapes=[
            pltpu.VMEM((rows, width), pieces[0].dtype),
            pltpu.SemaphoreType.DMA((len(pieces),)),
            pltpu.SemaphoreType.DMA((len(pieces),)),
        ],
        compiler_params=pltpu.CompilerParams(vmem_limit_bytes=56 * 2**20),
        cost_estimate=LITTLE,
        name="assemble",
    )(*pieces)


def norm_kernel(count, *refs):
    terms, (base, gain, shift) = refs[:count], refs[count : count + 3]
    total, unit, inverse, low = refs[-4:]
    v = base[...].astype(F32)
    for t in terms:
        v = v + t[...].astype(F32)
    centered = v - jnp.mean(v, -1, keepdims=True)
    scale = lax.rsqrt(jnp.mean(centered * centered, -1, keepdims=True) + EPS)
    normed = centered * scale
    total[...] = v
    unit[...] = normed
    inverse[...] = jnp.broadcast_to(scale, inverse.shape)
    low[...] = (normed * gain[...] + shift[...]).astype(BF)


def in_rows(rows, cols):
    return pl.BlockSpec((rows, cols), lambda i: (i, 0))


def fixed(*dims):
    return pl.BlockSpec(dims, lambda i: (0,) * len(dims))


def norm(base, terms, gain, shift, step=64):
    rows, width = base.shape
    return pl.pallas_call(
        functools.partial(norm_kernel, len(terms)),
        grid=(rows // step,),
        in_specs=[in_rows(step, width)] * (len(terms) + 1) + [fixed(1, width)] * 2,
        out_specs=[in_rows(step, width), in_rows(step, width), in_rows(step, 128), in_rows(step, width)],
        out_shape=[
            jax.ShapeDtypeStruct((rows, width), F32),
            jax.ShapeDtypeStruct((rows, width), F32),
            jax.ShapeDtypeStruct((rows, 128), F32),
            jax.ShapeDtypeStruct((rows, width), BF),
        ],
        compiler_params=pltpu.CompilerParams(vmem_limit_bytes=56 * 2**20),
        cost_estimate=LITTLE,
        name="norm",
    )(*terms, base, gain[None], shift[None])


def norm_back_kernel(count, *refs):
    terms, (base, unit, inverse, gain) = refs[:count], refs[count : count + 4]
    total, sums, low = refs[-3:]
    upstream = terms[0][...].astype(F32)
    for t in terms[1:]:
        upstream = upstream + t[...].astype(F32)
    normed = unit[...]
    scaled = upstream * gain[...]
    product = upstream * normed
    adjusted = (
        scaled
        - jnp.mean(scaled, -1, keepdims=True)
        - normed * jnp.mean(product * gain[...], -1, keepdims=True)
    )
    v = base[...].astype(F32) + inverse[:, :1] * adjusted
    total[...] = v
    low[...] = v.astype(BF)
    here = jnp.concatenate([jnp.sum(product, 0, keepdims=True), jnp.sum(upstream, 0, keepdims=True)], 0)

    @pl.when(pl.program_id(0) == 0)
    def _():
        sums[...] = here

    @pl.when(pl.program_id(0) > 0)
    def _():
        sums[...] += here


def norm_back(base, terms, unit, inverse, gain, step=64):
    rows, width = base.shape
    return pl.pallas_call(
        functools.partial(norm_back_kernel, len(terms)),
        grid=(rows // step,),
        in_specs=[in_rows(step, width)] * (len(terms) + 2) + [in_rows(step, 128), fixed(1, width)],
        out_specs=[in_rows(step, width), fixed(2, width), in_rows(step, width)],
        out_shape=[
            jax.ShapeDtypeStruct((rows, width), F32),
            jax.ShapeDtypeStruct((2, width), F32),
            jax.ShapeDtypeStruct((rows, width), BF),
        ],
        compiler_params=pltpu.CompilerParams(vmem_limit_bytes=56 * 2**20),
        cost_estimate=LITTLE,
        name="norm_back",
    )(*terms, base, unit, inverse, gain[None])


class Place:
    def __init__(self, n_dp, n_tensor):
        self.n_dp, self.n_tensor = n_dp, n_tensor
        self.n_line = n_dp // 2
        dp, tensor = lax.axis_index("dp"), lax.axis_index("tensor")
        self.dp, self.tensor = dp, tensor
        self.line, self.pair = dp // 2, dp % 2

    def to_pair(self, v):
        return lax.ppermute(v, "dp", [(i, i ^ 1) for i in range(self.n_dp)])

    def to_side(self, v):
        return lax.ppermute(v, "tensor", [(i, i ^ 2) for i in range(self.n_tensor)])

    def to_core(self, v):
        return lax.ppermute(v, "tensor", [(i, i ^ 1) for i in range(self.n_tensor)])

    def by_pair(self, first, second, axis):
        return jnp.where(
            self.pair == 0,
            jnp.concatenate([first, second], axis),
            jnp.concatenate([second, first], axis),
        )

    def halves(self, v, axis):
        half = v.shape[axis] // 2
        low = lax.slice_in_dim(v, 0, half, axis=axis)
        high = lax.slice_in_dim(v, half, 2 * half, axis=axis)
        return jnp.where(self.pair == 0, low, high), jnp.where(self.pair == 0, high, low)

    def line_groups(self):
        return [[2 * i + p for i in range(self.n_line)] for p in (0, 1)]

    def widen(self, *weights):
        mine, theirs = zip(*[self.halves(w, 1) for w in weights])
        mine, theirs = jnp.concatenate(mine, 1), jnp.concatenate(theirs, 1)
        return mine, self.to_pair(theirs), theirs

    def gather_weight(self, mine, other):
        return self.gather_piece(self.by_pair(mine, other, 0))

    def gather_piece(self, piece):
        return lax.all_gather(piece, "dp", axis=0, tiled=True, axis_index_groups=self.line_groups())

    def scatter_grad(self, grad):
        return lax.psum_scatter(
            grad,
            "dp",
            scatter_dimension=0,
            tiled=True,
            axis_index_groups=self.line_groups(),
        )

    def share_send(self, total):
        mine, theirs = self.halves(total, 0)
        return mine, self.to_pair(theirs)

    def share_grad(self, mine, other, parts):
        cols = mine.shape[1] // parts
        shares = []
        for i in range(parts):
            at = slice(i * cols, (i + 1) * cols)
            shares.append(self.by_pair(mine[:, at], other[:, at], 1).astype(F32))
        return shares

    def gather_links(self, own):
        return own, self.to_side(own), self.to_pair(own)

    def gather_cores(self, own, side, pair):
        return own, self.to_core(own), side, self.to_core(side), pair, self.to_core(pair)

    def gather_begin(self, own):
        return self.gather_cores(*self.gather_links(own))

    def gather_end(self, near):
        side, pair = near[2], near[4]
        half = side.shape[0] // 2
        one, two = lax.optimization_barrier((side[:half], pair[half:]))
        d1, d2 = self.to_pair(one), self.to_side(two)
        return (d1, d2, self.to_core(d1), self.to_core(d2)), one, two

    def core_sum(self, far, far_sent):
        half = far.shape[0] // 2
        other = self.to_core(far_sent)
        return tuple(
            (far[i].astype(F32) + other[i].astype(F32)).astype(BF)
            for i in (slice(0, half), slice(half, 2 * half))
        )

    def core_sums(self, near, near_sent):
        other = self.to_core(near_sent)
        own, side, pair = (near[k].astype(F32) + other[k].astype(F32) for k in range(3))
        return side, pair, own

    def scatter_begin(self, far, far_sent, near, near_sent):
        return (*self.core_sum(far, far_sent), *self.core_sums(near, near_sent))

    def scatter_begin_once(self, far, far_sent, near, near_sent):
        half = far.shape[0] // 2
        other = self.to_core(jnp.concatenate([far_sent[None], near_sent], 0))
        f1, f2 = (
            (far[i].astype(F32) + other[0, i].astype(F32)).astype(BF)
            for i in (slice(0, half), slice(half, 2 * half))
        )
        own, side, pair = (near[k].astype(F32) + other[k + 1].astype(F32) for k in range(3))
        return f1, f2, side, pair, own

    def scatter_far(self, f1, f2):
        return self.to_pair(f1), self.to_side(f2)

    def scatter_add(self, d1, d2, side, pair, own):
        none = jnp.zeros_like(d1)
        side = (side + jnp.concatenate([d1, none], 0).astype(F32)).astype(BF)
        pair = (pair + jnp.concatenate([none, d2], 0).astype(F32)).astype(BF)
        return side, pair, own

    def scatter_middle(self, begun, *hold):
        f1, f2, side, pair, own = begun
        d1, d2 = self.scatter_far(f1, f2)
        if hold:
            d1, d2, side, pair = all_after((d1, d2, side, pair), *hold)
        return self.scatter_add(d1, d2, side, pair, own)

    def scatter_end(self, middle):
        side, pair, own = middle
        return own, self.to_side(side), self.to_pair(pair)

    def scatter_rows(self, *parts):
        return self.scatter_end(self.scatter_middle(self.scatter_begin(*parts)))

    def sum_all(self, v):
        for axis, size in (("tensor", self.n_tensor), ("dp", self.n_dp)):
            step = 1
            while step < size:
                others = [
                    lax.ppermute(v, axis, [(i, i ^ (k * step)) for i in range(size)])
                    for k in range(1, 4 if 4 * step <= size else 2)
                ]
                v = v + others[0]
                if len(others) == 3:
                    v = v + (others[1] + others[2])
                step *= 1 + len(others)
        return v


def local(
    n_dp,
    n_tensor,
    block_input,
    cotangent,
    ln1_gain,
    ln1_bias,
    w_query,
    q_bias,
    w_key,
    k_bias,
    w_value,
    v_bias,
    w_out,
    ln2_gain,
    ln2_bias,
    w_gate,
    w_up,
    w_down,
):
    at = Place(n_dp, n_tensor)
    width = block_input.shape[1]
    rows = block_input.shape[0]
    length = rows * n_tensor
    half = rows // 2
    cols = w_query.shape[1] // 2
    heads = cols // HEAD
    ff = w_gate.shape[1] // 2

    def in_halves(v):
        return v[:half], v[half:]

    first_mine, first_other, first_sent = at.widen(w_query, w_key, w_value, w_out)
    _, unit_one, inverse_one, act = norm(after(block_input, first_sent), (), ln1_gain, ln1_bias)
    first_piece = at.by_pair(*all_after((first_mine, first_other), act), 0)
    full_qkv = at.gather_piece(first_piece[:, : 3 * cols])
    full_out = at.gather_piece(first_piece[:, 3 * cols :])
    near = at.gather_begin(act)
    far, *halves = at.gather_end(near)
    rest_mine, rest_other, _ = at.widen(*all_after((w_gate, w_up, w_down), *halves))
    tokens = 8 * rows
    cut = 6 * rows

    slots = after(jnp.arange(n_tensor), act)
    place = ((at.tensor ^ slots)[:, None] * rows + jnp.arange(rows)[None, :]).reshape(length)
    cosine, sine = (v.reshape(n_tensor, rows, 128) for v in turn_tables(place))
    me = at.tensor.astype(jnp.int32).reshape(1)

    column = at.tensor * 2 * cols + at.pair * cols
    query_shift = lax.dynamic_slice_in_dim(q_bias, column, cols)
    value_shift = lax.dynamic_slice_in_dim(v_bias, column, cols)
    key_column = at.tensor * 2 * heads * ROT + at.pair * heads * ROT
    key_rows = lax.dynamic_slice_in_dim(k_bias, key_column, heads * ROT)
    key_shift = jnp.pad(key_rows.reshape(heads, ROT), ((0, 0), (0, HEAD - ROT))).reshape(cols)
    shift = jnp.concatenate([query_shift, key_shift, value_shift])[None]

    far = all_after(far, cosine, sine, shift)
    act_one, pre = project([*near, *far], rows, full_qkv, F32)
    pre = pre.reshape(2, n_tensor, rows, 3 * cols)
    rest_late = after(rest_other, pre)
    wide_piece = at.by_pair(rest_mine[:, : 2 * ff], rest_late[:, : 2 * ff], 0)
    down_piece = at.by_pair(rest_mine[:, 2 * ff :], rest_late[:, 2 * ff :], 0)
    full_wide = at.gather_piece(wide_piece)
    qkv, context, log_total = attend(me, after(pre, wide_piece, down_piece), shift, cosine, sine)
    context_all = context.reshape(tokens, cols)

    def product(left, right):
        far = times_transposed(left[cut:], right).astype(BF)
        far, far_sent = lax.optimization_barrier((far[:rows], far[rows:]))
        near = times_transposed(after(left[:cut], far_sent), right).astype(BF)
        near = near.reshape(3, 2, rows, width)
        return far, far_sent, near[:, 0], near[:, 1]

    mixed = at.scatter_rows(*product(context_all, full_out))
    hidden, unit_two, inverse_two, act = norm(block_input, mixed, ln2_gain, ln2_bias)
    full_down = at.gather_piece(after(down_piece, act))
    near = at.gather_begin(act)
    far, *_ = at.gather_end(near)
    fed_near = feed(near, rows, full_wide, total=tokens)
    cot_links = at.gather_links(after(cotangent, *far))
    act_two, inner, slope, swish = feed(far, rows, full_wide, fed_near, tokens)
    cot_near = at.gather_cores(*all_after(cot_links, fed_near[1]))
    cot_far, *_ = at.gather_end(cot_near)
    cot_all = assemble(*all_after((*cot_near, *cot_far), inner))
    down_grad = weight_grad((cot_all, inner))
    down_total = at.scatter_grad(down_grad)
    d_wide, far_sent, far_kept = feed_back(
        after(cot_all, down_grad), full_down, full_wide, slope, swish, FAR, rows
    )
    far_sum = at.core_sum(far_kept[0], far_sent[0])
    d_wide, near_sent, near_kept = feed_back(
        after(cot_all, *far_sum), full_down, full_wide, slope, swish, NEAR, rows, d_wide
    )
    d1, d2, near_kept, near_sent, d_wide = lax.optimization_barrier(
        (*at.scatter_far(*far_sum), near_kept, near_sent, d_wide)
    )
    middle = at.scatter_add(d1, d2, *at.core_sums(near_kept, near_sent))
    wide_grad = weight_grad((act_two, after(d_wide, *middle)))
    d_act_two = at.scatter_end(middle)
    *d_act_two, wide_grad, down_total = lax.optimization_barrier((*d_act_two, wide_grad, down_total))
    wide_total = at.scatter_grad(wide_grad)
    d_hidden, sums_two, low = norm_back(
        cotangent, d_act_two, unit_two, inverse_two, ln2_gain
    )
    links = at.gather_links(low)
    fed_parts = product(after(inner, low), full_down)
    own, side, pair, *fed_parts = lax.optimization_barrier((*links, *fed_parts))
    near = at.gather_cores(own, side, pair)
    far, *_ = at.gather_end(near)
    fed_begun = at.scatter_begin_once(*fed_parts)
    *far, f1, f2 = lax.optimization_barrier((*far, *fed_begun[:2]))
    fed_begun = (f1, f2, *fed_begun[2:])
    d_hidden_all, d_context = project([*near, *far], rows, full_out, BF)
    d_context = d_context.reshape(context.shape)
    fed_middle = at.scatter_middle(fed_begun, d_context)
    down_sent = at.share_send(after(down_total, d_hidden_all))
    fed = at.scatter_end(fed_middle)
    d_qkv, sums = attend_back(me, qkv, context, after(d_context, *fed_middle), log_total, cosine, sine)
    d_qkv, *fed = lax.optimization_barrier((d_qkv, *fed, *down_sent))
    *fed, down_mine, down_other = fed
    d_qkv = d_qkv.reshape(tokens, 3 * cols)
    sums = sums[0, 0] + sums[1, 0]
    qkvo_grad = weight_grad((act_one, d_qkv), (d_hidden_all, context_all))
    qkvo_total = at.scatter_grad(qkvo_grad)
    d_qkv, wide_total = all_after((d_qkv, wide_total), qkvo_grad)
    begun = at.scatter_begin(*product(d_qkv, full_qkv))
    *begun, wide_mine, wide_other = lax.optimization_barrier((*begun, *at.share_send(wide_total)))
    middle = at.scatter_middle(begun)
    block_output = (hidden + fed[0] + fed[1].astype(F32) + fed[2].astype(F32)).astype(BF)
    d_act_one = at.scatter_end(middle)
    (down_share,) = at.share_grad(*all_after((down_mine, down_other), *middle), 1)
    gate_share, up_share = at.share_grad(*all_after((wide_mine, wide_other), *middle), 2)
    input_grad, sums_one, _ = norm_back(d_hidden, d_act_one, unit_one, inverse_one, ln1_gain)
    query_share, key_share, value_share, out_share = at.share_grad(
        *at.share_send(after(qkvo_total, sums_one)), 4
    )

    query_part, value_part = sums[:cols], sums[2 * cols :]
    key_part = sums[cols : 2 * cols].reshape(heads, HEAD)[:, :ROT].reshape(heads * ROT)
    query_full = lax.dynamic_update_slice(jnp.zeros(q_bias.shape, F32), query_part, (column,))
    value_full = lax.dynamic_update_slice(jnp.zeros(v_bias.shape, F32), value_part, (column,))
    key_full = lax.dynamic_update_slice(jnp.zeros(k_bias.shape, F32), key_part, (key_column,))
    sums = at.sum_all(
        jnp.concatenate([sums_one[0], sums_one[1], sums_two[0], sums_two[1], query_full, value_full, key_full])
    )
    n = width
    return (
        block_output,
        input_grad,
        sums[:n],
        sums[n : 2 * n],
        query_share,
        sums[4 * n : 5 * n],
        key_share,
        sums[6 * n :],
        value_share,
        sums[5 * n : 6 * n],
        out_share,
        sums[2 * n : 3 * n],
        sums[3 * n : 4 * n],
        gate_share,
        up_share,
        down_share,
    )


def solution(mesh):
    rows = P(("dp", "tensor"), None)
    matrix = P("dp", "tensor")
    return jax.shard_map(
        functools.partial(local, mesh.shape["dp"], mesh.shape["tensor"]),
        mesh=mesh,
        in_specs=(
            rows, rows, P(), P(), matrix, P(), matrix, P(), matrix, P(), matrix, P(), P(),
            matrix, matrix, matrix,
        ),
        out_specs=(
            rows, rows, P(), P(), matrix, P(), matrix, P(), matrix, P(), matrix, P(), P(),
            matrix, matrix, matrix,
        ),
        check_vma=False,
    )
```

```python
import functools

import jax
import jax.numpy as jnp
from jax import lax
from jax.experimental import pallas as pl
from jax.experimental.pallas import tpu as pltpu
from jax.sharding import PartitionSpec as P

HEAD = 64
ROT = 16
EPS = 1e-05
LITTLE = pl.CostEstimate(flops=0, bytes_accessed=0, transcendentals=0)
BF = jnp.bfloat16
F32 = jnp.float32


def dot(left, right):
    return jnp.dot(left, right, preferred_element_type=F32)


def times_transposed(left, right):
    return lax.dot_general(left, right, (((1,), (1,)), ((), ())), preferred_element_type=F32)


def over_rows(left, right):
    return lax.dot_general(left, right, (((0,), (0,)), ((), ())), preferred_element_type=F32)


def dot_nt(left, right):
    return times_transposed(left, right)


def after(value, *others):
    return lax.optimization_barrier((value, *others))[0]


def all_after(values, *others):
    return lax.optimization_barrier((*values, *others))[: len(values)]


def head_mask(shape, head):
    lane = lax.broadcasted_iota(jnp.int32, shape, len(shape) - 1)
    return (lane >= head * HEAD) & (lane < (head + 1) * HEAD)


def turn(values, cosine, sine):
    half = ROT // 2
    parts = []
    for start in range(0, values.shape[1], 128):
        v = values[:, start : start + 128]
        lane = lax.broadcasted_iota(jnp.int32, v.shape, 1) % HEAD
        other = jnp.where(lane < half, pltpu.roll(v, 128 - half, 1), pltpu.roll(v, half, 1))
        parts.append(v * cosine + other * sine)
    return jnp.concatenate(parts, 1)


def turn_tables(place):
    half = ROT // 2
    frequency = 10000.0 ** (-2.0 * jnp.arange(half, dtype=F32) / ROT)
    angles = place.astype(F32)[:, None] * frequency[None, :]
    cosine, sine = jnp.cos(angles), jnp.sin(angles)
    rest = jnp.ones((place.shape[0], HEAD - ROT), F32)
    one = jnp.concatenate([cosine, cosine, rest], 1)
    two = jnp.concatenate([-sine, sine, 0.0 * rest], 1)
    return jnp.concatenate([one, one], 1), jnp.concatenate([two, two], 1)


def attend_kernel(me, pre, shift, cosine, sine, qkv, context, log_total):
    slots, rows, wide = pre.shape[1:]
    cols = wide // 3
    heads = cols // HEAD
    for s in range(slots):
        for part in range(3):
            at = slice(part * cols, (part + 1) * cols)
            v = pre[0, s, :, at] + shift[:, at]
            if part < 2:
                v = turn(v, cosine[s], sine[s])
            qkv[0, s, :, at] = v.astype(BF)
    where = [jnp.bitwise_xor(me[0], b) for b in range(slots)]
    key_row = lax.broadcasted_iota(jnp.int32, (rows, rows), 1)
    query_row = lax.broadcasted_iota(jnp.int32, (rows, rows), 0)
    lane = lax.broadcasted_iota(jnp.int32, (rows, 128), 1)
    for i in range(slots):
        query = qkv[0, where[i], :, :cols] * jnp.asarray(0.125, BF)
        total_context = jnp.zeros((rows, cols), F32)
        logs = jnp.zeros((rows, 128), F32)
        for h in range(heads):
            mask = head_mask((rows, cols), h)
            one = jnp.where(mask, query, jnp.zeros_like(query))
            scores = [dot_nt(one, qkv[0, where[j], :, cols : 2 * cols]) for j in range(i + 1)]
            scores[i] = jnp.where(key_row <= query_row, scores[i], -1e30)
            top = jnp.max(functools.reduce(jnp.maximum, scores), 1, keepdims=True)
            weights = [jnp.exp(v - top) for v in scores]
            total = jnp.sum(functools.reduce(jnp.add, weights), 1, keepdims=True)
            mixed = functools.reduce(
                jnp.add,
                [dot(w.astype(BF), qkv[0, where[j], :, 2 * cols :]) for j, w in enumerate(weights)],
            )
            total_context = jnp.where(mask, mixed * (1.0 / total), total_context)
            logs = jnp.where(lane == h, top + jnp.log(total), logs)
        context[0, where[i]] = total_context.astype(BF)
        log_total[0, i] = logs.T[:8]


def attend(me, pre, shift, cosine, sine):
    two, slots, rows, wide = pre.shape
    cols = wide // 3

    def seq(*dims):
        return pl.BlockSpec((1, *dims), lambda i, me: (i,) + (0,) * len(dims))

    def whole(*dims):
        return pl.BlockSpec(dims, lambda i, me: (0,) * len(dims))

    pairs = two * slots * (slots + 1) // 2 * (cols // HEAD)
    return pl.pallas_call(
        attend_kernel,
        grid_spec=pltpu.PrefetchScalarGridSpec(
            num_scalar_prefetch=1,
            grid=(two,),
            in_specs=[seq(slots, rows, wide), whole(1, wide), whole(slots, rows, 128), whole(slots, rows, 128)],
            out_specs=[seq(slots, rows, wide), seq(slots, rows, cols), seq(slots, 8, rows)],
        ),
        out_shape=[
            jax.ShapeDtypeStruct((two, slots, rows, wide), BF),
            jax.ShapeDtypeStruct((two, slots, rows, cols), BF),
            jax.ShapeDtypeStruct((two, slots, 8, rows), F32),
        ],
        compiler_params=pltpu.CompilerParams(vmem_limit_bytes=40 * 2**20),
        cost_estimate=LITTLE,
        name="attend",
    )(me, pre, shift, cosine, sine)


def attend_back_kernel(
    me, qkv, context, d_context, log_total, cosine, sine, d_qkv, sums, query, upstream, d_query, delta
):
    slots, rows, wide = qkv.shape[1:]
    cols = wide // 3
    heads = cols // HEAD
    where = [jnp.bitwise_xor(me[0], b) for b in range(slots)]
    row = lax.broadcasted_iota(jnp.int32, (8, cols), 0)
    picks = jnp.zeros((8, cols), F32)
    for h in range(heads):
        picks = jnp.where((row == h) & head_mask((8, cols), h), 1.0, picks)
    picks = picks.astype(BF)
    for i in range(slots):
        at = slice(i * rows, (i + 1) * rows)
        query[at] = qkv[0, where[i], :, :cols] * jnp.asarray(0.125, BF)
        up = d_context[0, where[i]]
        upstream[at] = up
        product = up.astype(F32) * context[0, where[i]].astype(F32)
        high = product.astype(BF)
        low = (product - high.astype(F32)).astype(BF)
        delta[:, at] = dot_nt(picks, high) + dot_nt(picks, low)
    key_row = lax.broadcasted_iota(jnp.int32, (rows, rows), 0)
    query_row = lax.broadcasted_iota(jnp.int32, (rows, rows), 1)
    total_sums = [jnp.zeros((1, cols), F32) for _ in range(3)]
    for j in range(slots):
        key = qkv[0, where[j], :, cols : 2 * cols]
        value = qkv[0, where[j], :, 2 * cols :]
        d_key = jnp.zeros((rows, cols), F32)
        d_value = jnp.zeros((rows, cols), F32)
        for h in range(heads):
            mask = head_mask((rows, cols), h)
            key_one = jnp.where(mask, key, jnp.zeros_like(key))
            value_one = jnp.where(mask, value, jnp.zeros_like(value))
            for i in range(j, slots):
                at = slice(i * rows, (i + 1) * rows)
                query_here, up_here = query[at], upstream[at]
                scores = dot_nt(key_one, query_here)
                if i == j:
                    scores = jnp.where(key_row <= query_row, scores, -1e30)
                probs = jnp.exp(scores - log_total[0, i, h : h + 1, :])
                d_probs = dot_nt(value_one, up_here)
                d_scores = (probs * (d_probs - delta[h : h + 1, at])).astype(BF)
                d_value = jnp.where(mask, d_value + dot(probs.astype(BF), up_here), d_value)
                d_key = jnp.where(mask, d_key + dot(d_scores, query_here), d_key)
                d_query_part = over_rows(d_scores, key_one)
                if j == 0 and h == 0:
                    d_query[at] = d_query_part
                else:
                    d_query[at] += d_query_part
        s = where[j]
        d_key_low = turn(d_key, cosine[s], -sine[s]).astype(BF)
        d_value_low = d_value.astype(BF)
        d_qkv[0, s, :, cols : 2 * cols] = d_key_low
        d_qkv[0, s, :, 2 * cols :] = d_value_low
        d_query_low = turn(d_query[j * rows : (j + 1) * rows] * 0.125, cosine[s], -sine[s]).astype(BF)
        d_qkv[0, s, :, :cols] = d_query_low
        for part, v in enumerate((d_query_low, d_key_low, d_value_low)):
            total_sums[part] += jnp.sum(v.astype(F32), 0, keepdims=True)
    sums[0] = jnp.concatenate(total_sums, 1)


def attend_back(me, qkv, context, d_context, log_total, cosine, sine):
    two, slots, rows, wide = qkv.shape
    cols = wide // 3

    def seq(*dims):
        return pl.BlockSpec((1, *dims), lambda i, me: (i,) + (0,) * len(dims))

    def whole(*dims):
        return pl.BlockSpec(dims, lambda i, me: (0,) * len(dims))

    return pl.pallas_call(
        attend_back_kernel,
        grid_spec=pltpu.PrefetchScalarGridSpec(
            num_scalar_prefetch=1,
            grid=(two,),
            in_specs=[
                seq(slots, rows, wide),
                seq(slots, rows, cols),
                seq(slots, rows, cols),
                seq(slots, 8, rows),
                whole(slots, rows, 128),
                whole(slots, rows, 128),
            ],
            out_specs=[seq(slots, rows, wide), seq(1, wide)],
            scratch_shapes=[
                pltpu.VMEM((slots * rows, cols), BF),
                pltpu.VMEM((slots * rows, cols), BF),
                pltpu.VMEM((slots * rows, cols), F32),
                pltpu.VMEM((8, slots * rows), F32),
            ],
        ),
        out_shape=[
            jax.ShapeDtypeStruct((two, slots, rows, wide), BF),
            jax.ShapeDtypeStruct((two, 1, wide), F32),
        ],
        compiler_params=pltpu.CompilerParams(vmem_limit_bytes=56 * 2**20),
        cost_estimate=LITTLE,
        name="attend_back",
    )(me, qkv, context, d_context, log_total, cosine, sine)


def feed_kernel(count, first, *refs):
    pieces, w = refs[:count], refs[count]
    act, inner, slope, swish, held, in_sem, out_sem = refs[-7:]
    step = pl.program_id(0)
    height = pieces[0].shape[0]
    rows, ff = inner.shape
    each = rows // height

    def bring(i):
        return pltpu.make_async_copy(pieces[i], held.at[pl.ds(i * height, height)], in_sem.at[i])

    def put(i):
        return pltpu.make_async_copy(
            held.at[pl.ds(i * height, height)], act.at[pl.ds(first + i * height, height)], out_sem.at[i]
        )

    @pl.when(step == 0)
    def _():
        for i in range(count):
            bring(i).start()

    for k in range(count // each):

        @pl.when(step == k)
        def _(k=k):
            for i in range(k * each, (k + 1) * each):
                bring(i).wait()
                put(i).start()

    here = held[pl.ds(pl.multiple_of(step * rows, rows), rows), :]
    wide = dot(here, w[...])
    gate, upward = wide[:, :ff], wide[:, ff:]
    sigmoid = 1.0 / (1.0 + jnp.exp(-gate))
    product = gate * sigmoid
    inner[...] = (product * upward).astype(BF)
    swish[...] = product.astype(BF)
    slope[...] = (upward * sigmoid * (1.0 + gate * (1.0 - sigmoid))).astype(BF)

    @pl.when(step == count // each - 1)
    def _():
        for i in range(count):
            put(i).wait()


def feed(pieces, rows, w, earlier=None, total=None):
    count = len(pieces)
    height, width = pieces[0].shape
    ff = w.shape[1] // 2
    all_rows = count * height
    first = 0 if earlier is None else total - all_rows
    kept = () if earlier is None else earlier
    block = pl.BlockSpec((rows, ff), lambda i: (i + first // rows, 0))
    return pl.pallas_call(
        functools.partial(feed_kernel, count, first),
        grid=(all_rows // rows,),
        in_specs=[pl.BlockSpec(memory_space=pltpu.HBM)] * count
        + [pl.BlockSpec(w.shape, lambda i: (0, 0))]
        + [pl.BlockSpec(memory_space=pltpu.HBM)] * len(kept),
        out_specs=[pl.BlockSpec(memory_space=pltpu.HBM), block, block, block],
        out_shape=[jax.ShapeDtypeStruct((total, width), BF)] + [jax.ShapeDtypeStruct((total, ff), BF)] * 3,
        scratch_shapes=[
            pltpu.VMEM((all_rows, width), BF),
            pltpu.SemaphoreType.DMA((count,)),
            pltpu.SemaphoreType.DMA((count,)),
        ],
        input_output_aliases={count + 1 + i: i for i in range(len(kept))},
        compiler_params=pltpu.CompilerParams(vmem_limit_bytes=56 * 2**20),
        cost_estimate=pl.CostEstimate(
            flops=2 * all_rows * width * 2 * ff, bytes_accessed=2 * w.size, transcendentals=0
        ),
        name="feed",
    )(*pieces, w, *kept)


def feed_back_kernel(sends, *refs):
    cot, down, w, slope, swish = refs[:5]
    d_wide, sent, kept = refs[-3:]
    step = pl.program_id(0)
    d_inner = dot(cot[...], down[...])
    d_gate = (d_inner * slope[...].astype(F32)).astype(BF)
    d_upward = (d_inner * swish[...].astype(F32)).astype(BF)
    both = jnp.concatenate([d_gate, d_upward], 1)
    d_wide[...] = both
    result = dot_nt(both, w[...]).astype(BF)

    @pl.when(step < sends)
    def _():
        sent[0] = result

    @pl.when(step >= sends)
    def _():
        kept[0] = result


def feed_back(cot, down, w, slope, swish, slots, rows, earlier=None):
    total, width = cot.shape
    ff = down.shape[1]
    sends = len(slots) // 2
    first, stride = slots[0], 2

    def slot(i):
        return jnp.where(i < sends, first + stride * i, first - 1 + stride * (i - sends))

    def whole_of(v):
        return pl.BlockSpec(v.shape, lambda i: (0, 0))

    narrow = pl.BlockSpec((rows, ff), lambda i: (slot(i), 0))
    part = jax.ShapeDtypeStruct((sends, rows, width), BF)
    extra = () if earlier is None else (earlier,)
    return pl.pallas_call(
        functools.partial(feed_back_kernel, sends),
        grid=(2 * sends,),
        in_specs=[
            pl.BlockSpec((rows, width), lambda i: (slot(i), 0)),
            whole_of(down),
            whole_of(w),
            narrow,
            narrow,
        ]
        + [pl.BlockSpec(memory_space=pl.ANY)] * len(extra),
        out_specs=[
            pl.BlockSpec((rows, 2 * ff), lambda i: (slot(i), 0)),
            pl.BlockSpec((1, rows, width), lambda i: (jnp.minimum(i, sends - 1), 0, 0)),
            pl.BlockSpec((1, rows, width), lambda i: (jnp.maximum(i - sends, 0), 0, 0)),
        ],
        out_shape=[jax.ShapeDtypeStruct((total, 2 * ff), BF), part, part],
        input_output_aliases={5: 0} if extra else {},
        compiler_params=pltpu.CompilerParams(vmem_limit_bytes=56 * 2**20),
        cost_estimate=pl.CostEstimate(
            flops=2 * 2 * sends * rows * width * 3 * ff,
            bytes_accessed=2 * (w.size + down.size + 2 * sends * rows * (2 * width + 4 * ff)),
            transcendentals=0,
        ),
        name="feed_back",
    )(cot, down, w, slope, swish, *extra)


def over_rows_kernel(*refs):
    out, start = refs[-1], 0
    for left, right in zip(refs[:-1:2], refs[1:-1:2]):
        stop = start + right.shape[1]
        out[:, start:stop] = over_rows(left[...], right[...]).astype(BF)
        start = stop


def weight_grad(*pairs, tile=512):
    rows, width = pairs[0][0].shape
    cols = sum(right.shape[1] for _, right in pairs)
    specs = []
    for _, right in pairs:
        specs += [pl.BlockSpec((rows, tile), lambda i: (0, i)), pl.BlockSpec(right.shape, lambda i: (0, 0))]
    return pl.pallas_call(
        over_rows_kernel,
        grid=(width // tile,),
        in_specs=specs,
        out_specs=pl.BlockSpec((tile, cols), lambda i: (i, 0)),
        out_shape=jax.ShapeDtypeStruct((width, cols), BF),
        compiler_params=pltpu.CompilerParams(vmem_limit_bytes=56 * 2**20),
        cost_estimate=LITTLE,
        name="weight_grad",
    )(*(v for pair in pairs for v in pair))


def project_kernel(count, *refs):
    pieces, w = refs[:count], refs[count]
    all_rows, out, held, in_sem, out_sem = refs[-5:]
    step = pl.program_id(0)
    starts = [sum(p.shape[0] for p in pieces[:i]) for i in range(count)]
    rows = out.shape[0]

    def bring(i):
        return pltpu.make_async_copy(pieces[i], held.at[pl.ds(starts[i], pieces[i].shape[0])], in_sem.at[i])

    def put(i):
        at = pl.ds(starts[i], pieces[i].shape[0])
        return pltpu.make_async_copy(held.at[at], all_rows.at[at], out_sem.at[i])

    @pl.when(step == 0)
    def _():
        for i in range(count):
            bring(i).start()

    for k in range(held.shape[0] // rows):

        @pl.when(step == k)
        def _(k=k):
            for i in range(count):
                if k * rows <= starts[i] < (k + 1) * rows:
                    bring(i).wait()
                    put(i).start()

    here = held[pl.ds(pl.multiple_of(step * rows, rows), rows), :]
    out[...] = dot(here, w[...]).astype(out.dtype)

    @pl.when(step == held.shape[0] // rows - 1)
    def _():
        for i in range(count):
            put(i).wait()


def project(pieces, rows, w, kind):
    total, width = sum(p.shape[0] for p in pieces), pieces[0].shape[1]
    cols = w.shape[1]
    return pl.pallas_call(
        functools.partial(project_kernel, len(pieces)),
        grid=(total // rows,),
        in_specs=[pl.BlockSpec(memory_space=pltpu.HBM)] * len(pieces) + [pl.BlockSpec(w.shape, lambda i: (0, 0))],
        out_specs=[pl.BlockSpec(memory_space=pltpu.HBM), pl.BlockSpec((rows, cols), lambda i: (i, 0))],
        out_shape=[jax.ShapeDtypeStruct((total, width), BF), jax.ShapeDtypeStruct((total, cols), kind)],
        scratch_shapes=[
            pltpu.VMEM((total, width), BF),
            pltpu.SemaphoreType.DMA((len(pieces),)),
            pltpu.SemaphoreType.DMA((len(pieces),)),
        ],
        compiler_params=pltpu.CompilerParams(vmem_limit_bytes=56 * 2**20),
        cost_estimate=LITTLE,
        name="project",
    )(*pieces, w)


FAR, NEAR = (7, 6), (1, 3, 5, 0, 2, 4)


def assemble_kernel(count, *refs):
    pieces, out, held, in_sem, out_sem = refs[:count], refs[count], *refs[count + 1 :]
    ins, outs, start = [], [], 0
    for i, piece in enumerate(pieces):
        at = pl.ds(start, piece.shape[0])
        ins.append(pltpu.make_async_copy(piece, held.at[at], in_sem.at[i]))
        outs.append(pltpu.make_async_copy(held.at[at], out.at[at], out_sem.at[i]))
        start += piece.shape[0]
    for copy in ins:
        copy.start()
    for one, two in zip(ins, outs):
        one.wait()
        two.start()
    for copy in outs:
        copy.wait()


def assemble(*pieces):
    rows, width = sum(p.shape[0] for p in pieces), pieces[0].shape[1]
    return pl.pallas_call(
        functools.partial(assemble_kernel, len(pieces)),
        in_specs=[pl.BlockSpec(memory_space=pl.ANY)] * len(pieces),
        out_specs=pl.BlockSpec(memory_space=pltpu.HBM),
        out_shape=jax.ShapeDtypeStruct((rows, width), pieces[0].dtype),
        scratch_shapes=[
            pltpu.VMEM((rows, width), pieces[0].dtype),
            pltpu.SemaphoreType.DMA((len(pieces),)),
            pltpu.SemaphoreType.DMA((len(pieces),)),
        ],
        compiler_params=pltpu.CompilerParams(vmem_limit_bytes=56 * 2**20),
        cost_estimate=LITTLE,
        name="assemble",
    )(*pieces)


def core_sums_kernel(near, other, *refs):
    own, side, pair = refs
    for k, out in enumerate((own, side, pair)):
        out[...] = near[k].astype(F32) + other[k].astype(F32)


def core_sums(near, other, step=64):
    three, rows, width = near.shape
    blocks = pl.BlockSpec((three, step, width), lambda i: (0, i, 0))
    return pl.pallas_call(
        core_sums_kernel,
        grid=(rows // step,),
        in_specs=[blocks, blocks],
        out_specs=[pl.BlockSpec((step, width), lambda i: (i, 0))] * 3,
        out_shape=[jax.ShapeDtypeStruct((rows, width), F32)] * 3,
        compiler_params=pltpu.CompilerParams(vmem_limit_bytes=56 * 2**20),
        cost_estimate=LITTLE,
        name="core_sums",
    )(near, other)


def add_halves_kernel(side, pair, d1, d2, side_low, pair_low):
    half = d1.shape[0]
    side_low[:half] = (side[:half] + d1[...].astype(F32)).astype(BF)
    side_low[half:] = side[half:].astype(BF)
    pair_low[:half] = pair[:half].astype(BF)
    pair_low[half:] = (pair[half:] + d2[...].astype(F32)).astype(BF)


def add_halves(side, pair, d1, d2):
    return pl.pallas_call(
        add_halves_kernel,
        out_shape=[jax.ShapeDtypeStruct(side.shape, BF)] * 2,
        compiler_params=pltpu.CompilerParams(vmem_limit_bytes=56 * 2**20),
        cost_estimate=LITTLE,
        name="add_halves",
    )(side, pair, d1, d2)


def norm_kernel(count, *refs):
    terms, (base, gain, shift) = refs[:count], refs[count : count + 3]
    total, unit, inverse, low = refs[-4:]
    v = base[...].astype(F32)
    for t in terms:
        v = v + t[...].astype(F32)
    centered = v - jnp.mean(v, -1, keepdims=True)
    scale = lax.rsqrt(jnp.mean(centered * centered, -1, keepdims=True) + EPS)
    normed = centered * scale
    total[...] = v
    unit[...] = normed
    inverse[...] = jnp.broadcast_to(scale, inverse.shape)
    low[...] = (normed * gain[...] + shift[...]).astype(BF)


def in_rows(rows, cols):
    return pl.BlockSpec((rows, cols), lambda i: (i, 0))


def fixed(*dims):
    return pl.BlockSpec(dims, lambda i: (0,) * len(dims))


def norm(base, terms, gain, shift, step=64):
    rows, width = base.shape
    return pl.pallas_call(
        functools.partial(norm_kernel, len(terms)),
        grid=(rows // step,),
        in_specs=[in_rows(step, width)] * (len(terms) + 1) + [fixed(1, width)] * 2,
        out_specs=[in_rows(step, width), in_rows(step, width), in_rows(step, 128), in_rows(step, width)],
        out_shape=[
            jax.ShapeDtypeStruct((rows, width), F32),
            jax.ShapeDtypeStruct((rows, width), F32),
            jax.ShapeDtypeStruct((rows, 128), F32),
            jax.ShapeDtypeStruct((rows, width), BF),
        ],
        compiler_params=pltpu.CompilerParams(vmem_limit_bytes=56 * 2**20),
        cost_estimate=LITTLE,
        name="norm",
    )(*terms, base, gain[None], shift[None])


def norm_back_kernel(count, *refs):
    terms, (base, unit, inverse, gain) = refs[:count], refs[count : count + 4]
    total, sums, low = refs[-3:]
    upstream = terms[0][...].astype(F32)
    for t in terms[1:]:
        upstream = upstream + t[...].astype(F32)
    normed = unit[...]
    scaled = upstream * gain[...]
    product = upstream * normed
    adjusted = (
        scaled
        - jnp.mean(scaled, -1, keepdims=True)
        - normed * jnp.mean(product * gain[...], -1, keepdims=True)
    )
    v = base[...].astype(F32) + inverse[:, :1] * adjusted
    total[...] = v
    low[...] = v.astype(BF)
    here = jnp.concatenate([jnp.sum(product, 0, keepdims=True), jnp.sum(upstream, 0, keepdims=True)], 0)

    @pl.when(pl.program_id(0) == 0)
    def _():
        sums[...] = here

    @pl.when(pl.program_id(0) > 0)
    def _():
        sums[...] += here


def norm_back(base, terms, unit, inverse, gain, step=64):
    rows, width = base.shape
    return pl.pallas_call(
        functools.partial(norm_back_kernel, len(terms)),
        grid=(rows // step,),
        in_specs=[in_rows(step, width)] * (len(terms) + 2) + [in_rows(step, 128), fixed(1, width)],
        out_specs=[in_rows(step, width), fixed(2, width), in_rows(step, width)],
        out_shape=[
            jax.ShapeDtypeStruct((rows, width), F32),
            jax.ShapeDtypeStruct((2, width), F32),
            jax.ShapeDtypeStruct((rows, width), BF),
        ],
        compiler_params=pltpu.CompilerParams(vmem_limit_bytes=56 * 2**20),
        cost_estimate=LITTLE,
        name="norm_back",
    )(*terms, base, unit, inverse, gain[None])


class Place:
    def __init__(self, n_dp, n_tensor):
        self.n_dp, self.n_tensor = n_dp, n_tensor
        self.n_line = n_dp // 2
        dp, tensor = lax.axis_index("dp"), lax.axis_index("tensor")
        self.dp, self.tensor = dp, tensor
        self.line, self.pair = dp // 2, dp % 2

    def to_pair(self, v):
        return lax.ppermute(v, "dp", [(i, i ^ 1) for i in range(self.n_dp)])

    def to_side(self, v):
        return lax.ppermute(v, "tensor", [(i, i ^ 2) for i in range(self.n_tensor)])

    def to_core(self, v):
        return lax.ppermute(v, "tensor", [(i, i ^ 1) for i in range(self.n_tensor)])

    def by_pair(self, first, second, axis):
        return jnp.where(
            self.pair == 0,
            jnp.concatenate([first, second], axis),
            jnp.concatenate([second, first], axis),
        )

    def halves(self, v, axis):
        half = v.shape[axis] // 2
        low = lax.slice_in_dim(v, 0, half, axis=axis)
        high = lax.slice_in_dim(v, half, 2 * half, axis=axis)
        return jnp.where(self.pair == 0, low, high), jnp.where(self.pair == 0, high, low)

    def line_groups(self):
        return [[2 * i + p for i in range(self.n_line)] for p in (0, 1)]

    def widen(self, *weights):
        mine, theirs = zip(*[self.halves(w, 1) for w in weights])
        mine, theirs = jnp.concatenate(mine, 1), jnp.concatenate(theirs, 1)
        return mine, self.to_pair(theirs), theirs

    def gather_weight(self, mine, other):
        return self.gather_piece(self.by_pair(mine, other, 0))

    def gather_piece(self, piece):
        return lax.all_gather(piece, "dp", axis=0, tiled=True, axis_index_groups=self.line_groups())

    def scatter_grad(self, grad):
        return lax.psum_scatter(
            grad,
            "dp",
            scatter_dimension=0,
            tiled=True,
            axis_index_groups=self.line_groups(),
        )

    def share_send(self, total):
        mine, theirs = self.halves(total, 0)
        return mine, self.to_pair(theirs)

    def share_grad(self, mine, other, parts):
        cols = mine.shape[1] // parts
        shares = []
        for i in range(parts):
            at = slice(i * cols, (i + 1) * cols)
            shares.append(self.by_pair(mine[:, at], other[:, at], 1).astype(F32))
        return shares

    def gather_links(self, own):
        return own, self.to_side(own), self.to_pair(own)

    def gather_cores(self, own, side, pair):
        return own, self.to_core(own), side, self.to_core(side), pair, self.to_core(pair)

    def gather_begin(self, own):
        return self.gather_cores(*self.gather_links(own))

    def gather_far(self, near):
        side, pair = near[2], near[4]
        half = side.shape[0] // 2
        one, two = lax.optimization_barrier((side[:half], pair[half:]))
        return self.to_pair(one), self.to_side(two), one, two

    def gather_end(self, near):
        d1, d2, one, two = self.gather_far(near)
        return (d1, d2, self.to_core(d1), self.to_core(d2)), one, two

    def core_sum(self, far, far_sent):
        half = far.shape[0] // 2
        other = self.to_core(far_sent)
        return tuple(
            (far[i].astype(F32) + other[i].astype(F32)).astype(BF)
            for i in (slice(0, half), slice(half, 2 * half))
        )

    def core_sums(self, near, near_sent):
        other = self.to_core(near_sent)
        own, side, pair = (near[k].astype(F32) + other[k].astype(F32) for k in range(3))
        return side, pair, own

    def scatter_begin(self, far, far_sent, near, near_sent):
        return (*self.core_sum(far, far_sent), *self.core_sums(near, near_sent))

    def scatter_begin_once(self, far, far_sent, near, near_sent):
        half = far.shape[0] // 2
        other = self.to_core(jnp.concatenate([far_sent[None], near_sent], 0))
        f1, f2 = (
            (far[i].astype(F32) + other[0, i].astype(F32)).astype(BF)
            for i in (slice(0, half), slice(half, 2 * half))
        )
        own, side, pair = (near[k].astype(F32) + other[k + 1].astype(F32) for k in range(3))
        return f1, f2, side, pair, own

    def scatter_far(self, f1, f2):
        return self.to_pair(f1), self.to_side(f2)

    def scatter_add(self, d1, d2, side, pair, own):
        none = jnp.zeros_like(d1)
        side = (side + jnp.concatenate([d1, none], 0).astype(F32)).astype(BF)
        pair = (pair + jnp.concatenate([none, d2], 0).astype(F32)).astype(BF)
        return side, pair, own

    def scatter_middle(self, begun, *hold):
        f1, f2, side, pair, own = begun
        d1, d2 = self.scatter_far(f1, f2)
        if hold:
            d1, d2, side, pair = all_after((d1, d2, side, pair), *hold)
        return self.scatter_add(d1, d2, side, pair, own)

    def scatter_end(self, middle):
        side, pair, own = middle
        return own, self.to_side(side), self.to_pair(pair)

    def scatter_rows(self, *parts):
        return self.scatter_end(self.scatter_middle(self.scatter_begin(*parts)))

    def sum_all(self, v):
        for axis, size, first in (("tensor", self.n_tensor, 1), ("dp", self.n_dp, 2), ("dp", 2, 1)):
            length = self.n_tensor if axis == "tensor" else self.n_dp
            step = first
            while step < size:
                others = [
                    lax.ppermute(v, axis, [(i, i ^ (k * step)) for i in range(length)])
                    for k in range(1, 4 if 4 * step <= size else 2)
                ]
                v = v + others[0]
                if len(others) == 3:
                    v = v + (others[1] + others[2])
                step *= 1 + len(others)
        return v


def local(
    n_dp,
    n_tensor,
    block_input,
    cotangent,
    ln1_gain,
    ln1_bias,
    w_query,
    q_bias,
    w_key,
    k_bias,
    w_value,
    v_bias,
    w_out,
    ln2_gain,
    ln2_bias,
    w_gate,
    w_up,
    w_down,
):
    at = Place(n_dp, n_tensor)
    width = block_input.shape[1]
    rows = block_input.shape[0]
    length = rows * n_tensor
    half = rows // 2
    cols = w_query.shape[1] // 2
    heads = cols // HEAD
    ff = w_gate.shape[1] // 2

    def in_halves(v):
        return v[:half], v[half:]

    first_mine, first_other, first_sent = at.widen(w_query, w_key, w_value, w_out)
    _, unit_one, inverse_one, act = norm(after(block_input, first_sent), (), ln1_gain, ln1_bias)
    first_piece = at.by_pair(*all_after((first_mine, first_other), act), 0)
    full_qkv = at.gather_piece(first_piece[:, : 3 * cols])
    full_out = at.gather_piece(first_piece[:, 3 * cols :])
    near = at.gather_begin(act)
    far, *halves = at.gather_end(near)
    rest_mine, rest_other, _ = at.widen(*all_after((w_gate, w_up, w_down), *halves))
    tokens = 8 * rows
    cut = 6 * rows

    slots = after(jnp.arange(n_tensor), act)
    place = ((at.tensor ^ slots)[:, None] * rows + jnp.arange(rows)[None, :]).reshape(length)
    cosine, sine = (v.reshape(n_tensor, rows, 128) for v in turn_tables(place))
    me = at.tensor.astype(jnp.int32).reshape(1)

    column = at.tensor * 2 * cols + at.pair * cols
    query_shift = lax.dynamic_slice_in_dim(q_bias, column, cols)
    value_shift = lax.dynamic_slice_in_dim(v_bias, column, cols)
    key_column = at.tensor * 2 * heads * ROT + at.pair * heads * ROT
    key_rows = lax.dynamic_slice_in_dim(k_bias, key_column, heads * ROT)
    key_shift = jnp.pad(key_rows.reshape(heads, ROT), ((0, 0), (0, HEAD - ROT))).reshape(cols)
    shift = jnp.concatenate([query_shift, key_shift, value_shift])[None]

    far = all_after(far, cosine, sine, shift)
    act_one, pre = project([*near, *far], rows, full_qkv, F32)
    pre = pre.reshape(2, n_tensor, rows, 3 * cols)
    rest_late = after(rest_other, pre)
    wide_piece = at.by_pair(rest_mine[:, : 2 * ff], rest_late[:, : 2 * ff], 0)
    down_piece = at.by_pair(rest_mine[:, 2 * ff :], rest_late[:, 2 * ff :], 0)
    full_wide = at.gather_piece(wide_piece)
    qkv, context, log_total = attend(me, after(pre, wide_piece, down_piece), shift, cosine, sine)
    context_all = context.reshape(tokens, cols)

    def product(left, right):
        far = times_transposed(left[cut:], right).astype(BF)
        far, far_sent = lax.optimization_barrier((far[:rows], far[rows:]))
        near = times_transposed(after(left[:cut], far_sent), right).astype(BF)
        near = near.reshape(3, 2, rows, width)
        return far, far_sent, near[:, 0], near[:, 1]

    mixed = at.scatter_rows(*product(context_all, full_out))
    hidden, unit_two, inverse_two, act = norm(block_input, mixed, ln2_gain, ln2_bias)
    full_down = at.gather_piece(after(down_piece, act))
    near = at.gather_begin(act)
    far, *_ = at.gather_end(near)
    fed_near = feed(near, rows, full_wide, total=tokens)
    cot_links = at.gather_links(after(cotangent, *far))
    cot_near = at.gather_cores(*all_after(cot_links, fed_near[1]))
    d1, d2, *halves = at.gather_far(cot_near)
    far, *_ = lax.optimization_barrier((far, *halves))
    act_two, inner, slope, swish = feed(far, rows, full_wide, fed_near, tokens)
    d1, d2, inner = lax.optimization_barrier((d1, d2, inner))
    cot_all = assemble(*cot_near, d1, d2, at.to_core(d1), at.to_core(d2))
    down_grad = weight_grad((cot_all, inner))
    down_total = at.scatter_grad(down_grad)
    d_wide, far_sent, far_kept = feed_back(
        after(cot_all, down_grad), full_down, full_wide, slope, swish, FAR, rows
    )
    far_sum = at.core_sum(far_kept[0], far_sent[0])
    d_wide, near_sent, near_kept = feed_back(
        after(cot_all, *far_sum), full_down, full_wide, slope, swish, NEAR, rows, d_wide
    )
    d1, d2, near_kept, near_sent, d_wide = lax.optimization_barrier(
        (*at.scatter_far(*far_sum), near_kept, near_sent, d_wide)
    )
    middle = at.scatter_add(d1, d2, *at.core_sums(near_kept, near_sent))
    wide_grad = weight_grad((act_two, after(d_wide, *middle)))
    d_act_two = at.scatter_end(middle)
    *d_act_two, wide_grad, down_total = lax.optimization_barrier((*d_act_two, wide_grad, down_total))
    wide_total = at.scatter_grad(wide_grad)
    d_hidden, sums_two, low = norm_back(
        cotangent, d_act_two, unit_two, inverse_two, ln2_gain
    )
    links = at.gather_links(low)
    fed_parts = product(after(inner, low), full_down)
    own, side, pair, *fed_parts = lax.optimization_barrier((*links, *fed_parts))
    near = at.gather_cores(own, side, pair)
    far, *_ = at.gather_end(near)
    fed_begun = at.scatter_begin_once(*fed_parts)
    *far, f1, f2 = lax.optimization_barrier((*far, *fed_begun[:2]))
    fed_begun = (f1, f2, *fed_begun[2:])
    d_hidden_all, d_context = project([*near, *far], rows, full_out, BF)
    d_context = d_context.reshape(context.shape)
    fed_middle = at.scatter_middle(fed_begun, d_context)
    down_sent = at.share_send(after(down_total, d_hidden_all))
    fed = at.scatter_end(fed_middle)
    d_qkv, sums = attend_back(me, qkv, context, after(d_context, *fed_middle), log_total, cosine, sine)
    d_qkv, *fed = lax.optimization_barrier((d_qkv, *fed, *down_sent))
    *fed, down_mine, down_other = fed
    d_qkv = d_qkv.reshape(tokens, 3 * cols)
    sums = sums[0, 0] + sums[1, 0]
    wide_sent = at.share_send(after(wide_total, d_qkv))
    qkvo_grad = weight_grad((act_one, after(d_qkv, *wide_sent[:1])), (d_hidden_all, context_all))
    qkvo_grad, wide_mine, wide_other = lax.optimization_barrier((qkvo_grad, *wide_sent))
    qkvo_total = at.scatter_grad(qkvo_grad)
    far_kept, far_sent, near_kept, near_sent = product(after(d_qkv, qkvo_grad), full_qkv)
    far_sum = at.core_sum(far_kept, far_sent)
    own, side, pair = core_sums(near_kept, at.to_core(near_sent))
    d1, d2, own, side, pair = lax.optimization_barrier((*at.scatter_far(*far_sum), own, side, pair))
    middle = (*add_halves(side, pair, d1, d2), own)
    block_output = (hidden + fed[0] + fed[1].astype(F32) + fed[2].astype(F32)).astype(BF)
    d_act_one = at.scatter_end(middle)
    (down_share,) = at.share_grad(*all_after((down_mine, down_other), *middle), 1)
    gate_share, up_share = at.share_grad(*all_after((wide_mine, wide_other), *middle), 2)
    *d_act_one, down_share, gate_share, up_share, block_output = lax.optimization_barrier(
        (*d_act_one, down_share, gate_share, up_share, block_output)
    )
    input_grad, sums_one, _ = norm_back(d_hidden, d_act_one, unit_one, inverse_one, ln1_gain)
    qkvo_sent = at.share_send(after(qkvo_total, sums_one))
    query_share, key_share, value_share, out_share = at.share_grad(*qkvo_sent, 4)

    query_part, value_part = sums[:cols], sums[2 * cols :]
    key_part = sums[cols : 2 * cols].reshape(heads, HEAD)[:, :ROT].reshape(heads * ROT)
    query_full = lax.dynamic_update_slice(jnp.zeros(q_bias.shape, F32), query_part, (column,))
    value_full = lax.dynamic_update_slice(jnp.zeros(v_bias.shape, F32), value_part, (column,))
    key_full = lax.dynamic_update_slice(jnp.zeros(k_bias.shape, F32), key_part, (key_column,))
    sums = at.sum_all(
        after(
            jnp.concatenate([sums_one[0], sums_one[1], sums_two[0], sums_two[1], query_full, value_full, key_full]),
            qkvo_sent[0],
        )
    )
    n = width
    return (
        block_output,
        input_grad,
        sums[:n],
        sums[n : 2 * n],
        query_share,
        sums[4 * n : 5 * n],
        key_share,
        sums[6 * n :],
        value_share,
        sums[5 * n : 6 * n],
        out_share,
        sums[2 * n : 3 * n],
        sums[3 * n : 4 * n],
        gate_share,
        up_share,
        down_share,
    )


def solution(mesh):
    rows = P(("dp", "tensor"), None)
    matrix = P("dp", "tensor")
    return jax.shard_map(
        functools.partial(local, mesh.shape["dp"], mesh.shape["tensor"]),
        mesh=mesh,
        in_specs=(
            rows, rows, P(), P(), matrix, P(), matrix, P(), matrix, P(), matrix, P(), P(),
            matrix, matrix, matrix,
        ),
        out_specs=(
            rows, rows, P(), P(), matrix, P(), matrix, P(), matrix, P(), matrix, P(), P(),
            matrix, matrix, matrix,
        ),
        check_vma=False,
    )
```

```python
import functools

import jax
import jax.numpy as jnp
from jax import lax
from jax.experimental import pallas as pl
from jax.experimental.pallas import tpu as pltpu
from jax.sharding import PartitionSpec as P

HEAD = 64
ROT = 16
EPS = 1e-05
LITTLE = pl.CostEstimate(flops=0, bytes_accessed=0, transcendentals=0)
BF = jnp.bfloat16
F32 = jnp.float32


def dot(left, right):
    return jnp.dot(left, right, preferred_element_type=F32)


def times_transposed(left, right):
    return lax.dot_general(left, right, (((1,), (1,)), ((), ())), preferred_element_type=F32)


def over_rows(left, right):
    return lax.dot_general(left, right, (((0,), (0,)), ((), ())), preferred_element_type=F32)


def dot_nt(left, right):
    return times_transposed(left, right)


def after(value, *others):
    return lax.optimization_barrier((value, *others))[0]


def all_after(values, *others):
    return lax.optimization_barrier((*values, *others))[: len(values)]


def head_mask(shape, head):
    lane = lax.broadcasted_iota(jnp.int32, shape, len(shape) - 1)
    return (lane >= head * HEAD) & (lane < (head + 1) * HEAD)


def turn(values, cosine, sine):
    half = ROT // 2
    parts = []
    for start in range(0, values.shape[1], 128):
        v = values[:, start : start + 128]
        lane = lax.broadcasted_iota(jnp.int32, v.shape, 1) % HEAD
        other = jnp.where(lane < half, pltpu.roll(v, 128 - half, 1), pltpu.roll(v, half, 1))
        parts.append(v * cosine + other * sine)
    return jnp.concatenate(parts, 1)


def turn_tables(place):
    half = ROT // 2
    frequency = 10000.0 ** (-2.0 * jnp.arange(half, dtype=F32) / ROT)
    angles = place.astype(F32)[:, None] * frequency[None, :]
    cosine, sine = jnp.cos(angles), jnp.sin(angles)
    rest = jnp.ones((place.shape[0], HEAD - ROT), F32)
    one = jnp.concatenate([cosine, cosine, rest], 1)
    two = jnp.concatenate([-sine, sine, 0.0 * rest], 1)
    return jnp.concatenate([one, one], 1), jnp.concatenate([two, two], 1)


def attend_kernel(me, pre, shift, cosine, sine, qkv, context, log_total):
    slots, rows, wide = pre.shape[1:]
    cols = wide // 3
    heads = cols // HEAD
    for s in range(slots):
        for part in range(3):
            at = slice(part * cols, (part + 1) * cols)
            v = pre[0, s, :, at] + shift[:, at]
            if part < 2:
                v = turn(v, cosine[s], sine[s])
            qkv[0, s, :, at] = v.astype(BF)
    where = [jnp.bitwise_xor(me[0], b) for b in range(slots)]
    key_row = lax.broadcasted_iota(jnp.int32, (rows, rows), 1)
    query_row = lax.broadcasted_iota(jnp.int32, (rows, rows), 0)
    lane = lax.broadcasted_iota(jnp.int32, (rows, 128), 1)
    for i in range(slots):
        query = qkv[0, where[i], :, :cols] * jnp.asarray(0.125, BF)
        total_context = jnp.zeros((rows, cols), F32)
        logs = jnp.zeros((rows, 128), F32)
        for h in range(heads):
            mask = head_mask((rows, cols), h)
            one = jnp.where(mask, query, jnp.zeros_like(query))
            scores = [dot_nt(one, qkv[0, where[j], :, cols : 2 * cols]) for j in range(i + 1)]
            scores[i] = jnp.where(key_row <= query_row, scores[i], -1e30)
            top = jnp.max(functools.reduce(jnp.maximum, scores), 1, keepdims=True)
            weights = [jnp.exp(v - top) for v in scores]
            total = jnp.sum(functools.reduce(jnp.add, weights), 1, keepdims=True)
            mixed = functools.reduce(
                jnp.add,
                [dot(w.astype(BF), qkv[0, where[j], :, 2 * cols :]) for j, w in enumerate(weights)],
            )
            total_context = jnp.where(mask, mixed * (1.0 / total), total_context)
            logs = jnp.where(lane == h, top + jnp.log(total), logs)
        context[0, where[i]] = total_context.astype(BF)
        log_total[0, i] = logs.T[:8]


def attend(me, pre, shift, cosine, sine):
    two, slots, rows, wide = pre.shape
    cols = wide // 3

    def seq(*dims):
        return pl.BlockSpec((1, *dims), lambda i, me: (i,) + (0,) * len(dims))

    def whole(*dims):
        return pl.BlockSpec(dims, lambda i, me: (0,) * len(dims))

    pairs = two * slots * (slots + 1) // 2 * (cols // HEAD)
    return pl.pallas_call(
        attend_kernel,
        grid_spec=pltpu.PrefetchScalarGridSpec(
            num_scalar_prefetch=1,
            grid=(two,),
            in_specs=[seq(slots, rows, wide), whole(1, wide), whole(slots, rows, 128), whole(slots, rows, 128)],
            out_specs=[seq(slots, rows, wide), seq(slots, rows, cols), seq(slots, 8, rows)],
        ),
        out_shape=[
            jax.ShapeDtypeStruct((two, slots, rows, wide), BF),
            jax.ShapeDtypeStruct((two, slots, rows, cols), BF),
            jax.ShapeDtypeStruct((two, slots, 8, rows), F32),
        ],
        compiler_params=pltpu.CompilerParams(vmem_limit_bytes=40 * 2**20),
        cost_estimate=LITTLE,
        name="attend",
    )(me, pre, shift, cosine, sine)


def attend_back_kernel(
    me, qkv, context, d_context, log_total, cosine, sine, d_qkv, sums, query, upstream, d_query, delta
):
    slots, rows, wide = qkv.shape[1:]
    cols = wide // 3
    heads = cols // HEAD
    where = [jnp.bitwise_xor(me[0], b) for b in range(slots)]
    row = lax.broadcasted_iota(jnp.int32, (8, cols), 0)
    picks = jnp.zeros((8, cols), F32)
    for h in range(heads):
        picks = jnp.where((row == h) & head_mask((8, cols), h), 1.0, picks)
    picks = picks.astype(BF)
    for i in range(slots):
        at = slice(i * rows, (i + 1) * rows)
        query[at] = qkv[0, where[i], :, :cols] * jnp.asarray(0.125, BF)
        up = d_context[0, where[i]]
        upstream[at] = up
        product = up.astype(F32) * context[0, where[i]].astype(F32)
        high = product.astype(BF)
        low = (product - high.astype(F32)).astype(BF)
        delta[:, at] = dot_nt(picks, high) + dot_nt(picks, low)
    key_row = lax.broadcasted_iota(jnp.int32, (rows, rows), 0)
    query_row = lax.broadcasted_iota(jnp.int32, (rows, rows), 1)
    total_sums = [jnp.zeros((1, cols), F32) for _ in range(3)]
    for j in range(slots):
        key = qkv[0, where[j], :, cols : 2 * cols]
        value = qkv[0, where[j], :, 2 * cols :]
        d_key = jnp.zeros((rows, cols), F32)
        d_value = jnp.zeros((rows, cols), F32)
        for h in range(heads):
            mask = head_mask((rows, cols), h)
            key_one = jnp.where(mask, key, jnp.zeros_like(key))
            value_one = jnp.where(mask, value, jnp.zeros_like(value))
            for i in range(j, slots):
                at = slice(i * rows, (i + 1) * rows)
                query_here, up_here = query[at], upstream[at]
                scores = dot_nt(key_one, query_here)
                if i == j:
                    scores = jnp.where(key_row <= query_row, scores, -1e30)
                probs = jnp.exp(scores - log_total[0, i, h : h + 1, :])
                d_probs = dot_nt(value_one, up_here)
                d_scores = (probs * (d_probs - delta[h : h + 1, at])).astype(BF)
                d_value = jnp.where(mask, d_value + dot(probs.astype(BF), up_here), d_value)
                d_key = jnp.where(mask, d_key + dot(d_scores, query_here), d_key)
                d_query_part = over_rows(d_scores, key_one)
                if j == 0 and h == 0:
                    d_query[at] = d_query_part
                else:
                    d_query[at] += d_query_part
        s = where[j]
        d_key_low = turn(d_key, cosine[s], -sine[s]).astype(BF)
        d_value_low = d_value.astype(BF)
        d_qkv[0, s, :, cols : 2 * cols] = d_key_low
        d_qkv[0, s, :, 2 * cols :] = d_value_low
        d_query_low = turn(d_query[j * rows : (j + 1) * rows] * 0.125, cosine[s], -sine[s]).astype(BF)
        d_qkv[0, s, :, :cols] = d_query_low
        for part, v in enumerate((d_query_low, d_key_low, d_value_low)):
            total_sums[part] += jnp.sum(v.astype(F32), 0, keepdims=True)
    sums[0] = jnp.concatenate(total_sums, 1)


def attend_back(me, qkv, context, d_context, log_total, cosine, sine):
    two, slots, rows, wide = qkv.shape
    cols = wide // 3

    def seq(*dims):
        return pl.BlockSpec((1, *dims), lambda i, me: (i,) + (0,) * len(dims))

    def whole(*dims):
        return pl.BlockSpec(dims, lambda i, me: (0,) * len(dims))

    return pl.pallas_call(
        attend_back_kernel,
        grid_spec=pltpu.PrefetchScalarGridSpec(
            num_scalar_prefetch=1,
            grid=(two,),
            in_specs=[
                seq(slots, rows, wide),
                seq(slots, rows, cols),
                seq(slots, rows, cols),
                seq(slots, 8, rows),
                whole(slots, rows, 128),
                whole(slots, rows, 128),
            ],
            out_specs=[seq(slots, rows, wide), seq(1, wide)],
            scratch_shapes=[
                pltpu.VMEM((slots * rows, cols), BF),
                pltpu.VMEM((slots * rows, cols), BF),
                pltpu.VMEM((slots * rows, cols), F32),
                pltpu.VMEM((8, slots * rows), F32),
            ],
        ),
        out_shape=[
            jax.ShapeDtypeStruct((two, slots, rows, wide), BF),
            jax.ShapeDtypeStruct((two, 1, wide), F32),
        ],
        compiler_params=pltpu.CompilerParams(vmem_limit_bytes=56 * 2**20),
        cost_estimate=LITTLE,
        name="attend_back",
    )(me, qkv, context, d_context, log_total, cosine, sine)


def feed_kernel(count, first, *refs):
    pieces, w = refs[:count], refs[count]
    act, inner, slope, swish, held, in_sem, out_sem = refs[-7:]
    ragged = slope.shape[1] - inner.shape[1]
    step = pl.program_id(0)
    height = pieces[0].shape[0]
    rows, ff = inner.shape
    each = rows // height

    def bring(i):
        return pltpu.make_async_copy(pieces[i], held.at[pl.ds(i * height, height)], in_sem.at[i])

    def put(i):
        return pltpu.make_async_copy(
            held.at[pl.ds(i * height, height)], act.at[pl.ds(first + i * height, height)], out_sem.at[i]
        )

    @pl.when(step == 0)
    def _():
        for i in range(count):
            bring(i).start()

    for k in range(count // each):

        @pl.when(step == k)
        def _(k=k):
            for i in range(k * each, (k + 1) * each):
                bring(i).wait()
                put(i).start()

    here = held[pl.ds(pl.multiple_of(step * rows, rows), rows), :]
    wide = dot(here, w[...])
    gate, upward = wide[:, :ff], wide[:, ff:]
    sigmoid = 1.0 / (1.0 + jnp.exp(-gate))
    product = gate * sigmoid
    inner[...] = (product * upward).astype(BF)
    swish[:, :ff] = product.astype(BF)
    slope[:, :ff] = (upward * sigmoid * (1.0 + gate * (1.0 - sigmoid))).astype(BF)
    if ragged:
        swish[:, ff:] = jnp.zeros((rows, ragged), BF)
        slope[:, ff:] = jnp.zeros((rows, ragged), BF)

    @pl.when(step == count // each - 1)
    def _():
        for i in range(count):
            put(i).wait()


def feed(pieces, rows, w, earlier=None, total=None):
    count = len(pieces)
    height, width = pieces[0].shape
    ff = w.shape[1] // 2
    all_rows = count * height
    first = 0 if earlier is None else total - all_rows
    kept = () if earlier is None else earlier
    block = pl.BlockSpec((rows, ff), lambda i: (i + first // rows, 0))
    padded = -(-ff // 128) * 128
    wide_block = pl.BlockSpec((rows, padded), lambda i: (i + first // rows, 0))
    return pl.pallas_call(
        functools.partial(feed_kernel, count, first),
        grid=(all_rows // rows,),
        in_specs=[pl.BlockSpec(memory_space=pltpu.HBM)] * count
        + [pl.BlockSpec(w.shape, lambda i: (0, 0))]
        + [pl.BlockSpec(memory_space=pltpu.HBM)] * len(kept),
        out_specs=[pl.BlockSpec(memory_space=pltpu.HBM), block, wide_block, wide_block],
        out_shape=[jax.ShapeDtypeStruct((total, n), BF) for n in (width, ff, padded, padded)],
        scratch_shapes=[
            pltpu.VMEM((all_rows, width), BF),
            pltpu.SemaphoreType.DMA((count,)),
            pltpu.SemaphoreType.DMA((count,)),
        ],
        input_output_aliases={count + 1 + i: i for i in range(len(kept))},
        compiler_params=pltpu.CompilerParams(vmem_limit_bytes=56 * 2**20),
        cost_estimate=pl.CostEstimate(
            flops=2 * all_rows * width * 2 * ff, bytes_accessed=2 * w.size, transcendentals=0
        ),
        name="feed",
    )(*pieces, w, *kept)


def feed_back_kernel(sends, *refs):
    cot, down, w, slope, swish = refs[:5]
    d_wide, sent, kept = refs[-3:]
    step = pl.program_id(0)
    ff = w.shape[1] // 2
    d_inner = dot(cot[...], down[...])
    d_gate = (d_inner * slope[...].astype(F32)).astype(BF)[:, :ff]
    d_upward = (d_inner * swish[...].astype(F32)).astype(BF)[:, :ff]
    both = jnp.concatenate([d_gate, d_upward], 1)
    d_wide[...] = both
    result = dot_nt(both, w[...]).astype(BF)

    @pl.when(step < sends)
    def _():
        sent[0] = result

    @pl.when(step >= sends)
    def _():
        kept[0] = result


def feed_back(cot, down, w, slope, swish, slots, rows, earlier=None):
    total, width = cot.shape
    ff = w.shape[1] // 2
    sends = len(slots) // 2
    first, stride = slots[0], 2

    def slot(i):
        return jnp.where(i < sends, first + stride * i, first - 1 + stride * (i - sends))

    def whole_of(v):
        return pl.BlockSpec(v.shape, lambda i: (0, 0))

    narrow = pl.BlockSpec((rows, slope.shape[1]), lambda i: (slot(i), 0))
    part = jax.ShapeDtypeStruct((sends, rows, width), BF)
    extra = () if earlier is None else (earlier,)
    return pl.pallas_call(
        functools.partial(feed_back_kernel, sends),
        grid=(2 * sends,),
        in_specs=[
            pl.BlockSpec((rows, width), lambda i: (slot(i), 0)),
            whole_of(down),
            whole_of(w),
            narrow,
            narrow,
        ]
        + [pl.BlockSpec(memory_space=pl.ANY)] * len(extra),
        out_specs=[
            pl.BlockSpec((rows, 2 * ff), lambda i: (slot(i), 0)),
            pl.BlockSpec((1, rows, width), lambda i: (jnp.minimum(i, sends - 1), 0, 0)),
            pl.BlockSpec((1, rows, width), lambda i: (jnp.maximum(i - sends, 0), 0, 0)),
        ],
        out_shape=[jax.ShapeDtypeStruct((total, 2 * ff), BF), part, part],
        input_output_aliases={5: 0} if extra else {},
        compiler_params=pltpu.CompilerParams(vmem_limit_bytes=56 * 2**20),
        cost_estimate=pl.CostEstimate(
            flops=2 * 2 * sends * rows * width * 3 * ff,
            bytes_accessed=2 * (w.size + down.size + 2 * sends * rows * (2 * width + 4 * ff)),
            transcendentals=0,
        ),
        name="feed_back",
    )(cot, down, w, slope, swish, *extra)


def over_rows_kernel(*refs):
    out, start = refs[-1], 0
    for left, right in zip(refs[:-1:2], refs[1:-1:2]):
        stop = start + right.shape[1]
        out[:, start:stop] = over_rows(left[...], right[...]).astype(BF)
        start = stop


def weight_grad(*pairs, tile=512):
    rows, width = pairs[0][0].shape
    cols = sum(right.shape[1] for _, right in pairs)
    specs = []
    for _, right in pairs:
        specs += [pl.BlockSpec((rows, tile), lambda i: (0, i)), pl.BlockSpec(right.shape, lambda i: (0, 0))]
    return pl.pallas_call(
        over_rows_kernel,
        grid=(width // tile,),
        in_specs=specs,
        out_specs=pl.BlockSpec((tile, cols), lambda i: (i, 0)),
        out_shape=jax.ShapeDtypeStruct((width, cols), BF),
        compiler_params=pltpu.CompilerParams(vmem_limit_bytes=56 * 2**20),
        cost_estimate=LITTLE,
        name="weight_grad",
    )(*(v for pair in pairs for v in pair))


def project_kernel(count, *refs):
    pieces, w = refs[:count], refs[count]
    all_rows, out, held, in_sem, out_sem = refs[-5:]
    step = pl.program_id(0)
    starts = [sum(p.shape[0] for p in pieces[:i]) for i in range(count)]
    rows = out.shape[0]

    def bring(i):
        return pltpu.make_async_copy(pieces[i], held.at[pl.ds(starts[i], pieces[i].shape[0])], in_sem.at[i])

    def put(i):
        at = pl.ds(starts[i], pieces[i].shape[0])
        return pltpu.make_async_copy(held.at[at], all_rows.at[at], out_sem.at[i])

    @pl.when(step == 0)
    def _():
        for i in range(count):
            bring(i).start()

    for k in range(held.shape[0] // rows):

        @pl.when(step == k)
        def _(k=k):
            for i in range(count):
                if k * rows <= starts[i] < (k + 1) * rows:
                    bring(i).wait()
                    put(i).start()

    here = held[pl.ds(pl.multiple_of(step * rows, rows), rows), :]
    out[...] = dot(here, w[...]).astype(out.dtype)

    @pl.when(step == held.shape[0] // rows - 1)
    def _():
        for i in range(count):
            put(i).wait()


def project(pieces, rows, w, kind):
    total, width = sum(p.shape[0] for p in pieces), pieces[0].shape[1]
    cols = w.shape[1]
    return pl.pallas_call(
        functools.partial(project_kernel, len(pieces)),
        grid=(total // rows,),
        in_specs=[pl.BlockSpec(memory_space=pltpu.HBM)] * len(pieces) + [pl.BlockSpec(w.shape, lambda i: (0, 0))],
        out_specs=[pl.BlockSpec(memory_space=pltpu.HBM), pl.BlockSpec((rows, cols), lambda i: (i, 0))],
        out_shape=[jax.ShapeDtypeStruct((total, width), BF), jax.ShapeDtypeStruct((total, cols), kind)],
        scratch_shapes=[
            pltpu.VMEM((total, width), BF),
            pltpu.SemaphoreType.DMA((len(pieces),)),
            pltpu.SemaphoreType.DMA((len(pieces),)),
        ],
        compiler_params=pltpu.CompilerParams(vmem_limit_bytes=56 * 2**20),
        cost_estimate=LITTLE,
        name="project",
    )(*pieces, w)


FAR, NEAR = (7, 6), (1, 3, 5, 0, 2, 4)


def assemble_kernel(count, *refs):
    pieces, out, held, in_sem, out_sem = refs[:count], refs[count], *refs[count + 1 :]
    ins, outs, start = [], [], 0
    for i, piece in enumerate(pieces):
        at = pl.ds(start, piece.shape[0])
        ins.append(pltpu.make_async_copy(piece, held.at[at], in_sem.at[i]))
        outs.append(pltpu.make_async_copy(held.at[at], out.at[at], out_sem.at[i]))
        start += piece.shape[0]
    for copy in ins:
        copy.start()
    for one, two in zip(ins, outs):
        one.wait()
        two.start()
    for copy in outs:
        copy.wait()


def assemble(*pieces):
    rows, width = sum(p.shape[0] for p in pieces), pieces[0].shape[1]
    return pl.pallas_call(
        functools.partial(assemble_kernel, len(pieces)),
        in_specs=[pl.BlockSpec(memory_space=pl.ANY)] * len(pieces),
        out_specs=pl.BlockSpec(memory_space=pltpu.HBM),
        out_shape=jax.ShapeDtypeStruct((rows, width), pieces[0].dtype),
        scratch_shapes=[
            pltpu.VMEM((rows, width), pieces[0].dtype),
            pltpu.SemaphoreType.DMA((len(pieces),)),
            pltpu.SemaphoreType.DMA((len(pieces),)),
        ],
        compiler_params=pltpu.CompilerParams(vmem_limit_bytes=56 * 2**20),
        cost_estimate=LITTLE,
        name="assemble",
    )(*pieces)


def core_sums_kernel(near, other, *refs):
    own, side, pair = refs
    for k, out in enumerate((own, side, pair)):
        out[...] = near[k].astype(F32) + other[k].astype(F32)


def core_sums(near, other, step=64):
    three, rows, width = near.shape
    blocks = pl.BlockSpec((three, step, width), lambda i: (0, i, 0))
    return pl.pallas_call(
        core_sums_kernel,
        grid=(rows // step,),
        in_specs=[blocks, blocks],
        out_specs=[pl.BlockSpec((step, width), lambda i: (i, 0))] * 3,
        out_shape=[jax.ShapeDtypeStruct((rows, width), F32)] * 3,
        compiler_params=pltpu.CompilerParams(vmem_limit_bytes=56 * 2**20),
        cost_estimate=LITTLE,
        name="core_sums",
    )(near, other)


def add_halves_kernel(side, pair, d1, d2, side_low, pair_low):
    half = d1.shape[0]
    side_low[:half] = (side[:half] + d1[...].astype(F32)).astype(BF)
    side_low[half:] = side[half:].astype(BF)
    pair_low[:half] = pair[:half].astype(BF)
    pair_low[half:] = (pair[half:] + d2[...].astype(F32)).astype(BF)


def add_halves(side, pair, d1, d2):
    return pl.pallas_call(
        add_halves_kernel,
        out_shape=[jax.ShapeDtypeStruct(side.shape, BF)] * 2,
        compiler_params=pltpu.CompilerParams(vmem_limit_bytes=56 * 2**20),
        cost_estimate=LITTLE,
        name="add_halves",
    )(side, pair, d1, d2)


def norm_kernel(count, *refs):
    terms, (base, gain, shift) = refs[:count], refs[count : count + 3]
    total, unit, inverse, low = refs[-4:]
    v = base[...].astype(F32)
    for t in terms:
        v = v + t[...].astype(F32)
    centered = v - jnp.mean(v, -1, keepdims=True)
    scale = lax.rsqrt(jnp.mean(centered * centered, -1, keepdims=True) + EPS)
    normed = centered * scale
    total[...] = v
    unit[...] = normed
    inverse[...] = jnp.broadcast_to(scale, inverse.shape)
    low[...] = (normed * gain[...] + shift[...]).astype(BF)


def in_rows(rows, cols):
    return pl.BlockSpec((rows, cols), lambda i: (i, 0))


def fixed(*dims):
    return pl.BlockSpec(dims, lambda i: (0,) * len(dims))


def norm(base, terms, gain, shift, step=64):
    rows, width = base.shape
    return pl.pallas_call(
        functools.partial(norm_kernel, len(terms)),
        grid=(rows // step,),
        in_specs=[in_rows(step, width)] * (len(terms) + 1) + [fixed(1, width)] * 2,
        out_specs=[in_rows(step, width), in_rows(step, width), in_rows(step, 128), in_rows(step, width)],
        out_shape=[
            jax.ShapeDtypeStruct((rows, width), F32),
            jax.ShapeDtypeStruct((rows, width), F32),
            jax.ShapeDtypeStruct((rows, 128), F32),
            jax.ShapeDtypeStruct((rows, width), BF),
        ],
        compiler_params=pltpu.CompilerParams(vmem_limit_bytes=56 * 2**20),
        cost_estimate=LITTLE,
        name="norm",
    )(*terms, base, gain[None], shift[None])


def norm_back_kernel(count, *refs):
    terms, (base, unit, inverse, gain) = refs[:count], refs[count : count + 4]
    total, sums, low = refs[-3:]
    upstream = terms[0][...].astype(F32)
    for t in terms[1:]:
        upstream = upstream + t[...].astype(F32)
    normed = unit[...]
    scaled = upstream * gain[...]
    product = upstream * normed
    adjusted = (
        scaled
        - jnp.mean(scaled, -1, keepdims=True)
        - normed * jnp.mean(product * gain[...], -1, keepdims=True)
    )
    v = base[...].astype(F32) + inverse[:, :1] * adjusted
    total[...] = v
    low[...] = v.astype(BF)
    here = jnp.concatenate([jnp.sum(product, 0, keepdims=True), jnp.sum(upstream, 0, keepdims=True)], 0)

    @pl.when(pl.program_id(0) == 0)
    def _():
        sums[...] = here

    @pl.when(pl.program_id(0) > 0)
    def _():
        sums[...] += here


def norm_back(base, terms, unit, inverse, gain, step=64):
    rows, width = base.shape
    return pl.pallas_call(
        functools.partial(norm_back_kernel, len(terms)),
        grid=(rows // step,),
        in_specs=[in_rows(step, width)] * (len(terms) + 2) + [in_rows(step, 128), fixed(1, width)],
        out_specs=[in_rows(step, width), fixed(2, width), in_rows(step, width)],
        out_shape=[
            jax.ShapeDtypeStruct((rows, width), F32),
            jax.ShapeDtypeStruct((2, width), F32),
            jax.ShapeDtypeStruct((rows, width), BF),
        ],
        compiler_params=pltpu.CompilerParams(vmem_limit_bytes=56 * 2**20),
        cost_estimate=LITTLE,
        name="norm_back",
    )(*terms, base, unit, inverse, gain[None])


class Place:
    def __init__(self, n_dp, n_tensor):
        self.n_dp, self.n_tensor = n_dp, n_tensor
        self.n_line = n_dp // 2
        dp, tensor = lax.axis_index("dp"), lax.axis_index("tensor")
        self.dp, self.tensor = dp, tensor
        self.line, self.pair = dp // 2, dp % 2

    def to_pair(self, v):
        return lax.ppermute(v, "dp", [(i, i ^ 1) for i in range(self.n_dp)])

    def to_side(self, v):
        return lax.ppermute(v, "tensor", [(i, i ^ 2) for i in range(self.n_tensor)])

    def to_core(self, v):
        return lax.ppermute(v, "tensor", [(i, i ^ 1) for i in range(self.n_tensor)])

    def by_pair(self, first, second, axis):
        return jnp.where(
            self.pair == 0,
            jnp.concatenate([first, second], axis),
            jnp.concatenate([second, first], axis),
        )

    def halves(self, v, axis):
        half = v.shape[axis] // 2
        low = lax.slice_in_dim(v, 0, half, axis=axis)
        high = lax.slice_in_dim(v, half, 2 * half, axis=axis)
        return jnp.where(self.pair == 0, low, high), jnp.where(self.pair == 0, high, low)

    def line_groups(self):
        return [[2 * i + p for i in range(self.n_line)] for p in (0, 1)]

    def widen(self, *weights):
        mine, theirs = zip(*[self.halves(w, 1) for w in weights])
        mine, theirs = jnp.concatenate(mine, 1), jnp.concatenate(theirs, 1)
        return mine, self.to_pair(theirs), theirs

    def gather_weight(self, mine, other):
        return self.gather_piece(self.by_pair(mine, other, 0))

    def gather_piece(self, piece):
        return lax.all_gather(piece, "dp", axis=0, tiled=True, axis_index_groups=self.line_groups())

    def scatter_grad(self, grad):
        return lax.psum_scatter(
            grad,
            "dp",
            scatter_dimension=0,
            tiled=True,
            axis_index_groups=self.line_groups(),
        )

    def share_send(self, total):
        mine, theirs = self.halves(total, 0)
        return mine, self.to_pair(theirs)

    def share_grad(self, mine, other, parts):
        cols = mine.shape[1] // parts
        shares = []
        for i in range(parts):
            at = slice(i * cols, (i + 1) * cols)
            shares.append(self.by_pair(mine[:, at], other[:, at], 1).astype(F32))
        return shares

    def gather_links(self, own):
        return own, self.to_side(own), self.to_pair(own)

    def gather_cores(self, own, side, pair):
        return own, self.to_core(own), side, self.to_core(side), pair, self.to_core(pair)

    def gather_begin(self, own):
        return self.gather_cores(*self.gather_links(own))

    def gather_far(self, near):
        side, pair = near[2], near[4]
        half = side.shape[0] // 2
        one, two = lax.optimization_barrier((side[:half], pair[half:]))
        return self.to_pair(one), self.to_side(two), one, two

    def gather_end(self, near):
        d1, d2, one, two = self.gather_far(near)
        return (d1, d2, self.to_core(d1), self.to_core(d2)), one, two

    def core_sum(self, far, far_sent):
        half = far.shape[0] // 2
        other = self.to_core(far_sent)
        return tuple(
            (far[i].astype(F32) + other[i].astype(F32)).astype(BF)
            for i in (slice(0, half), slice(half, 2 * half))
        )

    def core_sums(self, near, near_sent):
        other = self.to_core(near_sent)
        own, side, pair = (near[k].astype(F32) + other[k].astype(F32) for k in range(3))
        return side, pair, own

    def scatter_begin(self, far, far_sent, near, near_sent):
        return (*self.core_sum(far, far_sent), *self.core_sums(near, near_sent))

    def scatter_begin_once(self, far, far_sent, near, near_sent):
        half = far.shape[0] // 2
        other = self.to_core(jnp.concatenate([far_sent[None], near_sent], 0))
        f1, f2 = (
            (far[i].astype(F32) + other[0, i].astype(F32)).astype(BF)
            for i in (slice(0, half), slice(half, 2 * half))
        )
        own, side, pair = (near[k].astype(F32) + other[k + 1].astype(F32) for k in range(3))
        return f1, f2, side, pair, own

    def scatter_far(self, f1, f2):
        return self.to_pair(f1), self.to_side(f2)

    def scatter_add(self, d1, d2, side, pair, own):
        none = jnp.zeros_like(d1)
        side = (side + jnp.concatenate([d1, none], 0).astype(F32)).astype(BF)
        pair = (pair + jnp.concatenate([none, d2], 0).astype(F32)).astype(BF)
        return side, pair, own

    def scatter_middle(self, begun, *hold):
        f1, f2, side, pair, own = begun
        d1, d2 = self.scatter_far(f1, f2)
        if hold:
            d1, d2, side, pair = all_after((d1, d2, side, pair), *hold)
        return self.scatter_add(d1, d2, side, pair, own)

    def scatter_end(self, middle):
        side, pair, own = middle
        return own, self.to_side(side), self.to_pair(pair)

    def scatter_rows(self, *parts):
        return self.scatter_end(self.scatter_middle(self.scatter_begin(*parts)))

    def sum_all(self, v):
        for axis, size, first in (("tensor", self.n_tensor, 1), ("dp", self.n_dp, 2), ("dp", 2, 1)):
            length = self.n_tensor if axis == "tensor" else self.n_dp
            step = first
            while step < size:
                others = [
                    lax.ppermute(v, axis, [(i, i ^ (k * step)) for i in range(length)])
                    for k in range(1, 4 if 4 * step <= size else 2)
                ]
                v = v + others[0]
                if len(others) == 3:
                    v = v + (others[1] + others[2])
                step *= 1 + len(others)
        return v


def local(
    n_dp,
    n_tensor,
    block_input,
    cotangent,
    ln1_gain,
    ln1_bias,
    w_query,
    q_bias,
    w_key,
    k_bias,
    w_value,
    v_bias,
    w_out,
    ln2_gain,
    ln2_bias,
    w_gate,
    w_up,
    w_down,
):
    at = Place(n_dp, n_tensor)
    width = block_input.shape[1]
    rows = block_input.shape[0]
    length = rows * n_tensor
    half = rows // 2
    cols = w_query.shape[1] // 2
    heads = cols // HEAD
    ff = w_gate.shape[1] // 2

    def in_halves(v):
        return v[:half], v[half:]

    first_mine, first_other, first_sent = at.widen(w_query, w_key, w_value, w_out)
    _, unit_one, inverse_one, act = norm(after(block_input, first_sent), (), ln1_gain, ln1_bias)
    first_piece = at.by_pair(*all_after((first_mine, first_other), act), 0)
    full_qkv = at.gather_piece(first_piece[:, : 3 * cols])
    full_out = at.gather_piece(first_piece[:, 3 * cols :])
    near = at.gather_begin(act)
    far, *halves = at.gather_end(near)
    rest_mine, rest_other, _ = at.widen(*all_after((w_gate, w_up, w_down), *halves))
    tokens = 8 * rows
    cut = 6 * rows

    slots = after(jnp.arange(n_tensor), act)
    place = ((at.tensor ^ slots)[:, None] * rows + jnp.arange(rows)[None, :]).reshape(length)
    cosine, sine = (v.reshape(n_tensor, rows, 128) for v in turn_tables(place))
    me = at.tensor.astype(jnp.int32).reshape(1)

    column = at.tensor * 2 * cols + at.pair * cols
    query_shift = lax.dynamic_slice_in_dim(q_bias, column, cols)
    value_shift = lax.dynamic_slice_in_dim(v_bias, column, cols)
    key_column = at.tensor * 2 * heads * ROT + at.pair * heads * ROT
    key_rows = lax.dynamic_slice_in_dim(k_bias, key_column, heads * ROT)
    key_shift = jnp.pad(key_rows.reshape(heads, ROT), ((0, 0), (0, HEAD - ROT))).reshape(cols)
    shift = jnp.concatenate([query_shift, key_shift, value_shift])[None]

    far = all_after(far, cosine, sine, shift)
    act_one, pre = project([*near, *far], rows, full_qkv, F32)
    pre = pre.reshape(2, n_tensor, rows, 3 * cols)
    rest_late = after(rest_other, pre)
    wide_piece = at.by_pair(rest_mine[:, : 2 * ff], rest_late[:, : 2 * ff], 0)
    down_piece = at.by_pair(rest_mine[:, 2 * ff :], rest_late[:, 2 * ff :], 0)
    full_wide = at.gather_piece(wide_piece)
    qkv, context, log_total = attend(me, after(pre, wide_piece, down_piece), shift, cosine, sine)
    context_all = context.reshape(tokens, cols)

    def product(left, right):
        far = times_transposed(left[cut:], right).astype(BF)
        far, far_sent = lax.optimization_barrier((far[:rows], far[rows:]))
        near = times_transposed(after(left[:cut], far_sent), right).astype(BF)
        near = near.reshape(3, 2, rows, width)
        return far, far_sent, near[:, 0], near[:, 1]

    mixed = at.scatter_rows(*product(context_all, full_out))
    hidden, unit_two, inverse_two, act = norm(block_input, mixed, ln2_gain, ln2_bias)
    full_down = at.gather_piece(after(down_piece, act))
    near = at.gather_begin(act)
    far, *_ = at.gather_end(near)
    fed_near = feed(near, rows, full_wide, total=tokens)
    cot_links = at.gather_links(after(cotangent, *far))
    cot_near = at.gather_cores(*all_after(cot_links, fed_near[1]))
    d1, d2, *halves = at.gather_far(cot_near)
    far, *_ = lax.optimization_barrier((far, *halves))
    act_two, inner, slope, swish = feed(far, rows, full_wide, fed_near, tokens)
    d1, d2, inner = lax.optimization_barrier((d1, d2, inner))
    cot_all = assemble(*cot_near, d1, d2, at.to_core(d1), at.to_core(d2))
    down_grad = weight_grad((cot_all, inner))
    down_total = at.scatter_grad(down_grad)
    down_wide = jnp.pad(full_down, ((0, 0), (0, slope.shape[1] - ff)))
    d_wide, far_sent, far_kept = feed_back(
        after(cot_all, down_grad), down_wide, full_wide, slope, swish, FAR, rows
    )
    far_sum = at.core_sum(far_kept[0], far_sent[0])
    d_wide, near_sent, near_kept = feed_back(
        after(cot_all, *far_sum), down_wide, full_wide, slope, swish, NEAR, rows, d_wide
    )
    d1, d2, near_kept, near_sent, d_wide = lax.optimization_barrier(
        (*at.scatter_far(*far_sum), near_kept, near_sent, d_wide)
    )
    middle = at.scatter_add(d1, d2, *at.core_sums(near_kept, near_sent))
    wide_grad = weight_grad((act_two, after(d_wide, *middle)))
    d_act_two = at.scatter_end(middle)
    *d_act_two, wide_grad, down_total = lax.optimization_barrier((*d_act_two, wide_grad, down_total))
    wide_total = at.scatter_grad(wide_grad)
    d_hidden, sums_two, low = norm_back(
        cotangent, d_act_two, unit_two, inverse_two, ln2_gain
    )
    links = at.gather_links(low)
    fed_parts = product(after(inner, low), full_down)
    own, side, pair, *fed_parts = lax.optimization_barrier((*links, *fed_parts))
    near = at.gather_cores(own, side, pair)
    far, *_ = at.gather_end(near)
    fed_begun = at.scatter_begin_once(*fed_parts)
    *far, f1, f2 = lax.optimization_barrier((*far, *fed_begun[:2]))
    fed_begun = (f1, f2, *fed_begun[2:])
    d_hidden_all, d_context = project([*near, *far], rows, full_out, BF)
    d_context = d_context.reshape(context.shape)
    fed_middle = at.scatter_middle(fed_begun, d_context)
    down_sent = at.share_send(after(down_total, d_hidden_all))
    fed = at.scatter_end(fed_middle)
    d_qkv, sums = attend_back(me, qkv, context, after(d_context, *fed_middle), log_total, cosine, sine)
    d_qkv, *fed = lax.optimization_barrier((d_qkv, *fed, *down_sent))
    *fed, down_mine, down_other = fed
    d_qkv = d_qkv.reshape(tokens, 3 * cols)
    sums = sums[0, 0] + sums[1, 0]
    wide_sent = at.share_send(after(wide_total, d_qkv))
    qkvo_grad = weight_grad((act_one, after(d_qkv, *wide_sent[:1])), (d_hidden_all, context_all))
    qkvo_grad, wide_mine, wide_other = lax.optimization_barrier((qkvo_grad, *wide_sent))
    qkvo_total = at.scatter_grad(qkvo_grad)
    far_kept, far_sent, near_kept, near_sent = product(after(d_qkv, qkvo_grad), full_qkv)
    far_sum = at.core_sum(far_kept, far_sent)
    own, side, pair = core_sums(near_kept, at.to_core(near_sent))
    d1, d2, own, side, pair = lax.optimization_barrier((*at.scatter_far(*far_sum), own, side, pair))
    middle = (*add_halves(side, pair, d1, d2), own)
    block_output = (hidden + fed[0] + fed[1].astype(F32) + fed[2].astype(F32)).astype(BF)
    d_act_one = at.scatter_end(middle)
    (down_share,) = at.share_grad(*all_after((down_mine, down_other), *middle), 1)
    gate_share, up_share = at.share_grad(*all_after((wide_mine, wide_other), *middle), 2)
    *d_act_one, down_share, gate_share, up_share, block_output = lax.optimization_barrier(
        (*d_act_one, down_share, gate_share, up_share, block_output)
    )
    input_grad, sums_one, _ = norm_back(d_hidden, d_act_one, unit_one, inverse_one, ln1_gain)
    qkvo_sent = at.share_send(after(qkvo_total, sums_one))
    query_share, key_share, value_share, out_share = at.share_grad(*qkvo_sent, 4)

    query_part, value_part = sums[:cols], sums[2 * cols :]
    key_part = sums[cols : 2 * cols].reshape(heads, HEAD)[:, :ROT].reshape(heads * ROT)
    query_full = lax.dynamic_update_slice(jnp.zeros(q_bias.shape, F32), query_part, (column,))
    value_full = lax.dynamic_update_slice(jnp.zeros(v_bias.shape, F32), value_part, (column,))
    key_full = lax.dynamic_update_slice(jnp.zeros(k_bias.shape, F32), key_part, (key_column,))
    sums = at.sum_all(
        after(
            jnp.concatenate([sums_one[0], sums_one[1], sums_two[0], sums_two[1], query_full, value_full, key_full]),
            qkvo_sent[0],
        )
    )
    n = width
    return (
        block_output,
        input_grad,
        sums[:n],
        sums[n : 2 * n],
        query_share,
        sums[4 * n : 5 * n],
        key_share,
        sums[6 * n :],
        value_share,
        sums[5 * n : 6 * n],
        out_share,
        sums[2 * n : 3 * n],
        sums[3 * n : 4 * n],
        gate_share,
        up_share,
        down_share,
    )


def solution(mesh):
    rows = P(("dp", "tensor"), None)
    matrix = P("dp", "tensor")
    return jax.shard_map(
        functools.partial(local, mesh.shape["dp"], mesh.shape["tensor"]),
        mesh=mesh,
        in_specs=(
            rows, rows, P(), P(), matrix, P(), matrix, P(), matrix, P(), matrix, P(), P(),
            matrix, matrix, matrix,
        ),
        out_specs=(
            rows, rows, P(), P(), matrix, P(), matrix, P(), matrix, P(), matrix, P(), P(),
            matrix, matrix, matrix,
        ),
        check_vma=False,
    )
```

```python
import functools

import jax
import jax.numpy as jnp
from jax import lax
from jax.experimental import pallas as pl
from jax.experimental.pallas import tpu as pltpu
from jax.sharding import PartitionSpec as P

HEAD = 64
ROT = 16
EPS = 1e-05
LITTLE = pl.CostEstimate(flops=0, bytes_accessed=0, transcendentals=0)
BF = jnp.bfloat16
F32 = jnp.float32


def dot(left, right):
    return jnp.dot(left, right, preferred_element_type=F32)


def times_transposed(left, right):
    return lax.dot_general(left, right, (((1,), (1,)), ((), ())), preferred_element_type=F32)


def over_rows(left, right):
    return lax.dot_general(left, right, (((0,), (0,)), ((), ())), preferred_element_type=F32)


def dot_nt(left, right):
    return times_transposed(left, right)


def after(value, *others):
    return lax.optimization_barrier((value, *others))[0]


def all_after(values, *others):
    return lax.optimization_barrier((*values, *others))[: len(values)]


def head_mask(shape, head):
    lane = lax.broadcasted_iota(jnp.int32, shape, len(shape) - 1)
    return (lane >= head * HEAD) & (lane < (head + 1) * HEAD)


def turn(values, cosine, sine):
    half = ROT // 2
    parts = []
    for start in range(0, values.shape[1], 128):
        v = values[:, start : start + 128]
        lane = lax.broadcasted_iota(jnp.int32, v.shape, 1) % HEAD
        other = jnp.where(lane < half, pltpu.roll(v, 128 - half, 1), pltpu.roll(v, half, 1))
        parts.append(v * cosine + other * sine)
    return jnp.concatenate(parts, 1)


def turn_tables(place):
    half = ROT // 2
    frequency = 10000.0 ** (-2.0 * jnp.arange(half, dtype=F32) / ROT)
    angles = place.astype(F32)[:, None] * frequency[None, :]
    cosine, sine = jnp.cos(angles), jnp.sin(angles)
    rest = jnp.ones((place.shape[0], HEAD - ROT), F32)
    one = jnp.concatenate([cosine, cosine, rest], 1)
    two = jnp.concatenate([-sine, sine, 0.0 * rest], 1)
    return jnp.concatenate([one, one], 1), jnp.concatenate([two, two], 1)


def attend_kernel(me, pre, shift, cosine, sine, qkv, context, log_total):
    slots, rows, wide = pre.shape[1:]
    cols = wide // 3
    heads = cols // HEAD
    for s in range(slots):
        for part in range(3):
            at = slice(part * cols, (part + 1) * cols)
            v = pre[0, s, :, at] + shift[:, at]
            if part < 2:
                v = turn(v, cosine[s], sine[s])
            qkv[0, s, :, at] = v.astype(BF)
    where = [jnp.bitwise_xor(me[0], b) for b in range(slots)]
    key_row = lax.broadcasted_iota(jnp.int32, (rows, rows), 1)
    query_row = lax.broadcasted_iota(jnp.int32, (rows, rows), 0)
    lane = lax.broadcasted_iota(jnp.int32, (rows, 128), 1)
    for i in range(slots):
        query = qkv[0, where[i], :, :cols] * jnp.asarray(0.125, BF)
        total_context = jnp.zeros((rows, cols), F32)
        logs = jnp.zeros((rows, 128), F32)
        for h in range(heads):
            mask = head_mask((rows, cols), h)
            one = jnp.where(mask, query, jnp.zeros_like(query))
            scores = [dot_nt(one, qkv[0, where[j], :, cols : 2 * cols]) for j in range(i + 1)]
            scores[i] = jnp.where(key_row <= query_row, scores[i], -1e30)
            top = jnp.max(functools.reduce(jnp.maximum, scores), 1, keepdims=True)
            weights = [jnp.exp(v - top) for v in scores]
            total = jnp.sum(functools.reduce(jnp.add, weights), 1, keepdims=True)
            mixed = functools.reduce(
                jnp.add,
                [dot(w.astype(BF), qkv[0, where[j], :, 2 * cols :]) for j, w in enumerate(weights)],
            )
            total_context = jnp.where(mask, mixed * (1.0 / total), total_context)
            logs = jnp.where(lane == h, top + jnp.log(total), logs)
        context[0, where[i]] = total_context.astype(BF)
        log_total[0, i] = logs.T[:8]


def attend(me, pre, shift, cosine, sine):
    two, slots, rows, wide = pre.shape
    cols = wide // 3

    def seq(*dims):
        return pl.BlockSpec((1, *dims), lambda i, me: (i,) + (0,) * len(dims))

    def whole(*dims):
        return pl.BlockSpec(dims, lambda i, me: (0,) * len(dims))

    pairs = two * slots * (slots + 1) // 2 * (cols // HEAD)
    return pl.pallas_call(
        attend_kernel,
        grid_spec=pltpu.PrefetchScalarGridSpec(
            num_scalar_prefetch=1,
            grid=(two,),
            in_specs=[seq(slots, rows, wide), whole(1, wide), whole(slots, rows, 128), whole(slots, rows, 128)],
            out_specs=[seq(slots, rows, wide), seq(slots, rows, cols), seq(slots, 8, rows)],
        ),
        out_shape=[
            jax.ShapeDtypeStruct((two, slots, rows, wide), BF),
            jax.ShapeDtypeStruct((two, slots, rows, cols), BF),
            jax.ShapeDtypeStruct((two, slots, 8, rows), F32),
        ],
        compiler_params=pltpu.CompilerParams(vmem_limit_bytes=40 * 2**20),
        cost_estimate=LITTLE,
        name="attend",
    )(me, pre, shift, cosine, sine)


def attend_back_kernel(
    me, qkv, context, d_context, log_total, cosine, sine, d_qkv, sums, query, upstream, d_query, delta
):
    slots, rows, wide = qkv.shape[1:]
    cols = wide // 3
    heads = cols // HEAD
    where = [jnp.bitwise_xor(me[0], b) for b in range(slots)]
    row = lax.broadcasted_iota(jnp.int32, (8, cols), 0)
    picks = jnp.zeros((8, cols), F32)
    for h in range(heads):
        picks = jnp.where((row == h) & head_mask((8, cols), h), 1.0, picks)
    picks = picks.astype(BF)
    for i in range(slots):
        at = slice(i * rows, (i + 1) * rows)
        query[at] = qkv[0, where[i], :, :cols] * jnp.asarray(0.125, BF)
        up = d_context[0, where[i]]
        upstream[at] = up
        product = up.astype(F32) * context[0, where[i]].astype(F32)
        high = product.astype(BF)
        low = (product - high.astype(F32)).astype(BF)
        delta[:, at] = dot_nt(picks, high) + dot_nt(picks, low)
    key_row = lax.broadcasted_iota(jnp.int32, (rows, rows), 0)
    query_row = lax.broadcasted_iota(jnp.int32, (rows, rows), 1)
    total_sums = [jnp.zeros((1, cols), F32) for _ in range(3)]
    for j in range(slots):
        key = qkv[0, where[j], :, cols : 2 * cols]
        value = qkv[0, where[j], :, 2 * cols :]
        d_key = jnp.zeros((rows, cols), F32)
        d_value = jnp.zeros((rows, cols), F32)
        for h in range(heads):
            mask = head_mask((rows, cols), h)
            key_one = jnp.where(mask, key, jnp.zeros_like(key))
            value_one = jnp.where(mask, value, jnp.zeros_like(value))
            for i in range(j, slots):
                at = slice(i * rows, (i + 1) * rows)
                query_here, up_here = query[at], upstream[at]
                scores = dot_nt(key_one, query_here)
                if i == j:
                    scores = jnp.where(key_row <= query_row, scores, -1e30)
                probs = jnp.exp(scores - log_total[0, i, h : h + 1, :])
                d_probs = dot_nt(value_one, up_here)
                d_scores = (probs * (d_probs - delta[h : h + 1, at])).astype(BF)
                d_value = jnp.where(mask, d_value + dot(probs.astype(BF), up_here), d_value)
                d_key = jnp.where(mask, d_key + dot(d_scores, query_here), d_key)
                d_query_part = over_rows(d_scores, key_one)
                if j == 0 and h == 0:
                    d_query[at] = d_query_part
                else:
                    d_query[at] += d_query_part
        s = where[j]
        d_key_low = turn(d_key, cosine[s], -sine[s]).astype(BF)
        d_value_low = d_value.astype(BF)
        d_qkv[0, s, :, cols : 2 * cols] = d_key_low
        d_qkv[0, s, :, 2 * cols :] = d_value_low
        d_query_low = turn(d_query[j * rows : (j + 1) * rows] * 0.125, cosine[s], -sine[s]).astype(BF)
        d_qkv[0, s, :, :cols] = d_query_low
        for part, v in enumerate((d_query_low, d_key_low, d_value_low)):
            total_sums[part] += jnp.sum(v.astype(F32), 0, keepdims=True)
    sums[0] = jnp.concatenate(total_sums, 1)


def attend_back(me, qkv, context, d_context, log_total, cosine, sine):
    two, slots, rows, wide = qkv.shape
    cols = wide // 3

    def seq(*dims):
        return pl.BlockSpec((1, *dims), lambda i, me: (i,) + (0,) * len(dims))

    def whole(*dims):
        return pl.BlockSpec(dims, lambda i, me: (0,) * len(dims))

    return pl.pallas_call(
        attend_back_kernel,
        grid_spec=pltpu.PrefetchScalarGridSpec(
            num_scalar_prefetch=1,
            grid=(two,),
            in_specs=[
                seq(slots, rows, wide),
                seq(slots, rows, cols),
                seq(slots, rows, cols),
                seq(slots, 8, rows),
                whole(slots, rows, 128),
                whole(slots, rows, 128),
            ],
            out_specs=[seq(slots, rows, wide), seq(1, wide)],
            scratch_shapes=[
                pltpu.VMEM((slots * rows, cols), BF),
                pltpu.VMEM((slots * rows, cols), BF),
                pltpu.VMEM((slots * rows, cols), F32),
                pltpu.VMEM((8, slots * rows), F32),
            ],
        ),
        out_shape=[
            jax.ShapeDtypeStruct((two, slots, rows, wide), BF),
            jax.ShapeDtypeStruct((two, 1, wide), F32),
        ],
        compiler_params=pltpu.CompilerParams(vmem_limit_bytes=56 * 2**20),
        cost_estimate=LITTLE,
        name="attend_back",
    )(me, qkv, context, d_context, log_total, cosine, sine)


def feed_kernel(count, first, *refs):
    pieces, w = refs[:count], refs[count]
    act, inner, slope, swish, held, in_sem, out_sem = refs[-7:]
    step = pl.program_id(0)
    height = pieces[0].shape[0]
    rows, ff = inner.shape
    each = rows // height

    def bring(i):
        return pltpu.make_async_copy(pieces[i], held.at[pl.ds(i * height, height)], in_sem.at[i])

    def put(i):
        return pltpu.make_async_copy(
            held.at[pl.ds(i * height, height)], act.at[pl.ds(first + i * height, height)], out_sem.at[i]
        )

    @pl.when(step == 0)
    def _():
        for i in range(count):
            bring(i).start()

    for k in range(count // each):

        @pl.when(step == k)
        def _(k=k):
            for i in range(k * each, (k + 1) * each):
                bring(i).wait()
                put(i).start()

    here = held[pl.ds(pl.multiple_of(step * rows, rows), rows), :]
    wide = dot(here, w[...])
    gate, upward = wide[:, :ff], wide[:, ff:]
    sigmoid = 1.0 / (1.0 + jnp.exp(-gate))
    product = gate * sigmoid
    inner[...] = (product * upward).astype(BF)
    swish[...] = product.astype(BF)
    slope[...] = (upward * sigmoid * (1.0 + gate * (1.0 - sigmoid))).astype(BF)

    @pl.when(step == count // each - 1)
    def _():
        for i in range(count):
            put(i).wait()


def feed(pieces, rows, w, earlier=None, total=None):
    count = len(pieces)
    height, width = pieces[0].shape
    ff = w.shape[1] // 2
    all_rows = count * height
    first = 0 if earlier is None else total - all_rows
    kept = () if earlier is None else earlier
    block = pl.BlockSpec((rows, ff), lambda i: (i + first // rows, 0))
    return pl.pallas_call(
        functools.partial(feed_kernel, count, first),
        grid=(all_rows // rows,),
        in_specs=[pl.BlockSpec(memory_space=pltpu.HBM)] * count
        + [pl.BlockSpec(w.shape, lambda i: (0, 0))]
        + [pl.BlockSpec(memory_space=pltpu.HBM)] * len(kept),
        out_specs=[pl.BlockSpec(memory_space=pltpu.HBM), block, block, block],
        out_shape=[jax.ShapeDtypeStruct((total, width), BF)] + [jax.ShapeDtypeStruct((total, ff), BF)] * 3,
        scratch_shapes=[
            pltpu.VMEM((all_rows, width), BF),
            pltpu.SemaphoreType.DMA((count,)),
            pltpu.SemaphoreType.DMA((count,)),
        ],
        input_output_aliases={count + 1 + i: i for i in range(len(kept))},
        compiler_params=pltpu.CompilerParams(vmem_limit_bytes=56 * 2**20),
        cost_estimate=pl.CostEstimate(
            flops=2 * all_rows * width * 2 * ff, bytes_accessed=2 * w.size, transcendentals=0
        ),
        name="feed",
    )(*pieces, w, *kept)


def feed_back_kernel(sends, *refs):
    cot, down, w, slope, swish = refs[:5]
    d_wide, sent, kept = refs[-3:]
    step = pl.program_id(0)
    d_inner = dot(cot[...], down[...])
    d_gate = (d_inner * slope[...].astype(F32)).astype(BF)
    d_upward = (d_inner * swish[...].astype(F32)).astype(BF)
    both = jnp.concatenate([d_gate, d_upward], 1)
    d_wide[...] = both
    result = dot_nt(both, w[...]).astype(BF)

    @pl.when(step < sends)
    def _():
        sent[0] = result

    @pl.when(step >= sends)
    def _():
        kept[0] = result


def feed_back(cot, down, w, slope, swish, slots, rows, earlier=None):
    total, width = cot.shape
    ff = down.shape[1]
    sends = len(slots) // 2
    first, stride = slots[0], 2

    def slot(i):
        return jnp.where(i < sends, first + stride * i, first - 1 + stride * (i - sends))

    def whole_of(v):
        return pl.BlockSpec(v.shape, lambda i: (0, 0))

    narrow = pl.BlockSpec((rows, ff), lambda i: (slot(i), 0))
    part = jax.ShapeDtypeStruct((sends, rows, width), BF)
    extra = () if earlier is None else (earlier,)
    return pl.pallas_call(
        functools.partial(feed_back_kernel, sends),
        grid=(2 * sends,),
        in_specs=[
            pl.BlockSpec((rows, width), lambda i: (slot(i), 0)),
            whole_of(down),
            whole_of(w),
            narrow,
            narrow,
        ]
        + [pl.BlockSpec(memory_space=pl.ANY)] * len(extra),
        out_specs=[
            pl.BlockSpec((rows, 2 * ff), lambda i: (slot(i), 0)),
            pl.BlockSpec((1, rows, width), lambda i: (jnp.minimum(i, sends - 1), 0, 0)),
            pl.BlockSpec((1, rows, width), lambda i: (jnp.maximum(i - sends, 0), 0, 0)),
        ],
        out_shape=[jax.ShapeDtypeStruct((total, 2 * ff), BF), part, part],
        input_output_aliases={5: 0} if extra else {},
        compiler_params=pltpu.CompilerParams(vmem_limit_bytes=56 * 2**20),
        cost_estimate=pl.CostEstimate(
            flops=2 * 2 * sends * rows * width * 3 * ff,
            bytes_accessed=2 * (w.size + down.size + 2 * sends * rows * (2 * width + 4 * ff)),
            transcendentals=0,
        ),
        name="feed_back",
    )(cot, down, w, slope, swish, *extra)


def over_rows_kernel(*refs):
    out, start = refs[-1], 0
    for left, right in zip(refs[:-1:2], refs[1:-1:2]):
        stop = start + right.shape[1]
        out[:, start:stop] = over_rows(left[...], right[...]).astype(BF)
        start = stop


def weight_grad(*pairs, tile=512):
    rows, width = pairs[0][0].shape
    cols = sum(right.shape[1] for _, right in pairs)
    specs = []
    for _, right in pairs:
        specs += [pl.BlockSpec((rows, tile), lambda i: (0, i)), pl.BlockSpec(right.shape, lambda i: (0, 0))]
    return pl.pallas_call(
        over_rows_kernel,
        grid=(width // tile,),
        in_specs=specs,
        out_specs=pl.BlockSpec((tile, cols), lambda i: (i, 0)),
        out_shape=jax.ShapeDtypeStruct((width, cols), BF),
        compiler_params=pltpu.CompilerParams(vmem_limit_bytes=56 * 2**20),
        cost_estimate=LITTLE,
        name="weight_grad",
    )(*(v for pair in pairs for v in pair))


def project_kernel(count, *refs):
    pieces, w = refs[:count], refs[count]
    all_rows, out, held, in_sem, out_sem = refs[-5:]
    step = pl.program_id(0)
    starts = [sum(p.shape[0] for p in pieces[:i]) for i in range(count)]
    rows = out.shape[0]

    def bring(i):
        return pltpu.make_async_copy(pieces[i], held.at[pl.ds(starts[i], pieces[i].shape[0])], in_sem.at[i])

    def put(i):
        at = pl.ds(starts[i], pieces[i].shape[0])
        return pltpu.make_async_copy(held.at[at], all_rows.at[at], out_sem.at[i])

    @pl.when(step == 0)
    def _():
        for i in range(count):
            bring(i).start()

    for k in range(held.shape[0] // rows):

        @pl.when(step == k)
        def _(k=k):
            for i in range(count):
                if k * rows <= starts[i] < (k + 1) * rows:
                    bring(i).wait()
                    put(i).start()

    here = held[pl.ds(pl.multiple_of(step * rows, rows), rows), :]
    out[...] = dot(here, w[...]).astype(out.dtype)

    @pl.when(step == held.shape[0] // rows - 1)
    def _():
        for i in range(count):
            put(i).wait()


def project(pieces, rows, w, kind):
    total, width = sum(p.shape[0] for p in pieces), pieces[0].shape[1]
    cols = w.shape[1]
    return pl.pallas_call(
        functools.partial(project_kernel, len(pieces)),
        grid=(total // rows,),
        in_specs=[pl.BlockSpec(memory_space=pltpu.HBM)] * len(pieces) + [pl.BlockSpec(w.shape, lambda i: (0, 0))],
        out_specs=[pl.BlockSpec(memory_space=pltpu.HBM), pl.BlockSpec((rows, cols), lambda i: (i, 0))],
        out_shape=[jax.ShapeDtypeStruct((total, width), BF), jax.ShapeDtypeStruct((total, cols), kind)],
        scratch_shapes=[
            pltpu.VMEM((total, width), BF),
            pltpu.SemaphoreType.DMA((len(pieces),)),
            pltpu.SemaphoreType.DMA((len(pieces),)),
        ],
        compiler_params=pltpu.CompilerParams(vmem_limit_bytes=56 * 2**20),
        cost_estimate=LITTLE,
        name="project",
    )(*pieces, w)


FAR, NEAR = (7, 6), (1, 3, 5, 0, 2, 4)


def assemble_kernel(count, *refs):
    pieces, out, held, in_sem, out_sem = refs[:count], refs[count], *refs[count + 1 :]
    ins, outs, start = [], [], 0
    for i, piece in enumerate(pieces):
        at = pl.ds(start, piece.shape[0])
        ins.append(pltpu.make_async_copy(piece, held.at[at], in_sem.at[i]))
        outs.append(pltpu.make_async_copy(held.at[at], out.at[at], out_sem.at[i]))
        start += piece.shape[0]
    for copy in ins:
        copy.start()
    for one, two in zip(ins, outs):
        one.wait()
        two.start()
    for copy in outs:
        copy.wait()


def assemble(*pieces):
    rows, width = sum(p.shape[0] for p in pieces), pieces[0].shape[1]
    return pl.pallas_call(
        functools.partial(assemble_kernel, len(pieces)),
        in_specs=[pl.BlockSpec(memory_space=pl.ANY)] * len(pieces),
        out_specs=pl.BlockSpec(memory_space=pltpu.HBM),
        out_shape=jax.ShapeDtypeStruct((rows, width), pieces[0].dtype),
        scratch_shapes=[
            pltpu.VMEM((rows, width), pieces[0].dtype),
            pltpu.SemaphoreType.DMA((len(pieces),)),
            pltpu.SemaphoreType.DMA((len(pieces),)),
        ],
        compiler_params=pltpu.CompilerParams(vmem_limit_bytes=56 * 2**20),
        cost_estimate=LITTLE,
        name="assemble",
    )(*pieces)


def core_sums_kernel(near, other, *refs):
    own, side, pair = refs
    for k, out in enumerate((own, side, pair)):
        out[...] = near[k].astype(F32) + other[k].astype(F32)


def core_sums(near, other, step=64):
    three, rows, width = near.shape
    blocks = pl.BlockSpec((three, step, width), lambda i: (0, i, 0))
    return pl.pallas_call(
        core_sums_kernel,
        grid=(rows // step,),
        in_specs=[blocks, blocks],
        out_specs=[pl.BlockSpec((step, width), lambda i: (i, 0))] * 3,
        out_shape=[jax.ShapeDtypeStruct((rows, width), F32)] * 3,
        compiler_params=pltpu.CompilerParams(vmem_limit_bytes=56 * 2**20),
        cost_estimate=LITTLE,
        name="core_sums",
    )(near, other)


def add_halves_kernel(side, pair, d1, d2, side_low, pair_low):
    half = d1.shape[0]
    side_low[:half] = (side[:half] + d1[...].astype(F32)).astype(BF)
    side_low[half:] = side[half:].astype(BF)
    pair_low[:half] = pair[:half].astype(BF)
    pair_low[half:] = (pair[half:] + d2[...].astype(F32)).astype(BF)


def add_halves(side, pair, d1, d2):
    return pl.pallas_call(
        add_halves_kernel,
        out_shape=[jax.ShapeDtypeStruct(side.shape, BF)] * 2,
        compiler_params=pltpu.CompilerParams(vmem_limit_bytes=56 * 2**20),
        cost_estimate=LITTLE,
        name="add_halves",
    )(side, pair, d1, d2)


def norm_kernel(count, *refs):
    terms, (base, gain, shift) = refs[:count], refs[count : count + 3]
    total, unit, inverse, low = refs[-4:]
    v = base[...].astype(F32)
    for t in terms:
        v = v + t[...].astype(F32)
    centered = v - jnp.mean(v, -1, keepdims=True)
    scale = lax.rsqrt(jnp.mean(centered * centered, -1, keepdims=True) + EPS)
    normed = centered * scale
    total[...] = v
    unit[...] = normed
    inverse[...] = jnp.broadcast_to(scale, inverse.shape)
    low[...] = (normed * gain[...] + shift[...]).astype(BF)


def in_rows(rows, cols):
    return pl.BlockSpec((rows, cols), lambda i: (i, 0))


def fixed(*dims):
    return pl.BlockSpec(dims, lambda i: (0,) * len(dims))


def norm(base, terms, gain, shift, step=64):
    rows, width = base.shape
    return pl.pallas_call(
        functools.partial(norm_kernel, len(terms)),
        grid=(rows // step,),
        in_specs=[in_rows(step, width)] * (len(terms) + 1) + [fixed(1, width)] * 2,
        out_specs=[in_rows(step, width), in_rows(step, width), in_rows(step, 128), in_rows(step, width)],
        out_shape=[
            jax.ShapeDtypeStruct((rows, width), F32),
            jax.ShapeDtypeStruct((rows, width), F32),
            jax.ShapeDtypeStruct((rows, 128), F32),
            jax.ShapeDtypeStruct((rows, width), BF),
        ],
        compiler_params=pltpu.CompilerParams(vmem_limit_bytes=56 * 2**20),
        cost_estimate=LITTLE,
        name="norm",
    )(*terms, base, gain[None], shift[None])


def norm_back_kernel(count, *refs):
    terms, (base, unit, inverse, gain) = refs[:count], refs[count : count + 4]
    total, sums, low = refs[-3:]
    upstream = terms[0][...].astype(F32)
    for t in terms[1:]:
        upstream = upstream + t[...].astype(F32)
    normed = unit[...]
    scaled = upstream * gain[...]
    product = upstream * normed
    adjusted = (
        scaled
        - jnp.mean(scaled, -1, keepdims=True)
        - normed * jnp.mean(product * gain[...], -1, keepdims=True)
    )
    v = base[...].astype(F32) + inverse[:, :1] * adjusted
    total[...] = v
    low[...] = v.astype(BF)
    here = jnp.concatenate([jnp.sum(product, 0, keepdims=True), jnp.sum(upstream, 0, keepdims=True)], 0)

    @pl.when(pl.program_id(0) == 0)
    def _():
        sums[...] = here

    @pl.when(pl.program_id(0) > 0)
    def _():
        sums[...] += here


def norm_back(base, terms, unit, inverse, gain, step=64):
    rows, width = base.shape
    return pl.pallas_call(
        functools.partial(norm_back_kernel, len(terms)),
        grid=(rows // step,),
        in_specs=[in_rows(step, width)] * (len(terms) + 2) + [in_rows(step, 128), fixed(1, width)],
        out_specs=[in_rows(step, width), fixed(2, width), in_rows(step, width)],
        out_shape=[
            jax.ShapeDtypeStruct((rows, width), F32),
            jax.ShapeDtypeStruct((2, width), F32),
            jax.ShapeDtypeStruct((rows, width), BF),
        ],
        compiler_params=pltpu.CompilerParams(vmem_limit_bytes=56 * 2**20),
        cost_estimate=LITTLE,
        name="norm_back",
    )(*terms, base, unit, inverse, gain[None])


class Place:
    def __init__(self, n_dp, n_tensor):
        self.n_dp, self.n_tensor = n_dp, n_tensor
        self.n_line = n_dp // 2
        dp, tensor = lax.axis_index("dp"), lax.axis_index("tensor")
        self.dp, self.tensor = dp, tensor
        self.line, self.pair = dp // 2, dp % 2

    def to_pair(self, v):
        return lax.ppermute(v, "dp", [(i, i ^ 1) for i in range(self.n_dp)])

    def to_side(self, v):
        return lax.ppermute(v, "tensor", [(i, i ^ 2) for i in range(self.n_tensor)])

    def to_core(self, v):
        return lax.ppermute(v, "tensor", [(i, i ^ 1) for i in range(self.n_tensor)])

    def by_pair(self, first, second, axis):
        return jnp.where(
            self.pair == 0,
            jnp.concatenate([first, second], axis),
            jnp.concatenate([second, first], axis),
        )

    def halves(self, v, axis):
        half = v.shape[axis] // 2
        low = lax.slice_in_dim(v, 0, half, axis=axis)
        high = lax.slice_in_dim(v, half, 2 * half, axis=axis)
        return jnp.where(self.pair == 0, low, high), jnp.where(self.pair == 0, high, low)

    def line_groups(self):
        return [[2 * i + p for i in range(self.n_line)] for p in (0, 1)]

    def widen(self, *weights):
        mine, theirs = zip(*[self.halves(w, 1) for w in weights])
        mine, theirs = jnp.concatenate(mine, 1), jnp.concatenate(theirs, 1)
        return mine, self.to_pair(theirs), theirs

    def gather_weight(self, mine, other):
        return self.gather_piece(self.by_pair(mine, other, 0))

    def gather_piece(self, piece):
        return lax.all_gather(piece, "dp", axis=0, tiled=True, axis_index_groups=self.line_groups())

    def scatter_grad(self, grad):
        return lax.psum_scatter(
            grad,
            "dp",
            scatter_dimension=0,
            tiled=True,
            axis_index_groups=self.line_groups(),
        )

    def share_send(self, total):
        mine, theirs = self.halves(total, 0)
        return mine, self.to_pair(theirs)

    def share_grad(self, mine, other, parts):
        cols = mine.shape[1] // parts
        shares = []
        for i in range(parts):
            at = slice(i * cols, (i + 1) * cols)
            shares.append(self.by_pair(mine[:, at], other[:, at], 1).astype(F32))
        return shares

    def gather_links(self, own):
        return own, self.to_side(own), self.to_pair(own)

    def gather_cores(self, own, side, pair):
        return own, self.to_core(own), side, self.to_core(side), pair, self.to_core(pair)

    def gather_begin(self, own):
        return self.gather_cores(*self.gather_links(own))

    def gather_far(self, near):
        side, pair = near[2], near[4]
        half = side.shape[0] // 2
        one, two = lax.optimization_barrier((side[:half], pair[half:]))
        return self.to_pair(one), self.to_side(two), one, two

    def gather_end(self, near):
        d1, d2, one, two = self.gather_far(near)
        return (d1, d2, self.to_core(d1), self.to_core(d2)), one, two

    def core_sum(self, far, far_sent):
        half = far.shape[0] // 2
        other = self.to_core(far_sent)
        return tuple(
            (far[i].astype(F32) + other[i].astype(F32)).astype(BF)
            for i in (slice(0, half), slice(half, 2 * half))
        )

    def core_sums(self, near, near_sent):
        other = self.to_core(near_sent)
        own, side, pair = (near[k].astype(F32) + other[k].astype(F32) for k in range(3))
        return side, pair, own

    def scatter_begin(self, far, far_sent, near, near_sent):
        return (*self.core_sum(far, far_sent), *self.core_sums(near, near_sent))

    def scatter_begin_once(self, far, far_sent, near, near_sent):
        half = far.shape[0] // 2
        other = self.to_core(jnp.concatenate([far_sent[None], near_sent], 0))
        f1, f2 = (
            (far[i].astype(F32) + other[0, i].astype(F32)).astype(BF)
            for i in (slice(0, half), slice(half, 2 * half))
        )
        own, side, pair = (near[k].astype(F32) + other[k + 1].astype(F32) for k in range(3))
        return f1, f2, side, pair, own

    def scatter_far(self, f1, f2):
        return self.to_pair(f1), self.to_side(f2)

    def scatter_add(self, d1, d2, side, pair, own):
        none = jnp.zeros_like(d1)
        side = (side + jnp.concatenate([d1, none], 0).astype(F32)).astype(BF)
        pair = (pair + jnp.concatenate([none, d2], 0).astype(F32)).astype(BF)
        return side, pair, own

    def scatter_middle(self, begun, *hold):
        f1, f2, side, pair, own = begun
        d1, d2 = self.scatter_far(f1, f2)
        if hold:
            d1, d2, side, pair = all_after((d1, d2, side, pair), *hold)
        return self.scatter_add(d1, d2, side, pair, own)

    def scatter_end(self, middle):
        side, pair, own = middle
        return own, self.to_side(side), self.to_pair(pair)

    def scatter_rows(self, *parts):
        return self.scatter_end(self.scatter_middle(self.scatter_begin(*parts)))

    def sum_all(self, v):
        for axis, size, first in (("tensor", self.n_tensor, 1), ("dp", self.n_dp, 2), ("dp", 2, 1)):
            length = self.n_tensor if axis == "tensor" else self.n_dp
            step = first
            while step < size:
                others = [
                    lax.ppermute(v, axis, [(i, i ^ (k * step)) for i in range(length)])
                    for k in range(1, 4 if 4 * step <= size else 2)
                ]
                v = v + others[0]
                if len(others) == 3:
                    v = v + (others[1] + others[2])
                step *= 1 + len(others)
        return v


def local(
    n_dp,
    n_tensor,
    block_input,
    cotangent,
    ln1_gain,
    ln1_bias,
    w_query,
    q_bias,
    w_key,
    k_bias,
    w_value,
    v_bias,
    w_out,
    ln2_gain,
    ln2_bias,
    w_gate,
    w_up,
    w_down,
):
    at = Place(n_dp, n_tensor)
    width = block_input.shape[1]
    rows = block_input.shape[0]
    length = rows * n_tensor
    half = rows // 2
    cols = w_query.shape[1] // 2
    heads = cols // HEAD
    ff = w_gate.shape[1] // 2

    def in_halves(v):
        return v[:half], v[half:]

    first_mine, first_other, first_sent = at.widen(w_query, w_key, w_value, w_out)
    _, unit_one, inverse_one, act = norm(after(block_input, first_sent), (), ln1_gain, ln1_bias)
    first_piece = at.by_pair(*all_after((first_mine, first_other), act), 0)
    full_qkv = at.gather_piece(first_piece[:, : 3 * cols])
    full_out = at.gather_piece(first_piece[:, 3 * cols :])
    near = at.gather_begin(act)
    far, *halves = at.gather_end(near)
    rest_mine, rest_other, _ = at.widen(*all_after((w_gate, w_up, w_down), *halves))
    tokens = 8 * rows
    cut = 6 * rows

    slots = after(jnp.arange(n_tensor), act)
    place = ((at.tensor ^ slots)[:, None] * rows + jnp.arange(rows)[None, :]).reshape(length)
    cosine, sine = (v.reshape(n_tensor, rows, 128) for v in turn_tables(place))
    me = at.tensor.astype(jnp.int32).reshape(1)

    column = at.tensor * 2 * cols + at.pair * cols
    query_shift = lax.dynamic_slice_in_dim(q_bias, column, cols)
    value_shift = lax.dynamic_slice_in_dim(v_bias, column, cols)
    key_column = at.tensor * 2 * heads * ROT + at.pair * heads * ROT
    key_rows = lax.dynamic_slice_in_dim(k_bias, key_column, heads * ROT)
    key_shift = jnp.pad(key_rows.reshape(heads, ROT), ((0, 0), (0, HEAD - ROT))).reshape(cols)
    shift = jnp.concatenate([query_shift, key_shift, value_shift])[None]

    far = all_after(far, cosine, sine, shift)
    act_one, pre = project([*near, *far], rows, full_qkv, F32)
    pre = pre.reshape(2, n_tensor, rows, 3 * cols)
    rest_late = after(rest_other, pre)
    wide_piece = at.by_pair(rest_mine[:, : 2 * ff], rest_late[:, : 2 * ff], 0)
    down_piece = at.by_pair(rest_mine[:, 2 * ff :], rest_late[:, 2 * ff :], 0)
    full_wide = at.gather_piece(wide_piece)
    qkv, context, log_total = attend(me, after(pre, wide_piece, down_piece), shift, cosine, sine)
    context_all = context.reshape(tokens, cols)

    def product(left, right):
        far = times_transposed(left[cut:], right).astype(BF)
        far, far_sent = lax.optimization_barrier((far[:rows], far[rows:]))
        near = times_transposed(after(left[:cut], far_sent), right).astype(BF)
        near = near.reshape(3, 2, rows, width)
        return far, far_sent, near[:, 0], near[:, 1]

    mixed = at.scatter_rows(*product(context_all, full_out))
    hidden, unit_two, inverse_two, act = norm(block_input, mixed, ln2_gain, ln2_bias)
    full_down = at.gather_piece(after(down_piece, act))
    near = at.gather_begin(act)
    far, *_ = at.gather_end(near)
    fed_near = feed(near, rows, full_wide, total=tokens)
    cot_links = at.gather_links(after(cotangent, *far))
    cot_near = at.gather_cores(*all_after(cot_links, fed_near[1]))
    d1, d2, *halves = at.gather_far(cot_near)
    far, *_ = lax.optimization_barrier((far, *halves))
    act_two, inner, slope, swish = feed(far, rows, full_wide, fed_near, tokens)
    d1, d2, inner = lax.optimization_barrier((d1, d2, inner))
    cot_all = assemble(*cot_near, d1, d2, at.to_core(d1), at.to_core(d2))
    down_grad = weight_grad((cot_all, inner))
    down_total = at.scatter_grad(down_grad)
    d_wide, far_sent, far_kept = feed_back(
        after(cot_all, down_grad), full_down, full_wide, slope, swish, FAR, rows
    )
    far_sum = at.core_sum(far_kept[0], far_sent[0])
    d_wide, near_sent, near_kept = feed_back(
        after(cot_all, *far_sum), full_down, full_wide, slope, swish, NEAR, rows, d_wide
    )
    d1, d2, near_kept, near_sent, d_wide = lax.optimization_barrier(
        (*at.scatter_far(*far_sum), near_kept, near_sent, d_wide)
    )
    middle = at.scatter_add(d1, d2, *at.core_sums(near_kept, near_sent))
    wide_grad = weight_grad((act_two, after(d_wide, *middle)))
    d_act_two = at.scatter_end(middle)
    *d_act_two, wide_grad, down_total = lax.optimization_barrier((*d_act_two, wide_grad, down_total))
    wide_total = at.scatter_grad(wide_grad)
    d_hidden, sums_two, low = norm_back(
        cotangent, d_act_two, unit_two, inverse_two, ln2_gain
    )
    links = at.gather_links(low)
    fed_parts = product(after(inner, low), full_down)
    own, side, pair, *fed_parts = lax.optimization_barrier((*links, *fed_parts))
    near = at.gather_cores(own, side, pair)
    far, *_ = at.gather_end(near)
    fed_begun = at.scatter_begin_once(*fed_parts)
    *far, f1, f2 = lax.optimization_barrier((*far, *fed_begun[:2]))
    fed_begun = (f1, f2, *fed_begun[2:])
    d_hidden_all, d_context = project([*near, *far], rows, full_out, BF)
    d_context = d_context.reshape(context.shape)
    fed_middle = at.scatter_middle(fed_begun, d_context)
    down_sent = at.share_send(after(down_total, d_hidden_all))
    fed = at.scatter_end(fed_middle)
    out_grad = weight_grad((d_hidden_all, context_all))
    out_total = at.scatter_grad(out_grad)
    d_qkv, sums = attend_back(me, qkv, context, after(d_context, out_grad, *fed_middle), log_total, cosine, sine)
    d_qkv, *fed = lax.optimization_barrier((d_qkv, *fed, *down_sent))
    *fed, down_mine, down_other = fed
    d_qkv = d_qkv.reshape(tokens, 3 * cols)
    sums = sums[0, 0] + sums[1, 0]
    wide_sent = at.share_send(after(wide_total, d_qkv))
    qkvo_grad = weight_grad((act_one, after(d_qkv, *wide_sent[:1])))
    qkvo_grad, wide_mine, wide_other = lax.optimization_barrier((qkvo_grad, *wide_sent))
    qkvo_total = at.scatter_grad(qkvo_grad)
    far_kept, far_sent, near_kept, near_sent = product(after(d_qkv, qkvo_grad), full_qkv)
    far_sum = at.core_sum(far_kept, far_sent)
    own, side, pair = core_sums(near_kept, at.to_core(near_sent))
    d1, d2, own, side, pair, out_total = lax.optimization_barrier(
        (*at.scatter_far(*far_sum), own, side, pair, out_total)
    )
    middle = (*add_halves(side, pair, d1, d2), own)
    block_output = (hidden + fed[0] + fed[1].astype(F32) + fed[2].astype(F32)).astype(BF)
    d_act_one = at.scatter_end(middle)
    (down_share,) = at.share_grad(*all_after((down_mine, down_other), *middle), 1)
    gate_share, up_share = at.share_grad(*all_after((wide_mine, wide_other), *middle), 2)
    *d_act_one, down_share, gate_share, up_share, block_output = lax.optimization_barrier(
        (*d_act_one, down_share, gate_share, up_share, block_output)
    )
    input_grad, sums_one, _ = norm_back(d_hidden, d_act_one, unit_one, inverse_one, ln1_gain)
    qkvo_sent = at.share_send(jnp.concatenate([after(qkvo_total, sums_one), out_total], 1))
    query_share, key_share, value_share, out_share = at.share_grad(*qkvo_sent, 4)

    query_part, value_part = sums[:cols], sums[2 * cols :]
    key_part = sums[cols : 2 * cols].reshape(heads, HEAD)[:, :ROT].reshape(heads * ROT)
    query_full = lax.dynamic_update_slice(jnp.zeros(q_bias.shape, F32), query_part, (column,))
    value_full = lax.dynamic_update_slice(jnp.zeros(v_bias.shape, F32), value_part, (column,))
    key_full = lax.dynamic_update_slice(jnp.zeros(k_bias.shape, F32), key_part, (key_column,))
    sums = at.sum_all(
        after(
            jnp.concatenate([sums_one[0], sums_one[1], sums_two[0], sums_two[1], query_full, value_full, key_full]),
            qkvo_sent[0],
        )
    )
    n = width
    return (
        block_output,
        input_grad,
        sums[:n],
        sums[n : 2 * n],
        query_share,
        sums[4 * n : 5 * n],
        key_share,
        sums[6 * n :],
        value_share,
        sums[5 * n : 6 * n],
        out_share,
        sums[2 * n : 3 * n],
        sums[3 * n : 4 * n],
        gate_share,
        up_share,
        down_share,
    )


def solution(mesh):
    rows = P(("dp", "tensor"), None)
    matrix = P("dp", "tensor")
    return jax.shard_map(
        functools.partial(local, mesh.shape["dp"], mesh.shape["tensor"]),
        mesh=mesh,
        in_specs=(
            rows, rows, P(), P(), matrix, P(), matrix, P(), matrix, P(), matrix, P(), P(),
            matrix, matrix, matrix,
        ),
        out_specs=(
            rows, rows, P(), P(), matrix, P(), matrix, P(), matrix, P(), matrix, P(), P(),
            matrix, matrix, matrix,
        ),
        check_vma=False,
    )
```
